32 devices in a mesh: groups: 2 (over x), outc: 8 (over z, y), inc: 2 (over core).
Axes of the slice: x: 2, y: 2, z: 4, core: 2. Of those that a mesh axis runs over, the one named last changes fastest.
Arguments:
- tokens: bfloat16 [1024, 8192], P(('groups', 'outc'), 'inc'), parts along dimension 0, may hold values from -6 to 6
- w_zx: bfloat16 [8192, 128, 128], P('inc', 'outc'), may hold values from -0.0625 to 0.0625
- w_dt: bfloat16 [8192, 128], P('inc', 'outc'), may hold values from -0.0625 to 0.0625
- w_bc: bfloat16 [8192, 1024], P('inc', 'outc'), may hold values from -0.0625 to 0.0625
- conv_x: float32 [4, 128, 64], P(None, ('outc', 'inc')), may hold values from -3 to 3
- conv_bc: float32 [4, 1024], replicated, may hold values from -3 to 3
- dt_bias: float32 [128], P(('outc', 'inc')), may hold values from -3 to 1
- decay_rate: float32 [128], P(('outc', 'inc')), may hold values from 0.05 to 4
- skip_gain: float32 [128], P(('outc', 'inc')), may hold values from 0.5 to 1.5
- norm_gain: float32 [128, 64], P(('outc', 'inc')), may hold values from 0.1 to 1.9
- w_out: bfloat16 [8192, 8192], P('outc', 'inc'), may hold values from -0.0625 to 0.0625
- conv_x_state: bfloat16 [128, 3, 128, 64], P('groups', None, ('outc', 'inc')), parts along dimension 0, may hold values from -6 to 6
- conv_bc_state: bfloat16 [128, 3, 1024], P('groups'), parts along dimension 0, may hold values from -6 to 6
- ssm_state: bfloat16 [128, 128, 64, 128], P('groups', ('outc', 'inc')), parts along dimension 0, may hold values from -6 to 6
- span_start: int32 [128], P('groups'), parts along dimension 0, may hold values from 0 to 8
- accepted: int32 [128], P('groups'), parts along dimension 0, may hold values from 0 to 8
Outputs:
- output: bfloat16 [1024, 8192], P(('groups', 'outc'), 'inc'), parts along dimension 0
- new_state: bfloat16 [128, 128, 64, 128], P('groups', ('outc', 'inc')), parts along dimension 0
- new_conv_x: bfloat16 [128, 3, 128, 64], P('groups', None, ('outc', 'inc')), parts along dimension 0
- new_conv_bc: bfloat16 [128, 3, 1024], P('groups'), parts along dimension 0
The draws below stay inside these ranges and needn't reach their ends.
There are 2 independent parts, one for each index of `groups`. The reference program is written for one: setup_inputs(seed, part) draws one part's arguments, and reference() takes and returns one part's arrays. A program takes and returns all parts, laid end to end along the dimension named above; an argument that names none is the same for every part. Nothing has to cross between parts.
Inputs may be any that keep to these rules, and one draw needn't show every extreme that they name: `span_start`: 8 means that no new span begins among the drafts.
All inputs are finite; a program needn't handle non-finite values.
Results may differ from the reference program's by a relative error of at most 0.0075.
Values may be sent and summed in bfloat16 or wider, within the bound.
No kernel may reach another device: no remote copies, remote signals or barrier semaphores. Data moves between devices by JAX's collectives and lax.ppermute only.
A program may use at most 192 MiB of HBM per device.

```python
import math
import jax
import jax.numpy as jnp
from jax import lax

D = 8192
HEADS = 128
P_SIZE = 64
N = 128
G = 4
KW = 4
DRAFT = 8
REQ = 64
ROWS = 512
DI = 8192
BCW = 1024


def touch_ends(entries, stream_key, smallest, largest):
    longest = entries.shape.index(max(entries.shape))
    spots = []
    for shift in (0, 1):
        where = [jax.random.randint(jax.random.fold_in(stream_key, axis), (), 0, length) for axis, length in enumerate(entries.shape)]
        where[longest] = (where[longest] + shift) % entries.shape[longest]
        spots.append(tuple(where))
    return entries.at[spots[0]].set(smallest).at[spots[1]].set(largest)


def levels(key, dims, split, low, largest):
    level = 1.0
    for dim, parts in split:
        steps = jax.random.uniform(jax.random.fold_in(jax.random.fold_in(key, 6), dim), (parts,), jnp.float32, low / len(split), largest / len(split))
        level = level * jnp.repeat(jnp.exp(steps), dims[dim] // parts).reshape((-1,) + (1,) * (len(dims) - 1 - dim))
    return level


def bell_draw(stream_key, shape, width, limit, shards=(), kind=jnp.bfloat16):
    gain = levels(stream_key, shape, shards, -0.22, 0.18) if shards else 1.0
    array = jax.random.normal(stream_key, shape, jnp.float32) * width * gain
    return jnp.minimum(jnp.maximum(array, -limit), limit).astype(kind)


def setup_inputs(seed: int = 0, part: int = 0) -> dict:
    key_list = jax.random.split(jax.random.key(seed), 17)
    part_splits = jax.random.split(jax.random.fold_in(key_list[16], part), 17)
    tokens = bell_draw(part_splits[0], (ROWS, D), 1.0, 6.0, ((0, 8), (1, 2)))
    w_zx = bell_draw(key_list[1], (D, HEADS, 2 * P_SIZE), D ** -0.5, 0.0625, ((0, 2), (1, 8)))
    w_dt = bell_draw(key_list[2], (D, HEADS), D ** -0.5, 0.0625, ((0, 2), (1, 8)))
    w_bc = bell_draw(key_list[3], (D, BCW), D ** -0.5, 0.0625, ((0, 2), (1, 8)))
    conv_x = bell_draw(key_list[4], (KW, HEADS, P_SIZE), KW ** -0.5, 3.0, ((1, 16),), jnp.float32)
    conv_bc = bell_draw(key_list[5], (KW, BCW), KW ** -0.5, 3.0, (), jnp.float32)
    dt_bias = jnp.clip(-3.0 + 4.0 * jax.random.uniform(key_list[6], (HEADS,), jnp.float32) ** levels(key_list[6], (HEADS,), ((0, 16),), -0.2, 0.2), -3.0, 1.0)
    decay_rate = jnp.clip(jnp.exp(math.log(4.0) - 4.3820266 * jax.random.uniform(key_list[7], (HEADS,), jnp.float32) ** levels(key_list[7], (HEADS,), ((0, 16),), -0.2, 0.2)), 0.05, 4.0)
    skip_gain = jnp.clip(0.5 + 1.0 * jax.random.uniform(key_list[8], (HEADS,), jnp.float32) ** levels(key_list[8], (HEADS,), ((0, 16),), -0.2, 0.2), 0.5, 1.5)
    norm_gain = jnp.clip(1.0 + 0.18 * jax.random.normal(key_list[9], (HEADS, P_SIZE), jnp.float32), 0.1, 1.9)
    w_out = bell_draw(key_list[10], (DI, D), DI ** -0.5, 0.0625, ((0, 8), (1, 2)))
    conv_x_state = bell_draw(part_splits[11], (REQ, KW - 1, HEADS, P_SIZE), 1.0, 6.0, ((2, 16),))
    conv_bc_state = bell_draw(part_splits[12], (REQ, KW - 1, BCW), 1.0, 6.0)
    ssm_state = bell_draw(part_splits[13], (REQ, HEADS, P_SIZE, N), 1.0, 6.0, ((1, 16),))
    span_start = touch_ends(jax.random.randint(part_splits[14], (REQ,), 0, DRAFT + 1), jax.random.fold_in(part_splits[14], 1), 0, DRAFT).astype(jnp.int32)
    accepted = touch_ends(jax.random.randint(part_splits[15], (REQ,), 0, DRAFT + 1), jax.random.fold_in(part_splits[15], 1), 0, DRAFT).astype(jnp.int32)
    return dict(tokens=tokens, w_zx=w_zx, w_dt=w_dt, w_bc=w_bc, conv_x=conv_x, conv_bc=conv_bc, dt_bias=dt_bias, decay_rate=decay_rate, skip_gain=skip_gain, norm_gain=norm_gain, w_out=w_out, conv_x_state=conv_x_state, conv_bc_state=conv_bc_state, ssm_state=ssm_state, span_start=span_start, accepted=accepted)


def causal_conv(history, kernel, span_start):
    kernel_len = kernel.shape[0]
    draft_len = history.shape[1] - kernel_len + 1
    positions = jnp.arange(draft_len, dtype=jnp.int32)
    summed = jnp.zeros((history.shape[0], draft_len, history.shape[2]), jnp.float32)
    for offset in range(kernel_len):
        source_pos = positions + offset - (kernel_len - 1)
        visible = (positions[None, :] < span_start[:, None]) | (source_pos[None, :] >= span_start[:, None])
        summed = summed + kernel[offset][None, None, :] * history[:, offset:offset + draft_len].astype(jnp.float32) * visible[:, :, None].astype(jnp.float32)
    return summed

def conv_tail(history, span_start, accepted):
    offsets = jnp.arange(KW - 1, dtype=jnp.int32)
    wanted = accepted[:, None] + offsets[None, :]
    source_pos = wanted - (KW - 1)
    slots = jnp.arange(history.shape[1], dtype=jnp.int32)
    picker = (slots[None, None, :] == wanted[:, :, None]).astype(jnp.float32)
    picked = jnp.einsum('rjl,rlc->rjc', picker, history.astype(jnp.float32), precision=lax.Precision.HIGHEST)
    cleared = (source_pos < span_start[:, None]) & (span_start[:, None] < accepted[:, None])
    return jnp.where(cleared[:, :, None], jnp.zeros_like(picked), picked).astype(jnp.bfloat16)

def reference(tokens, w_zx, w_dt, w_bc, conv_x, conv_bc, dt_bias, decay_rate, skip_gain, norm_gain, w_out, conv_x_state, conv_bc_state, ssm_state, span_start, accepted):
    projected = jnp.dot(tokens, w_zx.reshape(D, HEADS * 2 * P_SIZE), preferred_element_type=jnp.float32).astype(jnp.bfloat16)
    projected = projected.reshape(REQ, DRAFT, HEADS, 2 * P_SIZE)
    gate_raw = projected[..., :P_SIZE]
    x_raw = projected[..., P_SIZE:]
    dt_raw = jnp.dot(tokens, w_dt, preferred_element_type=jnp.float32).astype(jnp.bfloat16).reshape(REQ, DRAFT, HEADS)
    bc_raw = jnp.dot(tokens, w_bc, preferred_element_type=jnp.float32).astype(jnp.bfloat16).reshape(REQ, DRAFT, BCW)
    x_history = jnp.concatenate([conv_x_state.reshape(REQ, KW - 1, DI), x_raw.reshape(REQ, DRAFT, DI)], axis=1)
    bc_history = jnp.concatenate([conv_bc_state, bc_raw], axis=1)
    x_conv = jax.nn.silu(causal_conv(x_history, conv_x.reshape(KW, DI), span_start)).reshape(REQ, DRAFT, HEADS, P_SIZE)
    bc_conv = jax.nn.silu(causal_conv(bc_history, conv_bc, span_start)).reshape(REQ, DRAFT, 2, G, N)
    group_of = jnp.arange(HEADS, dtype=jnp.int32) // (HEADS // G)
    b_heads = bc_conv[:, :, 0][:, :, group_of]
    c_heads = bc_conv[:, :, 1][:, :, group_of]
    step_size = jax.nn.softplus(dt_raw.astype(jnp.float32) + dt_bias)
    decay = jnp.exp(-step_size * decay_rate)
    state = ssm_state.astype(jnp.float32)
    kept = state
    outputs = []
    for position in range(DRAFT):
        fresh = (span_start == position)[:, None, None, None]
        state = jnp.where(fresh, jnp.zeros_like(state), state)
        update = (step_size[:, position, :, None] * x_conv[:, position])[..., None] * b_heads[:, position, :, None, :]
        state = decay[:, position, :, None, None] * state + update
        reading = jnp.einsum('rhpn,rhn->rhp', state, c_heads[:, position], precision=lax.Precision.HIGHEST)
        outputs.append(reading + skip_gain[None, :, None] * x_conv[:, position])
        kept = jnp.where((accepted == position + 1)[:, None, None, None], state, kept)
    mixed = jnp.stack(outputs, axis=1)
    gated = mixed * jax.nn.silu(gate_raw.astype(jnp.float32))
    grouped = gated.reshape(REQ, DRAFT, G, HEADS // G * P_SIZE)
    mean_sq = lax.optimization_barrier(jnp.mean(grouped * grouped, axis=-1, keepdims=True))
    normed = (grouped * lax.rsqrt(mean_sq + 1e-05)).reshape(REQ, DRAFT, HEADS, P_SIZE) * norm_gain
    normed = normed.astype(jnp.bfloat16).reshape(ROWS, DI)
    output = jnp.dot(normed, w_out, preferred_element_type=jnp.float32).astype(jnp.bfloat16)
    new_conv_x = conv_tail(x_history, span_start, accepted).reshape(REQ, KW - 1, HEADS, P_SIZE)
    new_conv_bc = conv_tail(bc_history, span_start, accepted)
    return (output, kept.astype(jnp.bfloat16), new_conv_x, new_conv_bc)
```

```python
import functools

import jax
import jax.numpy as jnp
from jax import lax
from jax.experimental import pallas as pl
from jax.experimental.pallas import tpu as pltpu
from jax.sharding import PartitionSpec as P

HEADS = 128
G = 4
KW = 4
DRAFT = 8
LANES = 128
BF = jnp.bfloat16
F32 = jnp.float32
HIGH = lax.Precision.HIGHEST
NT = (((1,), (1,)), ((), ()))
TN = (((0,), (0,)), ((), ()))
MIB = 1 << 20


def params(mib):
    return pltpu.CompilerParams(vmem_limit_bytes=mib * MIB)


def cost(flops, nbytes):
    return pl.CostEstimate(flops=int(flops), bytes_accessed=int(nbytes), transcendentals=0)


def whole_block(shape):
    return pl.BlockSpec(shape, lambda *_: (0,) * len(shape))


def relayout_kernel(heads, w_ref, o_ref, perm):
    kb = 256 // heads

    @pl.when(pl.program_id(0) == 0)
    def _():
        r = lax.broadcasted_iota(jnp.int32, (256, 256), 0)
        c = lax.broadcasted_iota(jnp.int32, (256, 256), 1)
        hit = (r // kb == lax.rem(c, heads)) & (lax.rem(r, kb) == c // heads)
        perm[...] = jnp.where(hit, 1.0, 0.0).astype(BF)

    bk = w_ref.shape[0]
    half = heads // 2
    for i in range(0, bk // kb, 2):
        first = w_ref[i * kb : (i + 1) * kb].reshape(256, LANES)
        second = w_ref[(i + 1) * kb : (i + 2) * kb].reshape(256, LANES)
        both = jnp.concatenate([first, second], axis=1)
        out = jnp.dot(perm[...], both, preferred_element_type=F32).astype(BF)
        for u in range(2):
            for h in range(heads):
                at = (h % half) * LANES
                o_ref[h // half, (i + u) * kb : (i + u + 1) * kb, at : at + LANES] = out[
                    h * kb : (h + 1) * kb, u * LANES : (u + 1) * LANES
                ]


def relayout(w_zx, bk=128):
    k, heads, width = w_zx.shape
    cols = heads // 2 * width
    return pl.pallas_call(
        functools.partial(relayout_kernel, heads),
        grid=(k // bk,),
        in_specs=[pl.BlockSpec((bk, heads, width), lambda i: (i, 0, 0))],
        out_specs=pl.BlockSpec((2, bk, cols), lambda i: (0, i, 0)),
        out_shape=jax.ShapeDtypeStruct((2, k, cols), BF),
        scratch_shapes=[pltpu.VMEM((256, 256), BF)],
        compiler_params=params(24),
        cost_estimate=cost(2 * k * heads * width * 256, 4 * k * heads * width),
        name="relayout",
    )(w_zx)


def gather_kernel(n, at_ref, own_ref, w_ref, *rest):
    ups, downs = rest[: n - 1], rest[n - 1 : 2 * (n - 1)]
    rows_ref, keep_ref, send_ref = rest[2 * (n - 1) :]
    rc, width = own_ref.shape
    half = width // 2

    def at(i):
        return pl.ds(pl.multiple_of(at_ref[i] * rc, 16), rc)

    rows_ref[at(0), :] = own_ref[...]
    for s in range(1, n):
        rows_ref[at(s), :half] = ups[s - 1][...]
        rows_ref[at(n + s), half:] = downs[s - 1][...]
    total = jnp.dot(rows_ref[...], w_ref[...], preferred_element_type=F32)
    keep_ref[...] = total
    send_ref[...] = total.astype(BF)


def gather_rows(owners, own, w_ext, ups, downs):
    n = len(ups) + 1
    rc, width = own.shape
    rows, cols = n * rc, w_ext.shape[1]
    arrays = [own, w_ext, *ups, *downs]
    return pl.pallas_call(
        functools.partial(gather_kernel, n),
        grid_spec=pltpu.PrefetchScalarGridSpec(
            num_scalar_prefetch=1,
            grid=(1,),
            in_specs=[whole_block(a.shape) for a in arrays],
            out_specs=[
                whole_block((rows, width)),
                whole_block((rows, cols)),
                whole_block((rows, cols)),
            ],
        ),
        out_shape=[
            jax.ShapeDtypeStruct((rows, width), BF),
            jax.ShapeDtypeStruct((rows, cols), F32),
            jax.ShapeDtypeStruct((rows, cols), BF),
        ],
        compiler_params=params(40),
        cost_estimate=cost(2 * rows * width * cols, 4 * rows * width + 2 * width * cols),
        name="gather_rows",
    )(owners, *arrays)


def project_kernel(which_ref, rows_ref, w_ref, o_ref):
    o_ref[...] = jnp.dot(rows_ref[...], w_ref[0], preferred_element_type=F32).astype(o_ref.dtype)


def project(which, rows, w, dtype, bn=256):
    m, k = rows.shape
    cols = w.shape[2]
    return pl.pallas_call(
        project_kernel,
        grid_spec=pltpu.PrefetchScalarGridSpec(
            num_scalar_prefetch=1,
            grid=(cols // bn,),
            in_specs=[
                pl.BlockSpec((m, k), lambda j, which: (0, 0)),
                pl.BlockSpec((1, k, bn), lambda j, which: (which[0], 0, j)),
            ],
            out_specs=pl.BlockSpec((m, bn), lambda j, which: (0, j)),
        ),
        out_shape=jax.ShapeDtypeStruct((m, cols), dtype),
        compiler_params=params(40),
        cost_estimate=cost(2 * m * k * cols, 2 * k * cols + 2 * m * k),
        name="project",
    )(which, rows, w)


def silu(v):
    return v / (1.0 + jnp.exp(-v))


def ssm_kernel(
    meta_ref, recv_ref, mine_ref, dt_ref, braw_ref, craw_ref, own_ref, prevx_ref, prevb_ref, prevc_ref,
    prevo_ref, tapx_ref, tapb_ref, tapc_ref, bias_ref, rate_ref, skip_ref, gain_ref, state_ref,
    gated_ref, ssq_ref, xw_ref, bconv_ref, sw_ref, xraw_ref, tail_ref,
):
    rb = recv_ref.shape[0]
    hp = gated_ref.shape[1]
    pairs = hp // LANES
    ss = meta_ref[..., 0:1].reshape(rb, 1)
    acc = meta_ref[..., 1:2].reshape(rb, 1)
    t = lax.broadcasted_iota(jnp.int32, (rb, 1), 0) & (DRAFT - 1)
    low = lax.broadcasted_iota(jnp.int32, (rb, LANES), 1) < LANES // 2
    seen = [
        jnp.where((t < ss) | (t - d >= ss), 1.0, 0.0).reshape(rb // DRAFT, DRAFT, 1) for d in range(KW)
    ]
    t3 = t.reshape(rb // DRAFT, DRAFT, 1)

    def conv(x, prev, taps):
        width = x.shape[1]
        x3 = x.reshape(rb // DRAFT, DRAFT, width)
        p3 = prev.reshape(rb // DRAFT, DRAFT, width)
        total = x3 * taps[KW - 1 : KW, :].reshape(1, 1, width)
        for d in range(1, KW):
            source = jnp.where(t3 >= d, pltpu.roll(x3, d, 1), pltpu.roll(p3, d, 1))
            total = total + (source * seen[d]) * taps[KW - 1 - d : KW - d, :].reshape(1, 1, width)
        return silu(total).reshape(rb, width)

    zx = (mine_ref[...].astype(F32) + recv_ref[...].astype(F32)).astype(BF).astype(F32)
    gates, xs = [], []
    for j in range(pairs):
        a = zx[:, 2 * j * LANES : (2 * j + 1) * LANES]
        b = zx[:, (2 * j + 1) * LANES : (2 * j + 2) * LANES]
        gates.append(jnp.where(low, a, pltpu.roll(b, LANES // 2, 1)))
        xs.append(jnp.where(low, pltpu.roll(a, LANES // 2, 1), b))
    prev_x = prevx_ref[...].reshape(rb, hp).astype(F32)
    convs = []
    for j in range(pairs):
        cut = slice(j * LANES, (j + 1) * LANES)
        xraw_ref[:, cut] = xs[j].astype(BF)
        convs.append(conv(xs[j], prev_x[:, cut], tapx_ref[:, cut]))
    b_conv = conv(braw_ref[...].astype(F32), prevb_ref[...].reshape(rb, LANES).astype(F32), tapb_ref[...])
    c_conv = conv(craw_ref[...].astype(F32), prevc_ref[...].reshape(rb, LANES).astype(F32), tapc_ref[...])
    bconv_ref[...] = b_conv.astype(BF)

    raw = dt_ref[...].astype(F32) + bias_ref[...]
    step = jnp.maximum(raw, 0.0) + jnp.log1p(jnp.exp(-jnp.abs(raw)))
    log_a = -step * rate_ref[...]
    ri = lax.broadcasted_iota(jnp.int32, (rb, rb), 0)
    ci = lax.broadcasted_iota(jnp.int32, (rb, rb), 1)
    same = (ri // DRAFT) == (ci // DRAFT)
    tt, tq = ri & (DRAFT - 1), ci & (DRAFT - 1)
    lower = same & (tq <= tt)
    linked = lower & jnp.logical_not((tq < ss) & (ss <= tt))
    cum = jnp.dot(jnp.where(lower, 1.0, 0.0), log_a, precision=HIGH, preferred_element_type=F32)
    cum_acc = jnp.dot(
        jnp.where(same & (tq < acc), 1.0, 0.0), log_a, precision=HIGH, preferred_element_type=F32
    )
    cum_t = cum.T
    step_t = step.T
    scores = lax.dot_general(c_conv, b_conv, NT, precision=HIGH, preferred_element_type=F32)

    def spread(v, j):
        return jnp.where(low, v[:, 2 * j : 2 * j + 1], v[:, 2 * j + 1 : 2 * j + 2])

    odd = (lax.broadcasted_iota(jnp.int32, (rb, 1), 0) & DRAFT) != 0
    c_pair = jnp.concatenate(
        [jnp.where(odd, 0.0, c_conv).astype(BF), jnp.where(odd, c_conv, 0.0).astype(BF)], axis=1
    )
    state = state_ref[...].reshape(rb // DRAFT, hp, LANES)
    carried = []
    for i in range(rb // (2 * DRAFT)):
        both = jnp.concatenate([state[2 * i], state[2 * i + 1]], axis=1)
        carried.append(
            lax.dot_general(
                c_pair[2 * DRAFT * i : 2 * DRAFT * (i + 1)], both, NT, preferred_element_type=F32
            )
        )
    carried = jnp.concatenate(carried, axis=0)

    kept = jnp.where(t < ss, jnp.exp(cum), 0.0)
    counted = (t < acc) & jnp.logical_not((t < ss) & (ss < acc))
    weight = jnp.where(counted, jnp.exp(jnp.where(counted, cum_acc - cum, 0.0)), 0.0) * step
    sw_ref[...] = jnp.where(ss < acc, 0.0, jnp.exp(cum_acc))
    squares = jnp.zeros((rb, LANES), F32)
    for j in range(pairs):
        cut = slice(j * LANES, (j + 1) * LANES)
        mixes = []
        for h in (2 * j, 2 * j + 1):
            gap = cum[:, h : h + 1] - cum_t[h : h + 1, :]
            mixes.append((jnp.exp(jnp.where(linked, gap, -1e30)) * (scores * step_t[h : h + 1, :])).astype(BF))
        x_conv = convs[j]
        x_pair = jnp.concatenate(
            [jnp.where(low, x_conv, 0.0).astype(BF), jnp.where(low, 0.0, x_conv).astype(BF)], axis=0
        )
        intra = jnp.dot(jnp.concatenate(mixes, axis=1), x_pair, preferred_element_type=F32)
        mixed = spread(kept, j) * carried[:, cut] + intra + skip_ref[:, cut] * x_conv
        gated = mixed * silu(gates[j])
        squares = squares + gated * gated
        gated_ref[:, cut] = (gated * gain_ref[:, cut]).astype(BF)
        xw_ref[:, cut] = (spread(weight, j) * x_conv).astype(BF)
    row_sum = jnp.broadcast_to(jnp.sum(squares, axis=1, keepdims=True), (rb, LANES))
    ssq_ref[...] = row_sum.T[:8]

    tail_ref[...] = pick_tail(ss, acc, own_ref[...], prevo_ref[...].reshape(own_ref.shape)).astype(BF)


def pick_tail(ss, acc, raw, prev):
    rb = raw.shape[0]
    ri = lax.broadcasted_iota(jnp.int32, (rb, rb), 0)
    ci = lax.broadcasted_iota(jnp.int32, (rb, rb), 1)
    same = (ri // DRAFT) == (ci // DRAFT)
    j, q = ri & (DRAFT - 1), ci & (DRAFT - 1)
    source = acc + j - (KW - 1)
    live = same & (j < KW - 1) & jnp.logical_not((source < ss) & (ss < acc))
    new = jnp.where(live & (q == source), 1.0, 0.0).astype(BF)
    old = jnp.where(live & (q == source + DRAFT), 1.0, 0.0).astype(BF)
    return jnp.dot(new, raw.astype(BF), preferred_element_type=F32) + jnp.dot(
        old, prev.astype(BF), preferred_element_type=F32
    )


def ssm(chunk, rb, per_row, tables, state):
    rows = per_row[1].shape[0]
    n, _, rq, hp, width_n = state.shape
    rc = rq * DRAFT
    ob = rb // rc
    cw = per_row[6].shape[1]

    def row_spec(a):
        if a.ndim == 2:
            return pl.BlockSpec((rb, a.shape[1]), lambda i: (i, 0))
        return pl.BlockSpec((ob, 1, rc, a.shape[3]), lambda i: (i, chunk, 0, 0))

    def flat(w):
        return pl.BlockSpec((rb, w), lambda i: (i, 0))

    return pl.pallas_call(
        ssm_kernel,
        grid=(rows // rb,),
        in_specs=[row_spec(a) for a in per_row]
        + [whole_block(a.shape) for a in tables]
        + [pl.BlockSpec((ob, 1, rq, hp, width_n), lambda i: (i, chunk, 0, 0, 0))],
        out_specs=[
            flat(hp),
            pl.BlockSpec((8, rb), lambda i: (0, i)),
            flat(hp),
            flat(LANES),
            flat(LANES),
            flat(hp),
            flat(cw),
        ],
        out_shape=[
            jax.ShapeDtypeStruct((rows, hp), BF),
            jax.ShapeDtypeStruct((8, rows), F32),
            jax.ShapeDtypeStruct((rows, hp), BF),
            jax.ShapeDtypeStruct((rows, LANES), BF),
            jax.ShapeDtypeStruct((rows, LANES), F32),
            jax.ShapeDtypeStruct((rows, hp), BF),
            jax.ShapeDtypeStruct((rows, cw), BF),
        ],
        compiler_params=params(40),
        cost_estimate=cost(2 * rows * hp * 4096, 6 * rows * hp * 16),
        name="ssm",
    )(*per_row, *tables, state)


def state_kernel(meta_ref, xw_ref, bconv_ref, sw_ref, xraw_ref, prevx_ref, state_ref, o_ref, tail_ref):
    rb, hp = xw_ref.shape
    width_p = LANES // 2
    ss = meta_ref[..., 0:1].reshape(rb, 1)
    acc = meta_ref[..., 1:2].reshape(rb, 1)
    tail_ref[...] = pick_tail(ss, acc, xraw_ref[...], prevx_ref[...].reshape(rb, hp)).astype(BF)
    request = lax.broadcasted_iota(jnp.int32, (rb, 1), 0) // DRAFT
    b_conv = bconv_ref[...].astype(F32)
    xw_t = xw_ref[...].astype(F32).T.astype(BF)
    rq = state_ref.shape[2]
    sw = sw_ref[...]
    for i in range(0, rb // DRAFT, 2):
        both = jnp.concatenate(
            [jnp.where(request == i + u, b_conv, 0.0).astype(BF) for u in range(2)], axis=1
        )
        added = jnp.dot(xw_t, both, preferred_element_type=F32)
        for u in range(2):
            r = i + u
            for h in range(hp // width_p):
                cut = slice(h * width_p, (h + 1) * width_p)
                old = state_ref[r // rq, 0, r % rq, cut, :].astype(F32)
                new = sw[r * DRAFT : r * DRAFT + 1, h : h + 1] * old + added[cut, u * LANES : (u + 1) * LANES]
                o_ref[r // rq, 0, r % rq, cut, :] = new.astype(BF)


def new_state(chunk, rb, meta, xw, bconv, sw, xraw, prev_x, state, into):
    rows, hp = xw.shape
    n, _, rq, _, width_n = state.shape
    rc = rq * DRAFT
    ob = rb // rc

    def four(w):
        return pl.BlockSpec((ob, 1, rc, w), lambda i: (i, chunk, 0, 0))

    def flat(w):
        return pl.BlockSpec((rb, w), lambda i: (i, 0))

    states = pl.BlockSpec((ob, 1, rq, hp, width_n), lambda i: (i, chunk, 0, 0, 0))
    args = [meta, xw, bconv, sw, xraw, prev_x, state]
    specs = [four(2), flat(hp), flat(LANES), flat(LANES), flat(hp), four(hp), states]
    kernel, aliases = state_kernel, {}
    if into is not None:
        args.append(into)
        specs.append(pl.BlockSpec(memory_space=pl.ANY))
        aliases = {7: 0}

        def kernel(*refs):
            return state_kernel(*refs[:7], *refs[8:])

    return pl.pallas_call(
        kernel,
        grid=(rows // rb,),
        in_specs=specs,
        out_specs=[states, flat(hp)],
        out_shape=[jax.ShapeDtypeStruct(state.shape, BF), jax.ShapeDtypeStruct((rows, hp), BF)],
        input_output_aliases=aliases,
        compiler_params=params(40),
        cost_estimate=cost(2 * rows * hp * 4096, 8 * rows * hp * 16),
        name="new_state",
    )(*args)


def out_kernel(scale_by, inc_ref, mine_ref, theirs_ref, w_mine_ref, w_theirs_ref, ssq_ref, o_ref):
    product = jnp.dot(mine_ref[...], w_mine_ref[...], preferred_element_type=F32) + jnp.dot(
        theirs_ref[...], w_theirs_ref[...], preferred_element_type=F32
    )
    scale = lax.rsqrt(ssq_ref[...] * scale_by + 1e-05)
    rows = scale.shape[1]
    column = jnp.broadcast_to(scale[0:1], (LANES, rows)).T[:, 0:1]
    o_ref[...] = (product * column).astype(o_ref.dtype)


def out_project(inc, mine, theirs, w_out, ssq, scale_by, bn=512):
    rows, hp = mine.shape
    cols = w_out.shape[1]
    return pl.pallas_call(
        functools.partial(out_kernel, scale_by),
        grid_spec=pltpu.PrefetchScalarGridSpec(
            num_scalar_prefetch=1,
            grid=(cols // bn,),
            in_specs=[
                pl.BlockSpec((rows, hp), lambda j, inc: (0, 0)),
                pl.BlockSpec((rows, hp), lambda j, inc: (0, 0)),
                pl.BlockSpec((hp, bn), lambda j, inc: (inc[0], j)),
                pl.BlockSpec((hp, bn), lambda j, inc: (1 - inc[0], j)),
                pl.BlockSpec((8, rows), lambda j, inc: (0, 0)),
            ],
            out_specs=pl.BlockSpec((rows, bn), lambda j, inc: (0, j)),
        ),
        out_shape=jax.ShapeDtypeStruct((rows, cols), F32),
        compiler_params=params(40),
        cost_estimate=cost(4 * rows * hp * cols, 4 * hp * cols + 4 * rows * cols),
        name="out_project",
    )(inc, mine, theirs, w_out, w_out, ssq)


def shards(n, chunks, tokens, w_zx, w_dt, w_bc, conv_x, conv_bc, dt_bias, decay_rate, skip_gain, norm_gain,
           w_out, conv_x_state, conv_bc_state, ssm_state, span_start, accepted):
    req, hd, width_p, width_n = ssm_state.shape
    hp = hd * width_p
    block_rows, half_d = tokens.shape
    cw = w_bc.shape[1]
    rc = block_rows // chunks
    rq = rc // DRAFT
    rows = n * rc
    rb = min(128, rows)
    order = list(range(0, n, 2)) + list(range(n - 1, 0, -2))
    place = [order.index(i) for i in range(n)]
    up = [(order[i], order[(i + 1) % n]) for i in range(n)]
    down = [(b, a) for a, b in up]
    swap = [(0, 1), (1, 0)]
    me = lax.axis_index("outc")
    inc = lax.axis_index("inc")
    pos = jnp.array(place, jnp.int32)[me]
    order_a = jnp.array(order, jnp.int32)
    steps = jnp.arange(n, dtype=jnp.int32)
    above = order_a[(pos - steps) % n]
    below = order_a[(pos + steps) % n]
    owners = jnp.concatenate([above, below])
    inc1 = inc.astype(jnp.int32).reshape(1)

    def other(a):
        return lax.ppermute(a, "inc", swap)

    member = n // G
    group = me // member
    seat = me % member
    w_ext = jnp.concatenate([w_bc, w_dt, jnp.zeros((half_d, LANES - w_dt.shape[1]), BF)], axis=1)
    if w_ext.shape[1] % LANES:
        w_ext = jnp.pad(w_ext, ((0, 0), (0, LANES - w_ext.shape[1] % LANES)))

    def history(a):
        a = a.reshape(req, KW - 1, -1)
        a = jnp.pad(a, ((0, 0), (DRAFT - KW + 1, 0), (0, 0)))
        return a.reshape(n, chunks, rc, a.shape[-1])

    def columns(a, start, size):
        return lax.dynamic_slice_in_dim(a, start, size, a.ndim - 1)

    prev_x = history(conv_x_state)
    prev_b = history(columns(conv_bc_state, group * width_n, width_n))
    prev_c = history(columns(conv_bc_state, (G + group) * width_n, width_n))
    prev_own = history(columns(conv_bc_state, me * cw, cw))
    meta = jnp.stack([span_start, accepted], axis=-1).astype(jnp.int32)
    meta = jnp.broadcast_to(meta[:, None, :], (req, DRAFT, 2)).reshape(n, chunks, rc, 2)

    def lanes(v):
        return jnp.pad(v, (0, LANES - hd)).reshape(1, LANES)

    tables = [
        conv_x.reshape(KW, hp),
        columns(conv_bc, group * width_n, width_n),
        columns(conv_bc, (G + group) * width_n, width_n),
        lanes(dt_bias),
        lanes(decay_rate),
        jnp.repeat(skip_gain, width_p).reshape(1, hp),
        norm_gain.reshape(1, hp),
    ]
    state = ssm_state.reshape(n, chunks, rq, hp, width_n)
    w = relayout(w_zx)
    scale_by = 1.0 / (HEADS // G * width_p)

    halves = []
    for c in range(chunks):
        own = tokens[c * rc : (c + 1) * rc]
        a, b = own[:, : half_d // 2], own[:, half_d // 2 :]
        ups, downs = [], []
        for s in range(n - 1):
            a = lax.ppermute(a, "outc", up)
            b = lax.ppermute(b, "outc", down)
            ups.append(a)
            downs.append(b)
        halves.append((own, ups, downs))

    outs, tails_x, tails_bc = [], [], []
    into = None
    for c in range(chunks):
        own, ups, downs = halves[c]
        rows_all, ext_keep, ext_send = gather_rows(owners, own, w_ext, ups, downs)
        ext = (ext_keep + other(ext_send).astype(F32)).astype(BF)
        bc_own = ext[:, :cw]
        dt = columns(ext[:, cw : cw + 2 * hd], inc * hd, hd)
        dt = jnp.pad(dt, ((0, 0), (0, LANES - hd)))
        got = []
        for k in range(member):
            pairs = []
            for g in range(G):
                width = member // 2
                sources = [g * width + i for i in range(width)] + [n // 2 + g * width + i for i in range(width)]
                for i in range(member):
                    pairs.append((sources[(i + k) % member], g * member + i))
            got.append(lax.ppermute(bc_own, "outc", pairs))
        pieces = []
        for i in range(member):
            piece = got[0]
            for k in range(1, member):
                piece = jnp.where((i - seat) % member == k, got[k], piece)
            pieces.append(piece)
        b_raw = jnp.concatenate(pieces[: member // 2], axis=1)
        c_raw = jnp.concatenate(pieces[member // 2 :], axis=1)
        theirs = other(project(1 - inc1, rows_all, w, BF))
        mine = project(inc1, rows_all, w, F32)
        gated, ssq, xw, bconv, sw, xraw, tail = ssm(
            c, rb, [meta, theirs, mine, dt, b_raw, c_raw, bc_own, prev_x, prev_b, prev_c, prev_own], tables, state
        )
        tails_bc.append(tail)
        gated_theirs = other(gated)
        ssq = ssq + other(ssq)
        d = 1
        while d < member:
            ssq = ssq + lax.ppermute(ssq, "outc", [(i, i ^ d) for i in range(n)])
            d *= 2
        partial = out_project(inc1, gated, gated_theirs, w_out, ssq, scale_by)
        half = partial.shape[1] // 2

        def part(i, side):
            owner = owners[i]
            return lax.dynamic_slice(partial, (owner * rc, side * half), (rc, half))

        p = part(1, 0).astype(BF)
        q = part(n + 1, 1).astype(BF)
        for s in range(n - 1):
            p = (lax.ppermute(p, "outc", up).astype(F32) + part((s + 2) % n, 0)).astype(BF)
            q = (lax.ppermute(q, "outc", down).astype(F32) + part(n + (s + 2) % n, 1)).astype(BF)
        outs.append(jnp.concatenate([p, q], axis=1))
        into, tail_x = new_state(c, rb, meta, xw, bconv, sw, xraw, prev_x, state, into)
        tails_x.append(tail_x)

    def tails(parts):
        a = jnp.stack([x.reshape(n, rq, DRAFT, x.shape[1]) for x in parts], axis=1)
        return a.reshape(req, DRAFT, a.shape[-1])[:, : KW - 1]

    new_x = tails(tails_x).reshape(req, KW - 1, hd, width_p)
    new_bc = lax.all_gather(tails(tails_bc), "outc", axis=2, tiled=True)
    return jnp.concatenate(outs, axis=0), into.reshape(ssm_state.shape), new_x, new_bc


def solution(mesh):
    n = mesh.shape["outc"]
    placed = (
        P(("groups", "outc"), "inc"),
        P("inc", "outc", None),
        P("inc", "outc"),
        P("inc", "outc"),
        P(None, ("outc", "inc"), None),
        P(),
        P(("outc", "inc")),
        P(("outc", "inc")),
        P(("outc", "inc")),
        P(("outc", "inc"), None),
        P("outc", "inc"),
        P("groups", None, ("outc", "inc"), None),
        P("groups", None, None),
        P("groups", ("outc", "inc"), None, None),
        P("groups"),
        P("groups"),
    )
    return jax.shard_map(
        functools.partial(shards, n, 2),
        mesh=mesh,
        in_specs=placed,
        out_specs=(
            P(("groups", "outc"), "inc"),
            P("groups", ("outc", "inc"), None, None),
            P("groups", None, ("outc", "inc"), None),
            P("groups", None, None),
        ),
        check_vma=False,
    )
```

```python
import functools

import jax
import jax.numpy as jnp
from jax import lax
from jax.experimental import pallas as pl
from jax.experimental.pallas import tpu as pltpu
from jax.sharding import PartitionSpec as P

HEADS = 128
G = 4
KW = 4
DRAFT = 8
LANES = 128
STREAMS = 2
BF = jnp.bfloat16
F32 = jnp.float32
HIGH = lax.Precision.HIGHEST
NT = (((1,), (1,)), ((), ()))
TN = (((0,), (0,)), ((), ()))
MIB = 1 << 20


def params(mib):
    return pltpu.CompilerParams(vmem_limit_bytes=mib * MIB)


def cost(flops, nbytes):
    return pl.CostEstimate(flops=int(flops), bytes_accessed=int(nbytes), transcendentals=0)


def whole_block(shape):
    return pl.BlockSpec(shape, lambda *_: (0,) * len(shape))


def relayout_kernel(heads, w_ref, o_ref, perm):
    kb = 256 // heads

    @pl.when(pl.program_id(0) == 0)
    def _():
        r = lax.broadcasted_iota(jnp.int32, (256, 256), 0)
        c = lax.broadcasted_iota(jnp.int32, (256, 256), 1)
        hit = (r // kb == lax.rem(c, heads)) & (lax.rem(r, kb) == c // heads)
        perm[...] = jnp.where(hit, 1.0, 0.0).astype(BF)

    bk = w_ref.shape[0]
    half = heads // 2
    for i in range(0, bk // kb, 2):
        first = w_ref[i * kb : (i + 1) * kb].reshape(256, LANES)
        second = w_ref[(i + 1) * kb : (i + 2) * kb].reshape(256, LANES)
        both = jnp.concatenate([first, second], axis=1)
        out = jnp.dot(perm[...], both, preferred_element_type=F32).astype(BF)
        for u in range(2):
            for h in range(heads):
                at = (h % half) * LANES
                o_ref[h // half, (i + u) * kb : (i + u + 1) * kb, at : at + LANES] = out[
                    h * kb : (h + 1) * kb, u * LANES : (u + 1) * LANES
                ]


def relayout(piece, pieces, w_zx, into, bk=512):
    k, heads, width = w_zx.shape
    cols = heads // 2 * width
    bk = min(bk, k // pieces)
    steps = k // bk // pieces
    kernel = functools.partial(relayout_kernel, heads)
    specs = [pl.BlockSpec((bk, heads, width), lambda i: (piece * steps + i, 0, 0))]
    args, aliases = [w_zx], {}
    if into is not None:
        args.append(into)
        specs.append(pl.BlockSpec(memory_space=pl.ANY))
        aliases = {1: 0}

        def kernel(w_ref, _, o_ref, perm):
            relayout_kernel(heads, w_ref, o_ref, perm)

    return pl.pallas_call(
        kernel,
        grid=(steps,),
        in_specs=specs,
        out_specs=pl.BlockSpec((2, bk, cols), lambda i: (0, piece * steps + i, 0)),
        out_shape=jax.ShapeDtypeStruct((2, k, cols), BF),
        scratch_shapes=[pltpu.VMEM((256, 256), BF)],
        input_output_aliases=aliases,
        compiler_params=params(52),
        cost_estimate=cost(2 * k * heads * width * 256 // pieces, 4 * k * heads * width // pieces),
        name="relayout",
    )(*args)


def project_kernel(parts, old, seq_ref, which_ref, *refs):
    ins, w_ref, ext_ref = refs[:parts], refs[parts], refs[parts + 1]
    rest = refs[parts + 2 :]
    olds, rest = rest[:old], rest[old:]
    o_ref, exts, rows = rest[0], rest[1:-1], rest[-1]
    piece = ins[0].shape[0]
    blocks = parts // STREAMS
    rc = piece * STREAMS

    def put(out, new, before):
        if not old:
            out[...] = new.astype(out.dtype)
            return
        for i in range(blocks):
            at = pl.ds(pl.multiple_of(seq_ref[i] * rc, 16), rc)
            out[at, :] = before[i * rc : (i + 1) * rc, :].astype(out.dtype)
            at = pl.ds(pl.multiple_of(seq_ref[blocks + i] * rc, 16), rc)
            out[at, :] = new[i * rc : (i + 1) * rc].astype(out.dtype)

    @pl.when(pl.program_id(0) == 0)
    def _():
        for i in range(parts):
            rows[i * piece : (i + 1) * piece, :] = ins[i][...]
        if exts:
            total = jnp.dot(rows[...], ext_ref[...], preferred_element_type=F32)
            for e in exts:
                put(e, total, olds[1] if old else None)

    total = jnp.dot(rows[...], w_ref[0], preferred_element_type=F32)
    put(o_ref, total, olds[0] if old else None)


def project(seq, which, ins, w, w_ext, dtype, ext_dtypes, olds=(), bn=512):
    parts = len(ins)
    rc, k = ins[0].shape
    m = rc * parts
    out_m = 2 * m if olds else m
    cols, ext_cols = w.shape[2], w_ext.shape[1]
    bn = min(bn, cols)
    in_specs = [whole_block((rc, k)) for _ in ins] + [
        pl.BlockSpec((1, k, bn), lambda j, seq, which: (which[0], 0, j)),
        whole_block((k, ext_cols)) if ext_dtypes else pl.BlockSpec(memory_space=pl.ANY),
    ]
    if olds:
        in_specs.append(pl.BlockSpec((m, bn), lambda j, seq, which: (0, j)))
        if ext_dtypes:
            in_specs.append(whole_block((m, ext_cols)))
    return pl.pallas_call(
        functools.partial(project_kernel, parts, len(olds)),
        grid_spec=pltpu.PrefetchScalarGridSpec(
            num_scalar_prefetch=2,
            grid=(cols // bn,),
            in_specs=in_specs,
            out_specs=[pl.BlockSpec((out_m, bn), lambda j, seq, which: (0, j))]
            + [whole_block((out_m, ext_cols)) for _ in ext_dtypes],
            scratch_shapes=[pltpu.VMEM((m, k), BF)],
        ),
        out_shape=[jax.ShapeDtypeStruct((out_m, cols), dtype)]
        + [jax.ShapeDtypeStruct((out_m, ext_cols), d) for d in ext_dtypes],
        compiler_params=params(52),
        cost_estimate=cost(2 * m * k * (cols + ext_cols), 2 * k * cols + 2 * m * k),
        name="project",
    )(seq, which, *ins, w, w_ext, *olds)


def silu(v):
    return v / (1.0 + jnp.exp(-v))


def ssm_kernel(
    meta_ref, recv_ref, mine_ref, dt_ref, braw_ref, craw_ref, prevx_ref, prevb_ref, prevc_ref, tapx_ref, tapb_ref, tapc_ref, bias_ref, rate_ref, skip_ref, gain_ref, state_ref,
    gated_ref, ssq_ref, xw_ref, bconv_ref, sw_ref, xraw_ref,
):
    rb = recv_ref.shape[0]
    hp = gated_ref.shape[1]
    pairs = hp // LANES
    ss = meta_ref[..., 0:1].reshape(rb, 1)
    acc = meta_ref[..., 1:2].reshape(rb, 1)
    t = lax.broadcasted_iota(jnp.int32, (rb, 1), 0) & (DRAFT - 1)
    low = lax.broadcasted_iota(jnp.int32, (rb, LANES), 1) < LANES // 2
    seen = [
        jnp.where((t < ss) | (t - d >= ss), 1.0, 0.0).reshape(rb // DRAFT, DRAFT, 1) for d in range(KW)
    ]
    t3 = t.reshape(rb // DRAFT, DRAFT, 1)

    def conv(x, prev, taps):
        width = x.shape[1]
        x3 = x.reshape(rb // DRAFT, DRAFT, width)
        p3 = prev.reshape(rb // DRAFT, DRAFT, width)
        total = x3 * taps[KW - 1 : KW, :].reshape(1, 1, width)
        for d in range(1, KW):
            source = jnp.where(t3 >= d, pltpu.roll(x3, d, 1), pltpu.roll(p3, d, 1))
            total = total + (source * seen[d]) * taps[KW - 1 - d : KW - d, :].reshape(1, 1, width)
        return silu(total).reshape(rb, width)

    zx = (mine_ref[...].astype(F32) + recv_ref[...].astype(F32)).astype(BF).astype(F32)
    gates, xs = [], []
    for j in range(pairs):
        a = zx[:, 2 * j * LANES : (2 * j + 1) * LANES]
        b = zx[:, (2 * j + 1) * LANES : (2 * j + 2) * LANES]
        gates.append(jnp.where(low, a, pltpu.roll(b, LANES // 2, 1)))
        xs.append(jnp.where(low, pltpu.roll(a, LANES // 2, 1), b))
    prev_x = prevx_ref[...].reshape(rb, hp).astype(F32)
    convs = []
    for j in range(pairs):
        cut = slice(j * LANES, (j + 1) * LANES)
        xraw_ref[:, cut] = xs[j].astype(BF)
        convs.append(conv(xs[j], prev_x[:, cut], tapx_ref[:, cut]))
    b_conv = conv(braw_ref[...].astype(F32), prevb_ref[...].reshape(rb, LANES).astype(F32), tapb_ref[...])
    c_conv = conv(craw_ref[...].astype(F32), prevc_ref[...].reshape(rb, LANES).astype(F32), tapc_ref[...])
    bconv_ref[...] = b_conv.astype(BF)

    raw = dt_ref[...].astype(F32) + bias_ref[...]
    step = jnp.maximum(raw, 0.0) + jnp.log1p(jnp.exp(-jnp.abs(raw)))
    log_a = -step * rate_ref[...]
    ri = lax.broadcasted_iota(jnp.int32, (rb, rb), 0)
    ci = lax.broadcasted_iota(jnp.int32, (rb, rb), 1)
    same = (ri // DRAFT) == (ci // DRAFT)
    tt, tq = ri & (DRAFT - 1), ci & (DRAFT - 1)
    lower = same & (tq <= tt)
    linked = lower & jnp.logical_not((tq < ss) & (ss <= tt))
    cum = jnp.dot(jnp.where(lower, 1.0, 0.0), log_a, precision=HIGH, preferred_element_type=F32)
    cum_acc = jnp.dot(
        jnp.where(same & (tq < acc), 1.0, 0.0), log_a, precision=HIGH, preferred_element_type=F32
    )
    cum_t = cum.T
    step_t = step.T
    scores = lax.dot_general(c_conv, b_conv, NT, precision=HIGH, preferred_element_type=F32)

    def spread(v, j):
        return jnp.where(low, v[:, 2 * j : 2 * j + 1], v[:, 2 * j + 1 : 2 * j + 2])

    odd = (lax.broadcasted_iota(jnp.int32, (rb, 1), 0) & DRAFT) != 0
    c_pair = jnp.concatenate(
        [jnp.where(odd, 0.0, c_conv).astype(BF), jnp.where(odd, c_conv, 0.0).astype(BF)], axis=1
    )
    state = state_ref[...].reshape(rb // DRAFT, hp, LANES)
    carried = []
    for i in range(rb // (2 * DRAFT)):
        both = jnp.concatenate([state[2 * i], state[2 * i + 1]], axis=1)
        carried.append(
            lax.dot_general(
                c_pair[2 * DRAFT * i : 2 * DRAFT * (i + 1)], both, NT, preferred_element_type=F32
            )
        )
    carried = jnp.concatenate(carried, axis=0)

    kept = jnp.where(t < ss, jnp.exp(cum), 0.0)
    counted = (t < acc) & jnp.logical_not((t < ss) & (ss < acc))
    weight = jnp.where(counted, jnp.exp(jnp.where(counted, cum_acc - cum, 0.0)), 0.0) * step
    sw_ref[...] = jnp.where(ss < acc, 0.0, jnp.exp(cum_acc))
    squares = jnp.zeros((rb, LANES), F32)
    for j in range(pairs):
        cut = slice(j * LANES, (j + 1) * LANES)
        mixes = []
        for h in (2 * j, 2 * j + 1):
            gap = cum[:, h : h + 1] - cum_t[h : h + 1, :]
            mixes.append((jnp.exp(jnp.where(linked, gap, -1e30)) * (scores * step_t[h : h + 1, :])).astype(BF))
        x_conv = convs[j]
        x_pair = jnp.concatenate(
            [jnp.where(low, x_conv, 0.0).astype(BF), jnp.where(low, 0.0, x_conv).astype(BF)], axis=0
        )
        intra = jnp.dot(jnp.concatenate(mixes, axis=1), x_pair, preferred_element_type=F32)
        mixed = spread(kept, j) * carried[:, cut] + intra + skip_ref[:, cut] * x_conv
        gated = mixed * silu(gates[j])
        squares = squares + gated * gated
        gated_ref[:, cut] = (gated * gain_ref[:, cut]).astype(BF)
        xw_ref[:, cut] = (spread(weight, j) * x_conv).astype(BF)
    row_sum = jnp.broadcast_to(jnp.sum(squares, axis=1, keepdims=True), (rb, LANES))
    ssq_ref[...] = row_sum.T[:8]


def pick_tail(ss, acc, raw, prev):
    rb = raw.shape[0]
    ri = lax.broadcasted_iota(jnp.int32, (rb, rb), 0)
    ci = lax.broadcasted_iota(jnp.int32, (rb, rb), 1)
    same = (ri // DRAFT) == (ci // DRAFT)
    j, q = ri & (DRAFT - 1), ci & (DRAFT - 1)
    source = acc + j - (KW - 1)
    live = same & (j < KW - 1) & jnp.logical_not((source < ss) & (ss < acc))
    new = jnp.where(live & (q == source), 1.0, 0.0).astype(BF)
    old = jnp.where(live & (q == source + DRAFT), 1.0, 0.0).astype(BF)
    return jnp.dot(new, raw.astype(BF), preferred_element_type=F32) + jnp.dot(
        old, prev.astype(BF), preferred_element_type=F32
    )


def ssm(chunk, rb, per_row, tables, state):
    rows = per_row[1].shape[0]
    n, _, rq, hp, width_n = state.shape
    rc = rq * DRAFT
    ob = rb // rc

    def row_spec(a):
        if a.ndim == 2:
            return pl.BlockSpec((rb, a.shape[1]), lambda i: (i, 0))
        return pl.BlockSpec((ob, 1, rc, a.shape[3]), lambda i: (i, chunk, 0, 0))

    def flat(w):
        return pl.BlockSpec((rb, w), lambda i: (i, 0))

    return pl.pallas_call(
        ssm_kernel,
        grid=(rows // rb,),
        in_specs=[row_spec(a) for a in per_row]
        + [whole_block(a.shape) for a in tables]
        + [pl.BlockSpec((ob, 1, rq, hp, width_n), lambda i: (i, chunk, 0, 0, 0))],
        out_specs=[
            flat(hp),
            pl.BlockSpec((8, rb), lambda i: (0, i)),
            flat(hp),
            flat(LANES),
            flat(LANES),
            flat(hp),
        ],
        out_shape=[
            jax.ShapeDtypeStruct((rows, hp), BF),
            jax.ShapeDtypeStruct((8, rows), F32),
            jax.ShapeDtypeStruct((rows, hp), BF),
            jax.ShapeDtypeStruct((rows, LANES), BF),
            jax.ShapeDtypeStruct((rows, LANES), F32),
            jax.ShapeDtypeStruct((rows, hp), BF),
        ],
        compiler_params=params(40),
        cost_estimate=cost(2 * rows * hp * 4096, 6 * rows * hp * 16),
        name="ssm",
    )(*per_row, *tables, state)


def state_kernel(meta_ref, xw_ref, bconv_ref, sw_ref, xraw_ref, prevx_ref, state_ref, o_ref, tail_ref):
    rb, hp = xw_ref.shape
    width_p = LANES // 2
    ss = meta_ref[..., 0:1].reshape(rb, 1)
    acc = meta_ref[..., 1:2].reshape(rb, 1)
    tail_ref[...] = pick_tail(ss, acc, xraw_ref[...], prevx_ref[...].reshape(rb, hp)).astype(BF)
    request = lax.broadcasted_iota(jnp.int32, (rb, 1), 0) // DRAFT
    b_conv = bconv_ref[...].astype(F32)
    xw_t = xw_ref[...].astype(F32).T.astype(BF)
    rq = state_ref.shape[2]
    sw = sw_ref[...]
    for i in range(0, rb // DRAFT, 2):
        both = jnp.concatenate(
            [jnp.where(request == i + u, b_conv, 0.0).astype(BF) for u in range(2)], axis=1
        )
        added = jnp.dot(xw_t, both, preferred_element_type=F32)
        for u in range(2):
            r = i + u
            for h in range(hp // width_p):
                cut = slice(h * width_p, (h + 1) * width_p)
                old = state_ref[r // rq, 0, r % rq, cut, :].astype(F32)
                new = sw[r * DRAFT : r * DRAFT + 1, h : h + 1] * old + added[cut, u * LANES : (u + 1) * LANES]
                o_ref[r // rq, 0, r % rq, cut, :] = new.astype(BF)


def tail_kernel(meta_ref, raw_ref, prev_ref, o_ref):
    rb = raw_ref.shape[0]
    ss = meta_ref[..., 0:1].reshape(rb, 1)
    acc = meta_ref[..., 1:2].reshape(rb, 1)
    o_ref[...] = pick_tail(ss, acc, raw_ref[...], prev_ref[...]).astype(BF)


def new_history(rb, meta, raw, prev):
    rows, cols = raw.shape

    def flat(w):
        return pl.BlockSpec((rb, w), lambda i: (i, 0))

    return pl.pallas_call(
        tail_kernel,
        grid=(rows // rb,),
        in_specs=[flat(2), flat(cols), flat(cols)],
        out_specs=flat(cols),
        out_shape=jax.ShapeDtypeStruct((rows, cols), BF),
        compiler_params=params(24),
        cost_estimate=cost(4 * rows * rb * cols, 6 * rows * cols),
        name="new_history",
    )(meta, raw, prev)


def new_state(chunk, rb, meta, xw, bconv, sw, xraw, prev_x, state, into):
    rows, hp = xw.shape
    n, _, rq, _, width_n = state.shape
    rc = rq * DRAFT
    ob = rb // rc

    def four(w):
        return pl.BlockSpec((ob, 1, rc, w), lambda i: (i, chunk, 0, 0))

    def flat(w):
        return pl.BlockSpec((rb, w), lambda i: (i, 0))

    states = pl.BlockSpec((ob, 1, rq, hp, width_n), lambda i: (i, chunk, 0, 0, 0))
    args = [meta, xw, bconv, sw, xraw, prev_x, state]
    specs = [four(2), flat(hp), flat(LANES), flat(LANES), flat(hp), four(hp), states]
    kernel, aliases = state_kernel, {}
    if into is not None:
        args.append(into)
        specs.append(pl.BlockSpec(memory_space=pl.ANY))
        aliases = {7: 0}

        def kernel(*refs):
            return state_kernel(*refs[:7], *refs[8:])

    return pl.pallas_call(
        kernel,
        grid=(rows // rb,),
        in_specs=specs,
        out_specs=[states, flat(hp)],
        out_shape=[jax.ShapeDtypeStruct(state.shape, BF), jax.ShapeDtypeStruct((rows, hp), BF)],
        input_output_aliases=aliases,
        compiler_params=params(40),
        cost_estimate=cost(2 * rows * hp * 4096, 8 * rows * hp * 16),
        name="new_state",
    )(*args)


def out_kernel(scale_by, inc_ref, mine_ref, theirs_ref, w_mine_ref, w_theirs_ref, ssq_ref, o_ref):
    product = jnp.dot(mine_ref[...], w_mine_ref[...], preferred_element_type=F32) + jnp.dot(
        theirs_ref[...], w_theirs_ref[...], preferred_element_type=F32
    )
    scale = lax.rsqrt(ssq_ref[...] * scale_by + 1e-05)
    rows = scale.shape[1]
    column = jnp.broadcast_to(scale[0:1], (LANES, rows)).T[:, 0:1]
    o_ref[...] = (product * column).astype(o_ref.dtype)


def out_project(inc, mine, theirs, w_out, ssq, scale_by, part, parts, bn=512):
    rows, hp = mine.shape
    cols = w_out.shape[1] // parts
    first = part * (cols // bn)
    return pl.pallas_call(
        functools.partial(out_kernel, scale_by),
        grid_spec=pltpu.PrefetchScalarGridSpec(
            num_scalar_prefetch=1,
            grid=(cols // bn,),
            in_specs=[
                pl.BlockSpec((rows, hp), lambda j, inc: (0, 0)),
                pl.BlockSpec((rows, hp), lambda j, inc: (0, 0)),
                pl.BlockSpec((hp, bn), lambda j, inc: (inc[0], first + j)),
                pl.BlockSpec((hp, bn), lambda j, inc: (1 - inc[0], first + j)),
                pl.BlockSpec((8, rows), lambda j, inc: (0, 0)),
            ],
            out_specs=pl.BlockSpec((rows, bn), lambda j, inc: (0, j)),
        ),
        out_shape=jax.ShapeDtypeStruct((rows, cols), F32),
        compiler_params=params(40),
        cost_estimate=cost(4 * rows * hp * cols, 4 * hp * cols + 4 * rows * cols),
        name="out_project",
    )(inc, mine, theirs, w_out, w_out, ssq)


def shards(n, chunks, tokens, w_zx, w_dt, w_bc, conv_x, conv_bc, dt_bias, decay_rate, skip_gain, norm_gain,
           w_out, conv_x_state, conv_bc_state, ssm_state, span_start, accepted):
    req, hd, width_p, width_n = ssm_state.shape
    hp = hd * width_p
    block_rows, half_d = tokens.shape
    cw = w_bc.shape[1]
    rc = block_rows // chunks
    rq = rc // DRAFT
    rows = n * rc
    rb = min(128, rows)
    order = list(range(0, n, 2)) + list(range(n - 1, 0, -2))
    place = [order.index(i) for i in range(n)]
    ring = [(2 * order[i], 2 * order[(i + 1) % n]) for i in range(n)]
    ring += [(2 * order[(i + 1) % n] + 1, 2 * order[i] + 1) for i in range(n)]
    swap = [(0, 1), (1, 0)]
    me = lax.axis_index("outc")
    inc = lax.axis_index("inc")
    pos = jnp.array(place, jnp.int32)[me]
    steps = jnp.arange(n, dtype=jnp.int32)
    seq = jnp.array(order, jnp.int32)[(pos + (2 * inc - 1) * steps) % n]
    inc1 = inc.astype(jnp.int32).reshape(1)

    def onward(a):
        return lax.ppermute(a, ("outc", "inc"), ring)

    def other(a):
        return lax.ppermute(a, "inc", swap)

    member = n // G
    group = me // member
    seat = me % member
    w_ext = jnp.concatenate([w_bc, w_dt, jnp.zeros((half_d, LANES - w_dt.shape[1]), BF)], axis=1)
    if w_ext.shape[1] % LANES:
        w_ext = jnp.pad(w_ext, ((0, 0), (0, LANES - w_ext.shape[1] % LANES)))

    def history(a):
        a = a.reshape(req, KW - 1, -1)
        a = jnp.pad(a, ((0, 0), (DRAFT - KW + 1, 0), (0, 0)))
        return a.reshape(n, chunks, rc, a.shape[-1])

    def columns(a, start, size):
        return lax.dynamic_slice_in_dim(a, start, size, a.ndim - 1)

    prev_x = history(conv_x_state)
    prev_b = history(columns(conv_bc_state, group * width_n, width_n))
    prev_c = history(columns(conv_bc_state, (G + group) * width_n, width_n))
    prev_own = history(columns(conv_bc_state, me * cw, cw)).reshape(rows, cw)
    meta = jnp.stack([span_start, accepted], axis=-1).astype(jnp.int32)
    meta = jnp.broadcast_to(meta[:, None, :], (req, DRAFT, 2)).reshape(n, chunks, rc, 2)

    def lanes(v):
        return jnp.pad(v, (0, LANES - hd)).reshape(1, LANES)

    tables = [
        conv_x.reshape(KW, hp),
        columns(conv_bc, group * width_n, width_n),
        columns(conv_bc, (G + group) * width_n, width_n),
        lanes(dt_bias),
        lanes(decay_rate),
        jnp.repeat(skip_gain, width_p).reshape(1, hp),
        norm_gain.reshape(1, hp),
    ]
    state = ssm_state.reshape(n, chunks, rq, hp, width_n)
    scale_by = 1.0 / (HEADS // G * width_p)

    pieces = 4
    w = None
    piece_rows = rc // STREAMS
    heads_of = [tokens[i * piece_rows : (i + 1) * piece_rows] for i in range(STREAMS)]
    blocks = list(heads_of)
    first = n // 2
    split = first * STREAMS
    for s in range(n - 1):
        heads_of = [onward(a) for a in heads_of]
        lead = heads_of[0]
        if s < pieces:
            w = relayout(s, pieces, w_zx, w)
            lead, w = lax.optimization_barrier((lead, w))
        elif s == max(pieces, first):
            theirs_1, ext_1 = project(seq, 1 - inc1, blocks[:split], w, w_ext, BF, [F32])
            lead, theirs_1, ext_1 = lax.optimization_barrier((lead, theirs_1, ext_1))
        elif s == max(pieces, first) + 1:
            (mine_1,) = project(seq, inc1, blocks[:split], w, w_ext, F32, [])
            lead, mine_1 = lax.optimization_barrier((lead, mine_1))
        heads_of[0] = lead
        blocks += heads_of

    prepared = [meta, prev_x, prev_b, prev_c, tables, prev_own, w_ext]
    blocks[-1], prepared = lax.optimization_barrier((blocks[-1], prepared))
    meta, prev_x, prev_b, prev_c, tables, prev_own, w_ext = prepared

    theirs, ext_keep, ext_send = project(
        seq, 1 - inc1, blocks[split:], w, w_ext, BF, [F32, BF], (theirs_1, ext_1)
    )
    ext = (ext_keep + other(ext_send).astype(F32)).astype(BF)
    bc_own = ext[:, :cw]
    history_bc = new_history(rb, meta.reshape(rows, 2), bc_own, prev_own)
    history_bc = history_bc.reshape(req, DRAFT, cw)[:, : KW - 1].reshape(1, req * (KW - 1), cw)
    dt = columns(ext[:, cw : cw + 2 * hd], inc * hd, hd)
    dt = jnp.pad(dt, ((0, 0), (0, LANES - hd)))
    got = []
    for k in range(member):
        pairs = []
        for g in range(G):
            width = member // 2
            sources = [g * width + i for i in range(width)] + [n // 2 + g * width + i for i in range(width)]
            for i in range(member):
                pairs.append((sources[(i + k) % member], g * member + i))
        got.append(lax.ppermute(bc_own, "outc", pairs))
    picked = []
    for i in range(member):
        piece = got[0]
        for k in range(1, member):
            piece = jnp.where((i - seat) % member == k, got[k], piece)
        picked.append(piece)
    b_raw = jnp.concatenate(picked[: member // 2], axis=1)
    c_raw = jnp.concatenate(picked[member // 2 :], axis=1)
    theirs = other(theirs)
    (mine,) = project(seq, inc1, blocks[split:], w, w_ext, F32, [], (mine_1,))
    gated, ssq, xw, bconv, sw, xraw = ssm(
        0, rb, [meta, theirs, mine, dt, b_raw, c_raw, prev_x, prev_b, prev_c], tables, state
    )

    def tails(a):
        return a.reshape(req, DRAFT, a.shape[-1])[:, : KW - 1]

    gated_theirs = other(gated)
    ssq = ssq + other(ssq)
    d = 1
    while d < member:
        ssq = ssq + lax.ppermute(ssq, "outc", [(i, i ^ d) for i in range(n)])
        d *= 2
    after, tail_x = new_state(0, rb, meta, xw, bconv, sw, xraw, prev_x, state, None)
    gated_theirs, ssq, after = lax.optimization_barrier((gated_theirs, ssq, after))

    sums, partials = [], []

    def part(i, s):
        return lax.dynamic_slice_in_dim(partials[i], seq[(s + 1) % n] * rc, rc, 0)

    for i in range(STREAMS):
        partials.append(out_project(inc1, gated, gated_theirs, w_out, ssq, scale_by, i, STREAMS))
        sums.append(part(i, 0).astype(BF))
    width = 1
    for s in range(n - 1):
        if width < n:
            history_bc, sums[0] = lax.optimization_barrier((history_bc, sums[0]))
            got = lax.ppermute(history_bc, "outc", [(i, i ^ width) for i in range(n)])
            history_bc = jnp.where(
                (me & width) != 0,
                jnp.concatenate([got, history_bc], axis=0),
                jnp.concatenate([history_bc, got], axis=0),
            )
            width *= 2
        for i in range(STREAMS):
            sums[i] = (onward(sums[i]).astype(F32) + part(i, s + 1)).astype(BF)
    new_bc = jnp.swapaxes(history_bc, 0, 1).reshape(req, KW - 1, n * cw)
    new_x = tails(tail_x).reshape(req, KW - 1, hd, width_p)
    return jnp.concatenate(sums, axis=1), after.reshape(ssm_state.shape), new_x, new_bc


def solution(mesh):
    n = mesh.shape["outc"]
    placed = (
        P(("groups", "outc"), "inc"),
        P("inc", "outc", None),
        P("inc", "outc"),
        P("inc", "outc"),
        P(None, ("outc", "inc"), None),
        P(),
        P(("outc", "inc")),
        P(("outc", "inc")),
        P(("outc", "inc")),
        P(("outc", "inc"), None),
        P("outc", "inc"),
        P("groups", None, ("outc", "inc"), None),
        P("groups", None, None),
        P("groups", ("outc", "inc"), None, None),
        P("groups"),
        P("groups"),
    )
    return jax.shard_map(
        functools.partial(shards, n, 1),
        mesh=mesh,
        in_specs=placed,
        out_specs=(
            P(("groups", "outc"), "inc"),
            P("groups", ("outc", "inc"), None, None),
            P("groups", None, ("outc", "inc"), None),
            P("groups", None, None),
        ),
        check_vma=False,
    )
```

```python
import functools

import jax
import jax.numpy as jnp
from jax import lax
from jax.experimental import pallas as pl
from jax.experimental.pallas import tpu as pltpu
from jax.sharding import PartitionSpec as P

HEADS = 128
G = 4
KW = 4
DRAFT = 8
LANES = 128
STREAMS = 2
BF = jnp.bfloat16
F32 = jnp.float32
HIGH = lax.Precision.HIGHEST
NT = (((1,), (1,)), ((), ()))
TN = (((0,), (0,)), ((), ()))
MIB = 1 << 20


def params(mib):
    return pltpu.CompilerParams(vmem_limit_bytes=mib * MIB)


def cost(flops, nbytes):
    return pl.CostEstimate(flops=int(flops), bytes_accessed=int(nbytes), transcendentals=0)


def whole_block(shape):
    return pl.BlockSpec(shape, lambda *_: (0,) * len(shape))


def relayout_kernel(heads, w_ref, o_ref, perm):
    kb = 256 // heads

    @pl.when(pl.program_id(0) == 0)
    def _():
        r = lax.broadcasted_iota(jnp.int32, (256, 256), 0)
        c = lax.broadcasted_iota(jnp.int32, (256, 256), 1)
        hit = (r // kb == lax.rem(c, heads)) & (lax.rem(r, kb) == c // heads)
        perm[...] = jnp.where(hit, 1.0, 0.0).astype(BF)

    bk = w_ref.shape[0]
    half = heads // 2
    for i in range(0, bk // kb, 2):
        first = w_ref[i * kb : (i + 1) * kb].reshape(256, LANES)
        second = w_ref[(i + 1) * kb : (i + 2) * kb].reshape(256, LANES)
        both = jnp.concatenate([first, second], axis=1)
        out = jnp.dot(perm[...], both, preferred_element_type=F32).astype(BF)
        for u in range(2):
            for h in range(heads):
                at = (h % half) * LANES
                o_ref[h // half, (i + u) * kb : (i + u + 1) * kb, at : at + LANES] = out[
                    h * kb : (h + 1) * kb, u * LANES : (u + 1) * LANES
                ]


def relayout(piece, pieces, w_zx, into, bk=512):
    k, heads, width = w_zx.shape
    cols = heads // 2 * width
    bk = min(bk, k // pieces)
    steps = k // bk // pieces
    kernel = functools.partial(relayout_kernel, heads)
    specs = [pl.BlockSpec((bk, heads, width), lambda i: (piece * steps + i, 0, 0))]
    args, aliases = [w_zx], {}
    if into is not None:
        args.append(into)
        specs.append(pl.BlockSpec(memory_space=pl.ANY))
        aliases = {1: 0}

        def kernel(w_ref, _, o_ref, perm):
            relayout_kernel(heads, w_ref, o_ref, perm)

    return pl.pallas_call(
        kernel,
        grid=(steps,),
        in_specs=specs,
        out_specs=pl.BlockSpec((2, bk, cols), lambda i: (0, piece * steps + i, 0)),
        out_shape=jax.ShapeDtypeStruct((2, k, cols), BF),
        scratch_shapes=[pltpu.VMEM((256, 256), BF)],
        input_output_aliases=aliases,
        compiler_params=params(52),
        cost_estimate=cost(2 * k * heads * width * 256 // pieces, 4 * k * heads * width // pieces),
        name="relayout",
    )(*args)


def project_kernel(parts, old, seq_ref, which_ref, *refs):
    ins, w_ref, ext_ref = refs[:parts], refs[parts], refs[parts + 1]
    rest = refs[parts + 2 :]
    olds, rest = rest[:old], rest[old:]
    o_ref, exts, rows = rest[0], rest[1:-1], rest[-1]
    piece = ins[0].shape[0]
    blocks = parts // STREAMS
    rc = piece * STREAMS

    def put(out, new, before):
        if not old:
            out[...] = new.astype(out.dtype)
            return
        for i in range(blocks):
            at = pl.ds(pl.multiple_of(seq_ref[i] * rc, 16), rc)
            out[at, :] = before[i * rc : (i + 1) * rc, :].astype(out.dtype)
            at = pl.ds(pl.multiple_of(seq_ref[blocks + i] * rc, 16), rc)
            out[at, :] = new[i * rc : (i + 1) * rc].astype(out.dtype)

    @pl.when(pl.program_id(0) == 0)
    def _():
        for i in range(parts):
            rows[i * piece : (i + 1) * piece, :] = ins[i][...]
        if exts:
            total = jnp.dot(rows[...], ext_ref[...], preferred_element_type=F32)
            for e in exts:
                put(e, total, olds[1] if old else None)

    total = jnp.dot(rows[...], w_ref[0], preferred_element_type=F32)
    put(o_ref, total, olds[0] if old else None)


def project(seq, which, ins, w, w_ext, dtype, ext_dtypes, olds=(), bn=512):
    parts = len(ins)
    rc, k = ins[0].shape
    m = rc * parts
    out_m = 2 * m if olds else m
    cols, ext_cols = w.shape[2], w_ext.shape[1]
    bn = min(bn, cols)
    in_specs = [whole_block((rc, k)) for _ in ins] + [
        pl.BlockSpec((1, k, bn), lambda j, seq, which: (which[0], 0, j)),
        whole_block((k, ext_cols)) if ext_dtypes else pl.BlockSpec(memory_space=pl.ANY),
    ]
    if olds:
        in_specs.append(pl.BlockSpec((m, bn), lambda j, seq, which: (0, j)))
        if ext_dtypes:
            in_specs.append(whole_block((m, ext_cols)))
    return pl.pallas_call(
        functools.partial(project_kernel, parts, len(olds)),
        grid_spec=pltpu.PrefetchScalarGridSpec(
            num_scalar_prefetch=2,
            grid=(cols // bn,),
            in_specs=in_specs,
            out_specs=[pl.BlockSpec((out_m, bn), lambda j, seq, which: (0, j))]
            + [whole_block((out_m, ext_cols)) for _ in ext_dtypes],
            scratch_shapes=[pltpu.VMEM((m, k), BF)],
        ),
        out_shape=[jax.ShapeDtypeStruct((out_m, cols), dtype)]
        + [jax.ShapeDtypeStruct((out_m, ext_cols), d) for d in ext_dtypes],
        compiler_params=params(46),
        cost_estimate=cost(2 * m * k * (cols + ext_cols), 2 * k * cols + 2 * m * k),
        name="project",
    )(seq, which, *ins, w, w_ext, *olds)


def extra_kernel(parts, seq_ref, *refs):
    ins, ext_ref, old_ref, o_ref, rows = refs[:parts], *refs[parts:]
    piece = ins[0].shape[0]
    blocks = parts // STREAMS
    rc = piece * STREAMS
    for i in range(parts):
        rows[i * piece : (i + 1) * piece, :] = ins[i][...]
    total = jnp.dot(rows[...], ext_ref[...], preferred_element_type=F32)
    for i in range(blocks):
        at = pl.ds(pl.multiple_of(seq_ref[i] * rc, 16), rc)
        o_ref[at, :] = old_ref[i * rc : (i + 1) * rc, :]
        at = pl.ds(pl.multiple_of(seq_ref[blocks + i] * rc, 16), rc)
        o_ref[at, :] = total[i * rc : (i + 1) * rc]


def extra(seq, ins, w_ext, old):
    parts = len(ins)
    piece, k = ins[0].shape
    m, cols = old.shape
    args = [*ins, w_ext, old]
    return pl.pallas_call(
        functools.partial(extra_kernel, parts),
        grid_spec=pltpu.PrefetchScalarGridSpec(
            num_scalar_prefetch=1,
            grid=(1,),
            in_specs=[whole_block(a.shape) for a in args],
            out_specs=whole_block((2 * m, cols)),
            scratch_shapes=[pltpu.VMEM((m, k), BF)],
        ),
        out_shape=jax.ShapeDtypeStruct((2 * m, cols), F32),
        compiler_params=params(46),
        cost_estimate=cost(2 * m * k * cols, 2 * m * k + 2 * k * cols),
        name="extra",
    )(seq, *args)


def silu(v):
    return v / (1.0 + jnp.exp(-v))


def history_rows(state):
    state = state.astype(F32)
    return jnp.concatenate([jnp.zeros((state.shape[0], DRAFT - KW + 1, state.shape[2]), F32), state], axis=1)


def ssm_kernel(
    group_ref, meta_ref, recv_ref, mine_ref, dt_ref, braw_ref, craw_ref, prevx_ref, prevb_ref, prevc_ref,
    tapx_ref, tapb_ref, tapc_ref, heads_ref, gain_ref, state_ref,
    gated_ref, ssq_ref, xw_ref, bconv_ref, sw_ref, xraw_ref,
):
    rb = recv_ref.shape[0]
    hp = gated_ref.shape[1]
    pairs = hp // LANES
    ss = meta_ref[..., 0:1].reshape(rb, 1)
    acc = meta_ref[..., 1:2].reshape(rb, 1)
    t = lax.broadcasted_iota(jnp.int32, (rb, 1), 0) & (DRAFT - 1)
    low = lax.broadcasted_iota(jnp.int32, (rb, LANES), 1) < LANES // 2
    seen = [
        jnp.where((t < ss) | (t - d >= ss), 1.0, 0.0).reshape(rb // DRAFT, DRAFT, 1) for d in range(KW)
    ]
    t3 = t.reshape(rb // DRAFT, DRAFT, 1)

    def pair(v, j):
        return jnp.concatenate([v[2 * j : 2 * j + 1, :], v[2 * j + 1 : 2 * j + 2, :]], axis=1)

    def conv(x, p3, taps):
        width = x.shape[1]
        x3 = x.reshape(rb // DRAFT, DRAFT, width)
        total = x3 * taps[KW - 1 : KW, :].reshape(1, 1, width)
        for d in range(1, KW):
            source = jnp.where(t3 >= d, pltpu.roll(x3, d, 1), pltpu.roll(p3, d, 1))
            total = total + (source * seen[d]) * taps[KW - 1 - d : KW - d, :].reshape(1, 1, width)
        return silu(total).reshape(rb, width)

    zx = (mine_ref[...].astype(F32) + recv_ref[...].astype(F32)).astype(BF).astype(F32)
    gates, xs = [], []
    for j in range(pairs):
        a = zx[:, 2 * j * LANES : (2 * j + 1) * LANES]
        b = zx[:, (2 * j + 1) * LANES : (2 * j + 2) * LANES]
        gates.append(jnp.where(low, a, pltpu.roll(b, LANES // 2, 1)))
        xs.append(jnp.where(low, pltpu.roll(a, LANES // 2, 1), b))
    prev_x = history_rows(prevx_ref[...])
    convs = []
    for j in range(pairs):
        cut = slice(j * LANES, (j + 1) * LANES)
        xraw_ref[:, cut] = xs[j].astype(BF)
        taps = jnp.concatenate([pair(tapx_ref[k], j) for k in range(KW)], axis=0)
        convs.append(conv(xs[j], prev_x[:, :, cut], taps))
    b_conv = conv(braw_ref[...].astype(F32), history_rows(prevb_ref[...]), tapb_ref[...])
    c_conv = conv(craw_ref[...].astype(F32), history_rows(prevc_ref[...]), tapc_ref[...])
    bconv_ref[...] = b_conv.astype(BF)

    raw = dt_ref[...].astype(F32) + heads_ref[0:1, :]
    step = jnp.maximum(raw, 0.0) + jnp.log1p(jnp.exp(-jnp.abs(raw)))
    log_a = -step * heads_ref[1:2, :]
    ri = lax.broadcasted_iota(jnp.int32, (rb, rb), 0)
    ci = lax.broadcasted_iota(jnp.int32, (rb, rb), 1)
    same = (ri // DRAFT) == (ci // DRAFT)
    tt, tq = ri & (DRAFT - 1), ci & (DRAFT - 1)
    lower = same & (tq <= tt)
    linked = lower & jnp.logical_not((tq < ss) & (ss <= tt))
    cum = jnp.dot(jnp.where(lower, 1.0, 0.0), log_a, precision=HIGH, preferred_element_type=F32)
    cum_acc = jnp.dot(
        jnp.where(same & (tq < acc), 1.0, 0.0), log_a, precision=HIGH, preferred_element_type=F32
    )
    cum_t = cum.T
    step_t = step.T
    scores = lax.dot_general(c_conv, b_conv, NT, precision=HIGH, preferred_element_type=F32)

    def spread(v, j):
        return jnp.where(low[: v.shape[0]], v[:, 2 * j : 2 * j + 1], v[:, 2 * j + 1 : 2 * j + 2])

    odd = (lax.broadcasted_iota(jnp.int32, (rb, 1), 0) & DRAFT) != 0
    c_pair = jnp.concatenate(
        [jnp.where(odd, 0.0, c_conv).astype(BF), jnp.where(odd, c_conv, 0.0).astype(BF)], axis=1
    )
    state = state_ref[...].reshape(rb // DRAFT, hp, LANES)
    carried = []
    for i in range(rb // (2 * DRAFT)):
        both = jnp.concatenate([state[2 * i], state[2 * i + 1]], axis=1)
        carried.append(
            lax.dot_general(
                c_pair[2 * DRAFT * i : 2 * DRAFT * (i + 1)], both, NT, preferred_element_type=F32
            )
        )
    carried = jnp.concatenate(carried, axis=0)

    kept = jnp.where(t < ss, jnp.exp(cum), 0.0)
    counted = (t < acc) & jnp.logical_not((t < ss) & (ss < acc))
    weight = jnp.where(counted, jnp.exp(jnp.where(counted, cum_acc - cum, 0.0)), 0.0) * step
    sw_ref[...] = jnp.where(ss < acc, 0.0, jnp.exp(cum_acc))
    skip = heads_ref[2:3, :]
    squares = jnp.zeros((rb, LANES), F32)
    for j in range(pairs):
        cut = slice(j * LANES, (j + 1) * LANES)
        mixes = []
        for h in (2 * j, 2 * j + 1):
            gap = cum[:, h : h + 1] - cum_t[h : h + 1, :]
            mixes.append((jnp.exp(jnp.where(linked, gap, -1e30)) * (scores * step_t[h : h + 1, :])).astype(BF))
        x_conv = convs[j]
        x_pair = jnp.concatenate(
            [jnp.where(low, x_conv, 0.0).astype(BF), jnp.where(low, 0.0, x_conv).astype(BF)], axis=0
        )
        intra = jnp.dot(jnp.concatenate(mixes, axis=1), x_pair, preferred_element_type=F32)
        mixed = spread(kept, j) * carried[:, cut] + intra + spread(skip, j) * x_conv
        gated = mixed * silu(gates[j])
        squares = squares + gated * gated
        gated_ref[:, cut] = (gated * pair(gain_ref, j)).astype(BF)
        xw_ref[:, cut] = (spread(weight, j) * x_conv).astype(BF)
    row_sum = jnp.broadcast_to(jnp.sum(squares, axis=1, keepdims=True), (rb, LANES))
    ssq_ref[...] = row_sum.T[:8]


def pick_tail(ss, acc, raw, prev):
    rb = raw.shape[0]
    ri = lax.broadcasted_iota(jnp.int32, (rb, rb), 0)
    ci = lax.broadcasted_iota(jnp.int32, (rb, rb), 1)
    same = (ri // DRAFT) == (ci // DRAFT)
    j, q = ri & (DRAFT - 1), ci & (DRAFT - 1)
    source = acc + j - (KW - 1)
    live = same & (j < KW - 1) & jnp.logical_not((source < ss) & (ss < acc))
    new = jnp.where(live & (q == source), 1.0, 0.0).astype(BF)
    old = jnp.where(live & (q == source + DRAFT), 1.0, 0.0).astype(BF)
    return jnp.dot(new, raw.astype(BF), preferred_element_type=F32) + jnp.dot(
        old, prev.astype(BF), preferred_element_type=F32
    )


def ssm(group, rb, meta, recv, mine, dt, b_raw, c_raw, x_state, bc_state, conv_x, conv_bc, heads, gain, state):
    rows = recv.shape[0]
    _, _, rq, hp, width_n = state.shape
    ob = rb // (rq * DRAFT)
    reqs = rb // DRAFT

    def flat(w):
        return pl.BlockSpec((rb, w), lambda i, group: (i, 0))

    def columns(shape, which):
        lead = (0,) * (len(shape) - 1)
        if len(shape) == 3:
            return pl.BlockSpec(shape, lambda i, group: (i, 0, which * G + group[0]))
        return pl.BlockSpec(shape, lambda i, group: (*lead, which * G + group[0]))

    return pl.pallas_call(
        ssm_kernel,
        grid_spec=pltpu.PrefetchScalarGridSpec(
            num_scalar_prefetch=1,
            grid=(rows // rb,),
            in_specs=[
                flat(2),
                flat(recv.shape[1]),
                flat(mine.shape[1]),
                flat(LANES),
                flat(LANES),
                flat(LANES),
                pl.BlockSpec((reqs, KW - 1, hp), lambda i, group: (i, 0, 0)),
                columns((reqs, KW - 1, LANES), 0),
                columns((reqs, KW - 1, LANES), 1),
                whole_block(conv_x.shape),
                columns((KW, LANES), 0),
                columns((KW, LANES), 1),
                whole_block(heads.shape),
                whole_block(gain.shape),
                pl.BlockSpec((ob, 1, rq, hp, width_n), lambda i, group: (i, 0, 0, 0, 0)),
            ],
            out_specs=[
                flat(hp),
                pl.BlockSpec((8, rb), lambda i, group: (0, i)),
                flat(hp),
                flat(LANES),
                flat(LANES),
                flat(hp),
            ],
        ),
        out_shape=[
            jax.ShapeDtypeStruct((rows, hp), BF),
            jax.ShapeDtypeStruct((8, rows), F32),
            jax.ShapeDtypeStruct((rows, hp), BF),
            jax.ShapeDtypeStruct((rows, LANES), BF),
            jax.ShapeDtypeStruct((rows, LANES), F32),
            jax.ShapeDtypeStruct((rows, hp), BF),
        ],
        compiler_params=params(46),
        cost_estimate=cost(2 * rows * hp * 4096, 6 * rows * hp * 16),
        name="ssm",
    )(group, meta, recv, mine, dt, b_raw, c_raw, x_state, bc_state, bc_state, conv_x, conv_bc, conv_bc, heads, gain, state)


def state_kernel(meta_ref, xw_ref, bconv_ref, sw_ref, xraw_ref, prevx_ref, state_ref, o_ref, tail_ref):
    rb, hp = xw_ref.shape
    width_p = LANES // 2
    ss = meta_ref[..., 0:1].reshape(rb, 1)
    acc = meta_ref[..., 1:2].reshape(rb, 1)
    tail_ref[...] = pick_tail(ss, acc, xraw_ref[...], history_rows(prevx_ref[...]).reshape(rb, hp)).astype(BF)
    request = lax.broadcasted_iota(jnp.int32, (rb, 1), 0) // DRAFT
    b_conv = bconv_ref[...].astype(F32)
    xw_t = xw_ref[...].astype(F32).T.astype(BF)
    rq = state_ref.shape[2]
    sw = sw_ref[...]
    for i in range(0, rb // DRAFT, 2):
        both = jnp.concatenate(
            [jnp.where(request == i + u, b_conv, 0.0).astype(BF) for u in range(2)], axis=1
        )
        added = jnp.dot(xw_t, both, preferred_element_type=F32)
        for u in range(2):
            r = i + u
            for h in range(hp // width_p):
                cut = slice(h * width_p, (h + 1) * width_p)
                old = state_ref[r // rq, 0, r % rq, cut, :].astype(F32)
                new = sw[r * DRAFT : r * DRAFT + 1, h : h + 1] * old + added[cut, u * LANES : (u + 1) * LANES]
                o_ref[r // rq, 0, r % rq, cut, :] = new.astype(BF)


def tail_kernel(meta_ref, raw_ref, prev_ref, o_ref):
    rb = raw_ref.shape[0]
    ss = meta_ref[..., 0:1].reshape(rb, 1)
    acc = meta_ref[..., 1:2].reshape(rb, 1)
    o_ref[...] = pick_tail(ss, acc, raw_ref[...], history_rows(prev_ref[...]).reshape(raw_ref.shape)).astype(BF)


def new_history(rb, meta, raw, prev):
    rows, cols = raw.shape

    def flat(w):
        return pl.BlockSpec((rb, w), lambda i: (i, 0))

    return pl.pallas_call(
        tail_kernel,
        grid=(rows // rb,),
        in_specs=[flat(2), flat(cols), pl.BlockSpec((rb // DRAFT, KW - 1, cols), lambda i: (i, 0, 0))],
        out_specs=flat(cols),
        out_shape=jax.ShapeDtypeStruct((rows, cols), BF),
        compiler_params=params(24),
        cost_estimate=cost(4 * rows * rb * cols, 6 * rows * cols),
        name="new_history",
    )(meta, raw, prev)


def new_state(piece, pieces, rb, meta, xw, bconv, sw, xraw, prev_x, state, into):
    rows, hp = xw.shape
    n, _, rq, _, width_n = state.shape
    ob = rb // (rq * DRAFT)
    steps = rows // rb // pieces
    first = piece * steps

    def flat(w):
        return pl.BlockSpec((rb, w), lambda i: (first + i, 0))

    states = pl.BlockSpec((ob, 1, rq, hp, width_n), lambda i: (first + i, 0, 0, 0, 0))
    args = [meta, xw, bconv, sw, xraw, prev_x, state]
    specs = [
        flat(2),
        flat(hp),
        flat(LANES),
        flat(LANES),
        flat(hp),
        pl.BlockSpec((rb // DRAFT, KW - 1, hp), lambda i: (first + i, 0, 0)),
        states,
    ]
    kernel, aliases = state_kernel, {}
    if into is not None:
        args.append(into)
        specs.append(pl.BlockSpec(memory_space=pl.ANY))
        aliases = {7: 0}

        def kernel(*refs):
            return state_kernel(*refs[:7], *refs[8:])

    return pl.pallas_call(
        kernel,
        grid=(steps,),
        in_specs=specs,
        out_specs=[states, pl.BlockSpec((rb, hp), lambda i: (i, 0))],
        out_shape=[jax.ShapeDtypeStruct(state.shape, BF), jax.ShapeDtypeStruct((rows // pieces, hp), BF)],
        input_output_aliases=aliases,
        compiler_params=params(40),
        cost_estimate=cost(2 * rows * hp * 4096 // pieces, 8 * rows * hp * 16 // pieces),
        name="new_state",
    )(*args)


def out_kernel(scale_by, inc_ref, mine_ref, theirs_ref, w_mine_ref, w_theirs_ref, ssq_ref, o_ref):
    product = jnp.dot(mine_ref[...], w_mine_ref[...], preferred_element_type=F32) + jnp.dot(
        theirs_ref[...], w_theirs_ref[...], preferred_element_type=F32
    )
    scale = lax.rsqrt(ssq_ref[...] * scale_by + 1e-05)
    rows = scale.shape[1]
    column = jnp.broadcast_to(scale[0:1], (LANES, rows)).T[:, 0:1]
    o_ref[...] = (product * column).astype(o_ref.dtype)


def out_project(inc, mine, theirs, w_out, ssq, scale_by, part, parts, bn=512):
    rows, hp = mine.shape
    cols = w_out.shape[1] // parts
    first = part * (cols // bn)
    return pl.pallas_call(
        functools.partial(out_kernel, scale_by),
        grid_spec=pltpu.PrefetchScalarGridSpec(
            num_scalar_prefetch=1,
            grid=(cols // bn,),
            in_specs=[
                pl.BlockSpec((rows, hp), lambda j, inc: (0, 0)),
                pl.BlockSpec((rows, hp), lambda j, inc: (0, 0)),
                pl.BlockSpec((hp, bn), lambda j, inc: (inc[0], first + j)),
                pl.BlockSpec((hp, bn), lambda j, inc: (1 - inc[0], first + j)),
                pl.BlockSpec((8, rows), lambda j, inc: (0, 0)),
            ],
            out_specs=pl.BlockSpec((rows, bn), lambda j, inc: (0, j)),
        ),
        out_shape=jax.ShapeDtypeStruct((rows, cols), BF),
        compiler_params=params(40),
        cost_estimate=cost(4 * rows * hp * cols, 4 * hp * cols + 4 * rows * cols),
        name="out_project",
    )(inc, mine, theirs, w_out, w_out, ssq)


def shards(n, chunks, tokens, w_zx, w_dt, w_bc, conv_x, conv_bc, dt_bias, decay_rate, skip_gain, norm_gain,
           w_out, conv_x_state, conv_bc_state, ssm_state, span_start, accepted):
    req, hd, width_p, width_n = ssm_state.shape
    hp = hd * width_p
    block_rows, half_d = tokens.shape
    cw = w_bc.shape[1]
    rc = block_rows // chunks
    rq = rc // DRAFT
    rows = n * rc
    rb = min(128, rows)
    order = list(range(0, n, 2)) + list(range(n - 1, 0, -2))
    ring = [(2 * order[i], 2 * order[(i + 1) % n]) for i in range(n)]
    ring += [(2 * order[(i + 1) % n] + 1, 2 * order[i] + 1) for i in range(n)]
    swap = [(0, 1), (1, 0)]
    me = lax.axis_index("outc")
    inc = lax.axis_index("inc")
    pos = jnp.where(me % 2 == 0, me // 2, n - 1 - me // 2)

    def owner(step):
        i = (pos + (2 * inc - 1) * step + n) % n
        return jnp.where(i < n // 2, 2 * i, 2 * n - 1 - 2 * i)

    seq = owner(jnp.arange(n, dtype=jnp.int32))
    inc1 = inc.astype(jnp.int32).reshape(1)

    def onward(a):
        return lax.ppermute(a, ("outc", "inc"), ring)

    def other(a):
        return lax.ppermute(a, "inc", swap)

    member = n // G
    group = me // member
    seat = me % member
    w_ext = jnp.concatenate([w_bc, w_dt, jnp.zeros((half_d, LANES - w_dt.shape[1]), BF)], axis=1)
    if w_ext.shape[1] % LANES:
        w_ext = jnp.pad(w_ext, ((0, 0), (0, LANES - w_ext.shape[1] % LANES)))

    def columns(a, start, size):
        return lax.dynamic_slice_in_dim(a, start, size, a.ndim - 1)

    x_state = conv_x_state.reshape(req, KW - 1, hp)
    own_state = columns(conv_bc_state, me * cw, cw)
    meta = jnp.stack([span_start, accepted], axis=-1).astype(jnp.int32)
    meta = jnp.broadcast_to(meta[:, None, :], (req, DRAFT, 2)).reshape(rows, 2)
    heads = jnp.pad(jnp.stack([dt_bias, decay_rate, skip_gain]), ((0, 5), (0, LANES - hd)))
    group1 = group.astype(jnp.int32).reshape(1)
    state = ssm_state.reshape(n, chunks, rq, hp, width_n)
    scale_by = 1.0 / (HEADS // G * width_p)

    pieces = 4
    w = None
    piece_rows = rc // STREAMS
    heads_of = [tokens[i * piece_rows : (i + 1) * piece_rows] for i in range(STREAMS)]
    blocks = list(heads_of)
    first = n // 2
    split = first * STREAMS
    for s in range(n - 1):
        heads_of = [onward(a) for a in heads_of]
        lead = heads_of[0]
        if s < pieces:
            w = relayout(s, pieces, w_zx, w)
            lead, w = lax.optimization_barrier((lead, w))
        elif s == max(pieces, first):
            theirs_1, ext_1 = project(seq, 1 - inc1, blocks[:split], w, w_ext, BF, [F32])
            lead, theirs_1, ext_1 = lax.optimization_barrier((lead, theirs_1, ext_1))
        elif s == max(pieces, first) + 1:
            (mine_1,) = project(seq, inc1, blocks[:split], w, w_ext, F32, [])
            lead, mine_1 = lax.optimization_barrier((lead, mine_1))
        heads_of[0] = lead
        blocks += heads_of

    prepared = [meta, x_state, own_state, heads, w_ext]
    blocks[-1], prepared = lax.optimization_barrier((blocks[-1], prepared))
    meta, x_state, own_state, heads, w_ext = prepared

    ext = extra(seq, blocks[split:], w_ext, ext_1)
    ext_other = other(ext)
    (theirs,) = project(seq, 1 - inc1, blocks[split:], w, w_ext, BF, [], (theirs_1,))
    theirs, ext, ext_other = lax.optimization_barrier((theirs, ext, ext_other))
    ext = (ext + ext_other).astype(BF)
    bc_own = ext[:, :cw]
    dt = columns(ext[:, cw : cw + 2 * hd], inc * hd, hd)
    dt = jnp.pad(dt, ((0, 0), (0, LANES - hd)))
    got = []
    for k in range(member):
        pairs = []
        for g in range(G):
            width = member // 2
            sources = [g * width + i for i in range(width)] + [n // 2 + g * width + i for i in range(width)]
            for i in range(member):
                pairs.append((sources[(i + k) % member], g * member + i))
        got.append(lax.ppermute(bc_own, "outc", pairs))
    picked = []
    for i in range(member):
        piece = got[0]
        for k in range(1, member):
            piece = jnp.where((i - seat) % member == k, got[k], piece)
        picked.append(piece)
    b_raw = jnp.concatenate(picked[: member // 2], axis=1)
    c_raw = jnp.concatenate(picked[member // 2 :], axis=1)
    theirs = other(theirs)
    late, bc_own, dt = lax.optimization_barrier((blocks[-1], bc_own, dt))
    blocks[-1] = late
    (mine,) = project(seq, inc1, blocks[split:], w, w_ext, F32, [], (mine_1,))
    gated, ssq, xw, bconv, sw, xraw = ssm(
        group1, rb, meta, theirs, mine, dt, b_raw, c_raw, x_state, conv_bc_state, conv_x, conv_bc, heads, norm_gain, state
    )

    def tails(a):
        return a.reshape(req, DRAFT, a.shape[-1])[:, : KW - 1]

    gated_theirs = other(gated)
    ssq = ssq + other(ssq)
    bc_own, gated, ssq = lax.optimization_barrier((bc_own, gated, ssq))
    d = 1
    while d < member:
        ssq = ssq + lax.ppermute(ssq, "outc", [(i, i ^ d) for i in range(n)])
        d *= 2
    history_bc = new_history(rb, meta, bc_own, own_state)
    history_bc = history_bc.reshape(req, DRAFT, cw)[:, : KW - 1].reshape(req * (KW - 1), cw)
    half_rows = req * (KW - 1) // 2
    history_bc = lax.dynamic_slice_in_dim(history_bc, inc * half_rows, half_rows, 0)
    widths = [n >> (i + 1) for i in range(n.bit_length() - 1)]

    def double(a, i):
        got = lax.ppermute(a, "outc", [(k, k ^ widths[i]) for k in range(n)])
        return jnp.where((me & widths[i]) != 0, jnp.stack([got, a], i), jnp.stack([a, got], i))

    history_bc = double(history_bc, 0)
    gated_theirs, ssq, history_bc = lax.optimization_barrier((gated_theirs, ssq, history_bc))
    history_bc = double(history_bc, 1)

    sums, partials = [], []

    def part(i, s):
        return lax.dynamic_slice_in_dim(partials[i], owner((s + 1) % n) * rc, rc, 0)

    for i in range(STREAMS):
        partials.append(out_project(inc1, gated, gated_theirs, w_out, ssq, scale_by, i, STREAMS))
        if i == 0:
            partials[0], history_bc = lax.optimization_barrier((partials[0], history_bc))
            for k in range(2, len(widths)):
                history_bc = double(history_bc, k)
        sums.append(part(i, 0))
    history_bc, sums[1] = lax.optimization_barrier((history_bc, sums[1]))
    history_bc = history_bc.reshape(n, half_rows, cw)
    history_other = other(history_bc)
    history_bc = jnp.where(
        inc != 0,
        jnp.concatenate([history_other, history_bc], axis=1),
        jnp.concatenate([history_bc, history_other], axis=1),
    )
    tails_x = []
    after = None
    for s in range(n - 1):
        if s in (1, 2):
            after, tail = new_state(s - 1, 2, rb, meta, xw, bconv, sw, xraw, x_state, state, after)
            tails_x.append(tail)
            after, sums[0] = lax.optimization_barrier((after, sums[0]))
        for i in range(STREAMS):
            sums[i] = (onward(sums[i]).astype(F32) + part(i, s + 1).astype(F32)).astype(BF)
    new_bc = jnp.swapaxes(history_bc, 0, 1).reshape(req, KW - 1, n * cw)
    new_x = tails(jnp.concatenate(tails_x, axis=0)).reshape(req, KW - 1, hd, width_p)
    return jnp.concatenate(sums, axis=1), after.reshape(ssm_state.shape), new_x, new_bc


def solution(mesh):
    n = mesh.shape["outc"]
    placed = (
        P(("groups", "outc"), "inc"),
        P("inc", "outc", None),
        P("inc", "outc"),
        P("inc", "outc"),
        P(None, ("outc", "inc"), None),
        P(),
        P(("outc", "inc")),
        P(("outc", "inc")),
        P(("outc", "inc")),
        P(("outc", "inc"), None),
        P("outc", "inc"),
        P("groups", None, ("outc", "inc"), None),
        P("groups", None, None),
        P("groups", ("outc", "inc"), None, None),
        P("groups"),
        P("groups"),
    )
    return jax.shard_map(
        functools.partial(shards, n, 1),
        mesh=mesh,
        in_specs=placed,
        out_specs=(
            P(("groups", "outc"), "inc"),
            P("groups", ("outc", "inc"), None, None),
            P("groups", None, ("outc", "inc"), None),
            P("groups", None, None),
        ),
        check_vma=False,
    )
```

```python
import functools

import jax
import jax.numpy as jnp
from jax import lax
from jax.experimental import pallas as pl
from jax.experimental.pallas import tpu as pltpu
from jax.sharding import PartitionSpec as P

HEADS = 128
G = 4
KW = 4
DRAFT = 8
LANES = 128
STREAMS = 2
BF = jnp.bfloat16
F32 = jnp.float32
HIGH = lax.Precision.HIGHEST
NT = (((1,), (1,)), ((), ()))
TN = (((0,), (0,)), ((), ()))
MIB = 1 << 20


def params(mib):
    return pltpu.CompilerParams(vmem_limit_bytes=mib * MIB)


def cost(flops, nbytes):
    return pl.CostEstimate(flops=int(flops), bytes_accessed=int(nbytes), transcendentals=0)


def whole_block(shape):
    return pl.BlockSpec(shape, lambda *_: (0,) * len(shape))


def relayout_kernel(heads, w_ref, o_ref, perm):
    kb = 256 // heads

    @pl.when(pl.program_id(0) == 0)
    def _():
        r = lax.broadcasted_iota(jnp.int32, (256, 256), 0)
        c = lax.broadcasted_iota(jnp.int32, (256, 256), 1)
        hit = (r // kb == lax.rem(c, heads)) & (lax.rem(r, kb) == c // heads)
        perm[...] = jnp.where(hit, 1.0, 0.0).astype(BF)

    bk = w_ref.shape[0]
    half = heads // 2
    for i in range(0, bk // kb, 2):
        first = w_ref[i * kb : (i + 1) * kb].reshape(256, LANES)
        second = w_ref[(i + 1) * kb : (i + 2) * kb].reshape(256, LANES)
        both = jnp.concatenate([first, second], axis=1)
        out = jnp.dot(perm[...], both, preferred_element_type=F32).astype(BF)
        for u in range(2):
            for h in range(heads):
                at = (h % half) * LANES
                o_ref[h // half, (i + u) * kb : (i + u + 1) * kb, at : at + LANES] = out[
                    h * kb : (h + 1) * kb, u * LANES : (u + 1) * LANES
                ]


def relayout(piece, pieces, w_zx, into, bk=512):
    k, heads, width = w_zx.shape
    cols = heads // 2 * width
    bk = min(bk, k // pieces)
    steps = k // bk // pieces
    kernel = functools.partial(relayout_kernel, heads)
    specs = [pl.BlockSpec((bk, heads, width), lambda i: (piece * steps + i, 0, 0))]
    args, aliases = [w_zx], {}
    if into is not None:
        args.append(into)
        specs.append(pl.BlockSpec(memory_space=pl.ANY))
        aliases = {1: 0}

        def kernel(w_ref, _, o_ref, perm):
            relayout_kernel(heads, w_ref, o_ref, perm)

    return pl.pallas_call(
        kernel,
        grid=(steps,),
        in_specs=specs,
        out_specs=pl.BlockSpec((2, bk, cols), lambda i: (0, piece * steps + i, 0)),
        out_shape=jax.ShapeDtypeStruct((2, k, cols), BF),
        scratch_shapes=[pltpu.VMEM((256, 256), BF)],
        input_output_aliases=aliases,
        compiler_params=params(52),
        cost_estimate=cost(2 * k * heads * width * 256 // pieces, 4 * k * heads * width // pieces),
        name="relayout",
    )(*args)


def project_kernel(parts, old, seq_ref, which_ref, *refs):
    ins, w_ref, ext_ref = refs[:parts], refs[parts], refs[parts + 1]
    rest = refs[parts + 2 :]
    olds, rest = rest[:old], rest[old:]
    o_ref, exts, rows = rest[0], rest[1:-1], rest[-1]
    piece = ins[0].shape[0]
    blocks = parts // STREAMS
    rc = piece * STREAMS

    def put(out, new, before):
        if not old:
            out[...] = new.astype(out.dtype)
            return
        for i in range(blocks):
            at = pl.ds(pl.multiple_of(seq_ref[i] * rc, 16), rc)
            out[at, :] = before[i * rc : (i + 1) * rc, :].astype(out.dtype)
            at = pl.ds(pl.multiple_of(seq_ref[blocks + i] * rc, 16), rc)
            out[at, :] = new[i * rc : (i + 1) * rc].astype(out.dtype)

    @pl.when(pl.program_id(0) == 0)
    def _():
        for i in range(parts):
            rows[i * piece : (i + 1) * piece, :] = ins[i][...]
        if exts:
            total = jnp.dot(rows[...], ext_ref[...], preferred_element_type=F32)
            for e in exts:
                put(e, total, olds[1] if old else None)

    total = jnp.dot(rows[...], w_ref[0], preferred_element_type=F32)
    put(o_ref, total, olds[0] if old else None)


def project(seq, which, ins, w, w_ext, dtype, ext_dtypes, olds=(), bn=512):
    parts = len(ins)
    rc, k = ins[0].shape
    m = rc * parts
    out_m = 2 * m if olds else m
    cols, ext_cols = w.shape[2], w_ext.shape[1]
    bn = min(bn, cols)
    in_specs = [whole_block((rc, k)) for _ in ins] + [
        pl.BlockSpec((1, k, bn), lambda j, seq, which: (which[0], 0, j)),
        whole_block((k, ext_cols)) if ext_dtypes else pl.BlockSpec(memory_space=pl.ANY),
    ]
    if olds:
        in_specs.append(pl.BlockSpec((m, bn), lambda j, seq, which: (0, j)))
        if ext_dtypes:
            in_specs.append(whole_block((m, ext_cols)))
    return pl.pallas_call(
        functools.partial(project_kernel, parts, len(olds)),
        grid_spec=pltpu.PrefetchScalarGridSpec(
            num_scalar_prefetch=2,
            grid=(cols // bn,),
            in_specs=in_specs,
            out_specs=[pl.BlockSpec((out_m, bn), lambda j, seq, which: (0, j))]
            + [whole_block((out_m, ext_cols)) for _ in ext_dtypes],
            scratch_shapes=[pltpu.VMEM((m, k), BF)],
        ),
        out_shape=[pltpu.HBM((out_m, cols), dtype)]
        + [pltpu.HBM((out_m, ext_cols), d) for d in ext_dtypes],
        compiler_params=params(46),
        cost_estimate=cost(2 * m * k * (cols + ext_cols), 2 * k * cols + 2 * m * k),
        name="project",
    )(seq, which, *ins, w, w_ext, *olds)


def extra_kernel(parts, seq_ref, *refs):
    ins, ext_ref, old_ref, o_ref, rows = refs[:parts], *refs[parts:]
    piece = ins[0].shape[0]
    blocks = parts // STREAMS
    rc = piece * STREAMS
    for i in range(parts):
        rows[i * piece : (i + 1) * piece, :] = ins[i][...]
    total = jnp.dot(rows[...], ext_ref[...], preferred_element_type=F32)
    for i in range(blocks):
        at = pl.ds(pl.multiple_of(seq_ref[i] * rc, 16), rc)
        o_ref[at, :] = old_ref[i * rc : (i + 1) * rc, :]
        at = pl.ds(pl.multiple_of(seq_ref[blocks + i] * rc, 16), rc)
        o_ref[at, :] = total[i * rc : (i + 1) * rc]


def extra(seq, ins, w_ext, old):
    parts = len(ins)
    piece, k = ins[0].shape
    m, cols = old.shape
    args = [*ins, w_ext, old]
    return pl.pallas_call(
        functools.partial(extra_kernel, parts),
        grid_spec=pltpu.PrefetchScalarGridSpec(
            num_scalar_prefetch=1,
            grid=(1,),
            in_specs=[whole_block(a.shape) for a in args],
            out_specs=whole_block((2 * m, cols)),
            scratch_shapes=[pltpu.VMEM((m, k), BF)],
        ),
        out_shape=jax.ShapeDtypeStruct((2 * m, cols), F32),
        compiler_params=params(46),
        cost_estimate=cost(2 * m * k * cols, 2 * m * k + 2 * k * cols),
        name="extra",
    )(seq, *args)


def silu(v):
    return v / (1.0 + jnp.exp(-v))


def history_rows(state):
    state = state.astype(F32)
    empty = jnp.zeros((state.shape[1], DRAFT - KW + 1, state.shape[2]), F32)
    return jnp.concatenate([empty, *[state[j][:, None, :] for j in range(KW - 1)]], axis=1)


def ssm_kernel(
    group_ref, meta_ref, recv_ref, mine_ref, dt_ref, braw_ref, craw_ref, prevx_ref, prevb_ref, prevc_ref,
    tapx_ref, tapb_ref, tapc_ref, heads_ref, gain_ref, state_ref,
    gated_ref, ssq_ref, xw_ref, bconv_ref, sw_ref, xraw_ref,
):
    rb = recv_ref.shape[0]
    hp = gated_ref.shape[1]
    pairs = hp // LANES
    ss = meta_ref[..., 0:1].reshape(rb, 1)
    acc = meta_ref[..., 1:2].reshape(rb, 1)
    t = lax.broadcasted_iota(jnp.int32, (rb, 1), 0) & (DRAFT - 1)
    low = lax.broadcasted_iota(jnp.int32, (rb, LANES), 1) < LANES // 2
    seen = [
        jnp.where((t < ss) | (t - d >= ss), 1.0, 0.0).reshape(rb // DRAFT, DRAFT, 1) for d in range(KW)
    ]
    t3 = t.reshape(rb // DRAFT, DRAFT, 1)

    def pair(v, j):
        return jnp.concatenate([v[2 * j : 2 * j + 1, :], v[2 * j + 1 : 2 * j + 2, :]], axis=1)

    def conv(x, p3, taps):
        width = x.shape[1]
        x3 = x.reshape(rb // DRAFT, DRAFT, width)
        total = x3 * taps[KW - 1 : KW, :].reshape(1, 1, width)
        for d in range(1, KW):
            source = jnp.where(t3 >= d, pltpu.roll(x3, d, 1), pltpu.roll(p3, d, 1))
            total = total + (source * seen[d]) * taps[KW - 1 - d : KW - d, :].reshape(1, 1, width)
        return silu(total).reshape(rb, width)

    zx = (mine_ref[...].astype(F32) + recv_ref[...].astype(F32)).astype(BF).astype(F32)
    gates, xs = [], []
    for j in range(pairs):
        a = zx[:, 2 * j * LANES : (2 * j + 1) * LANES]
        b = zx[:, (2 * j + 1) * LANES : (2 * j + 2) * LANES]
        gates.append(jnp.where(low, a, pltpu.roll(b, LANES // 2, 1)))
        xs.append(jnp.where(low, pltpu.roll(a, LANES // 2, 1), b))
    prev_x = history_rows(prevx_ref[...])
    convs = []
    for j in range(pairs):
        cut = slice(j * LANES, (j + 1) * LANES)
        xraw_ref[:, cut] = xs[j].astype(BF)
        taps = jnp.concatenate([pair(tapx_ref[k], j) for k in range(KW)], axis=0)
        convs.append(conv(xs[j], prev_x[:, :, cut], taps))
    b_conv = conv(braw_ref[...].astype(F32), history_rows(prevb_ref[...]), tapb_ref[...])
    c_conv = conv(craw_ref[...].astype(F32), history_rows(prevc_ref[...]), tapc_ref[...])
    bconv_ref[...] = b_conv.astype(BF)

    raw = dt_ref[...].astype(F32) + heads_ref[0:1, :]
    step = jnp.maximum(raw, 0.0) + jnp.log1p(jnp.exp(-jnp.abs(raw)))
    log_a = -step * heads_ref[1:2, :]
    ri = lax.broadcasted_iota(jnp.int32, (rb, rb), 0)
    ci = lax.broadcasted_iota(jnp.int32, (rb, rb), 1)
    same = (ri // DRAFT) == (ci // DRAFT)
    tt, tq = ri & (DRAFT - 1), ci & (DRAFT - 1)
    lower = same & (tq <= tt)
    linked = lower & jnp.logical_not((tq < ss) & (ss <= tt))
    cum = jnp.dot(jnp.where(lower, 1.0, 0.0), log_a, precision=HIGH, preferred_element_type=F32)
    cum_acc = jnp.dot(
        jnp.where(same & (tq < acc), 1.0, 0.0), log_a, precision=HIGH, preferred_element_type=F32
    )
    cum_t = cum.T
    step_t = step.T
    scores = lax.dot_general(c_conv, b_conv, NT, precision=HIGH, preferred_element_type=F32)

    def spread(v, j):
        return jnp.where(low[: v.shape[0]], v[:, 2 * j : 2 * j + 1], v[:, 2 * j + 1 : 2 * j + 2])

    odd = (lax.broadcasted_iota(jnp.int32, (rb, 1), 0) & DRAFT) != 0
    c_pair = jnp.concatenate(
        [jnp.where(odd, 0.0, c_conv).astype(BF), jnp.where(odd, c_conv, 0.0).astype(BF)], axis=1
    )
    state = state_ref[...].reshape(rb // DRAFT, hp, LANES)
    carried = []
    for i in range(rb // (2 * DRAFT)):
        both = jnp.concatenate([state[2 * i], state[2 * i + 1]], axis=1)
        carried.append(
            lax.dot_general(
                c_pair[2 * DRAFT * i : 2 * DRAFT * (i + 1)], both, NT, preferred_element_type=F32
            )
        )
    carried = jnp.concatenate(carried, axis=0)

    kept = jnp.where(t < ss, jnp.exp(cum), 0.0)
    counted = (t < acc) & jnp.logical_not((t < ss) & (ss < acc))
    weight = jnp.where(counted, jnp.exp(jnp.where(counted, cum_acc - cum, 0.0)), 0.0) * step
    sw_ref[...] = jnp.where(ss < acc, 0.0, jnp.exp(cum_acc))
    skip = heads_ref[2:3, :]
    squares = jnp.zeros((rb, LANES), F32)
    for j in range(pairs):
        cut = slice(j * LANES, (j + 1) * LANES)
        mixes = []
        for h in (2 * j, 2 * j + 1):
            gap = cum[:, h : h + 1] - cum_t[h : h + 1, :]
            mixes.append((jnp.exp(jnp.where(linked, gap, -1e30)) * (scores * step_t[h : h + 1, :])).astype(BF))
        x_conv = convs[j]
        x_pair = jnp.concatenate(
            [jnp.where(low, x_conv, 0.0).astype(BF), jnp.where(low, 0.0, x_conv).astype(BF)], axis=0
        )
        intra = jnp.dot(jnp.concatenate(mixes, axis=1), x_pair, preferred_element_type=F32)
        mixed = spread(kept, j) * carried[:, cut] + intra + spread(skip, j) * x_conv
        gated = mixed * silu(gates[j])
        squares = squares + gated * gated
        gated_ref[:, cut] = (gated * pair(gain_ref, j)).astype(BF)
        xw_ref[:, cut] = (spread(weight, j) * x_conv).astype(BF)
    row_sum = jnp.broadcast_to(jnp.sum(squares, axis=1, keepdims=True), (rb, LANES))
    ssq_ref[...] = row_sum.T[:8]


def pick_tail(ss, acc, raw, prev):
    rb = raw.shape[0]
    ri = lax.broadcasted_iota(jnp.int32, (rb, rb), 0)
    ci = lax.broadcasted_iota(jnp.int32, (rb, rb), 1)
    same = (ri // DRAFT) == (ci // DRAFT)
    j, q = ri & (DRAFT - 1), ci & (DRAFT - 1)
    source = acc + j - (KW - 1)
    live = same & (j < KW - 1) & jnp.logical_not((source < ss) & (ss < acc))
    new = jnp.where(live & (q == source), 1.0, 0.0).astype(BF)
    old = jnp.where(live & (q == source + DRAFT), 1.0, 0.0).astype(BF)
    return jnp.dot(new, raw.astype(BF), preferred_element_type=F32) + jnp.dot(
        old, prev.astype(BF), preferred_element_type=F32
    )


def ssm(group, rb, meta, recv, mine, dt, b_raw, c_raw, x_state, bc_state, conv_x, conv_bc, heads, gain, state):
    rows = recv.shape[0]
    _, _, rq, hp, width_n = state.shape
    ob = rb // (rq * DRAFT)
    reqs = rb // DRAFT

    def flat(w):
        return pl.BlockSpec((rb, w), lambda i, group: (i, 0))

    def columns(shape, which):
        lead = (0,) * (len(shape) - 1)
        if len(shape) == 3:
            return pl.BlockSpec(shape, lambda i, group: (0, i, which * G + group[0]))
        return pl.BlockSpec(shape, lambda i, group: (*lead, which * G + group[0]))

    return pl.pallas_call(
        ssm_kernel,
        grid_spec=pltpu.PrefetchScalarGridSpec(
            num_scalar_prefetch=1,
            grid=(rows // rb,),
            in_specs=[
                flat(2),
                flat(recv.shape[1]),
                flat(mine.shape[1]),
                flat(LANES),
                flat(LANES),
                flat(LANES),
                pl.BlockSpec((KW - 1, reqs, hp), lambda i, group: (0, i, 0)),
                columns((KW - 1, reqs, LANES), 0),
                columns((KW - 1, reqs, LANES), 1),
                whole_block(conv_x.shape),
                columns((KW, LANES), 0),
                columns((KW, LANES), 1),
                whole_block(heads.shape),
                whole_block(gain.shape),
                pl.BlockSpec((ob, 1, rq, hp, width_n), lambda i, group: (i, 0, 0, 0, 0)),
            ],
            out_specs=[
                flat(hp),
                pl.BlockSpec((8, rb), lambda i, group: (0, i)),
                flat(hp),
                flat(LANES),
                flat(LANES),
                flat(hp),
            ],
        ),
        out_shape=[
            jax.ShapeDtypeStruct((rows, hp), BF),
            jax.ShapeDtypeStruct((8, rows), F32),
            pltpu.HBM((rows, hp), BF),
            pltpu.HBM((rows, LANES), BF),
            pltpu.HBM((rows, LANES), F32),
            pltpu.HBM((rows, hp), BF),
        ],
        compiler_params=params(46),
        cost_estimate=cost(2 * rows * hp * 4096, 6 * rows * hp * 16),
        name="ssm",
    )(group, meta, recv, mine, dt, b_raw, c_raw, x_state, bc_state, bc_state, conv_x, conv_bc, conv_bc, heads, gain, state)


def state_kernel(meta_ref, xw_ref, bconv_ref, sw_ref, xraw_ref, prevx_ref, state_ref, o_ref, tail_ref):
    rb, hp = xw_ref.shape
    width_p = LANES // 2
    ss = meta_ref[..., 0:1].reshape(rb, 1)
    acc = meta_ref[..., 1:2].reshape(rb, 1)
    tail_ref[...] = pick_tail(ss, acc, xraw_ref[...], history_rows(prevx_ref[...]).reshape(rb, hp)).astype(BF)
    request = lax.broadcasted_iota(jnp.int32, (rb, 1), 0) // DRAFT
    b_conv = bconv_ref[...].astype(F32)
    xw_t = xw_ref[...].astype(F32).T.astype(BF)
    rq = state_ref.shape[2]
    sw = sw_ref[...]
    for i in range(0, rb // DRAFT, 2):
        both = jnp.concatenate(
            [jnp.where(request == i + u, b_conv, 0.0).astype(BF) for u in range(2)], axis=1
        )
        added = jnp.dot(xw_t, both, preferred_element_type=F32)
        for u in range(2):
            r = i + u
            for h in range(hp // width_p):
                cut = slice(h * width_p, (h + 1) * width_p)
                old = state_ref[r // rq, 0, r % rq, cut, :].astype(F32)
                new = sw[r * DRAFT : r * DRAFT + 1, h : h + 1] * old + added[cut, u * LANES : (u + 1) * LANES]
                o_ref[r // rq, 0, r % rq, cut, :] = new.astype(BF)


def tail_kernel(meta_ref, raw_ref, prev_ref, o_ref):
    rb = raw_ref.shape[0]
    ss = meta_ref[..., 0:1].reshape(rb, 1)
    acc = meta_ref[..., 1:2].reshape(rb, 1)
    o_ref[...] = pick_tail(ss, acc, raw_ref[...], history_rows(prev_ref[...]).reshape(raw_ref.shape)).astype(BF)


def new_history(rb, meta, raw, prev):
    rows, cols = raw.shape

    def flat(w):
        return pl.BlockSpec((rb, w), lambda i: (i, 0))

    return pl.pallas_call(
        tail_kernel,
        grid=(rows // rb,),
        in_specs=[flat(2), flat(cols), pl.BlockSpec((KW - 1, rb // DRAFT, cols), lambda i: (0, i, 0))],
        out_specs=flat(cols),
        out_shape=jax.ShapeDtypeStruct((rows, cols), BF),
        compiler_params=params(24),
        cost_estimate=cost(4 * rows * rb * cols, 6 * rows * cols),
        name="new_history",
    )(meta, raw, prev)


def new_state(piece, pieces, rb, meta, xw, bconv, sw, xraw, prev_x, state, into):
    rows, hp = xw.shape
    n, _, rq, _, width_n = state.shape
    ob = rb // (rq * DRAFT)
    steps = rows // rb // pieces
    first = piece * steps

    def flat(w):
        return pl.BlockSpec((rb, w), lambda i: (first + i, 0))

    states = pl.BlockSpec((ob, 1, rq, hp, width_n), lambda i: (first + i, 0, 0, 0, 0))
    args = [meta, xw, bconv, sw, xraw, prev_x, state]
    specs = [
        flat(2),
        flat(hp),
        flat(LANES),
        flat(LANES),
        flat(hp),
        pl.BlockSpec((KW - 1, rb // DRAFT, hp), lambda i: (0, first + i, 0)),
        states,
    ]
    kernel, aliases = state_kernel, {}
    if into is not None:
        args.append(into)
        specs.append(pl.BlockSpec(memory_space=pl.ANY))
        aliases = {7: 0}

        def kernel(*refs):
            return state_kernel(*refs[:7], *refs[8:])

    return pl.pallas_call(
        kernel,
        grid=(steps,),
        in_specs=specs,
        out_specs=[states, pl.BlockSpec((rb, hp), lambda i: (i, 0))],
        out_shape=[jax.ShapeDtypeStruct(state.shape, BF), jax.ShapeDtypeStruct((rows // pieces, hp), BF)],
        input_output_aliases=aliases,
        compiler_params=params(40),
        cost_estimate=cost(2 * rows * hp * 4096 // pieces, 8 * rows * hp * 16 // pieces),
        name="new_state",
    )(*args)


def out_kernel(scale_by, inc_ref, mine_ref, theirs_ref, w_mine_ref, w_theirs_ref, ssq_ref, o_ref):
    product = jnp.dot(mine_ref[...], w_mine_ref[...], preferred_element_type=F32) + jnp.dot(
        theirs_ref[...], w_theirs_ref[...], preferred_element_type=F32
    )
    scale = lax.rsqrt(ssq_ref[...] * scale_by + 1e-05)
    rows = scale.shape[1]
    column = jnp.broadcast_to(scale[0:1], (LANES, rows)).T[:, 0:1]
    o_ref[...] = (product * column).astype(o_ref.dtype)


def out_project(inc, mine, theirs, w_out, ssq, scale_by, part, parts, bn=512):
    rows, hp = mine.shape
    cols = w_out.shape[1] // parts
    first = part * (cols // bn)
    return pl.pallas_call(
        functools.partial(out_kernel, scale_by),
        grid_spec=pltpu.PrefetchScalarGridSpec(
            num_scalar_prefetch=1,
            grid=(cols // bn,),
            in_specs=[
                pl.BlockSpec((rows, hp), lambda j, inc: (0, 0)),
                pl.BlockSpec((rows, hp), lambda j, inc: (0, 0)),
                pl.BlockSpec((hp, bn), lambda j, inc: (inc[0], first + j)),
                pl.BlockSpec((hp, bn), lambda j, inc: (1 - inc[0], first + j)),
                pl.BlockSpec((8, rows), lambda j, inc: (0, 0)),
            ],
            out_specs=pl.BlockSpec((rows, bn), lambda j, inc: (0, j)),
        ),
        out_shape=jax.ShapeDtypeStruct((rows, cols), BF),
        compiler_params=params(40),
        cost_estimate=cost(4 * rows * hp * cols, 4 * hp * cols + 4 * rows * cols),
        name="out_project",
    )(inc, mine, theirs, w_out, w_out, ssq)


def shards(n, chunks, tokens, w_zx, w_dt, w_bc, conv_x, conv_bc, dt_bias, decay_rate, skip_gain, norm_gain,
           w_out, conv_x_state, conv_bc_state, ssm_state, span_start, accepted):
    req, hd, width_p, width_n = ssm_state.shape
    hp = hd * width_p
    block_rows, half_d = tokens.shape
    cw = w_bc.shape[1]
    rc = block_rows // chunks
    rq = rc // DRAFT
    rows = n * rc
    rb = min(128, rows)
    order = list(range(0, n, 2)) + list(range(n - 1, 0, -2))
    ring = [(2 * order[i], 2 * order[(i + 1) % n]) for i in range(n)]
    ring += [(2 * order[(i + 1) % n] + 1, 2 * order[i] + 1) for i in range(n)]
    swap = [(0, 1), (1, 0)]
    me = lax.axis_index("outc")
    inc = lax.axis_index("inc")
    pos = jnp.where(me % 2 == 0, me // 2, n - 1 - me // 2)

    def owner(step):
        i = (pos + (2 * inc - 1) * step + n) % n
        return jnp.where(i < n // 2, 2 * i, 2 * n - 1 - 2 * i)

    seq = owner(jnp.arange(n, dtype=jnp.int32))
    inc1 = inc.astype(jnp.int32).reshape(1)

    def onward(a):
        return lax.ppermute(a, ("outc", "inc"), ring)

    def other(a):
        return lax.ppermute(a, "inc", swap)

    member = n // G
    group = me // member
    seat = me % member
    w_ext = jnp.concatenate([w_bc, w_dt, jnp.zeros((half_d, LANES - w_dt.shape[1]), BF)], axis=1)
    if w_ext.shape[1] % LANES:
        w_ext = jnp.pad(w_ext, ((0, 0), (0, LANES - w_ext.shape[1] % LANES)))

    def columns(a, start, size):
        return lax.dynamic_slice_in_dim(a, start, size, a.ndim - 1)

    x_state = jnp.swapaxes(conv_x_state.reshape(req, KW - 1, hp), 0, 1)
    bc_state = jnp.swapaxes(conv_bc_state, 0, 1)
    own_state = columns(bc_state, me * cw, cw)
    meta = jnp.stack([span_start, accepted], axis=-1).astype(jnp.int32)
    meta = jnp.broadcast_to(meta[:, None, :], (req, DRAFT, 2)).reshape(rows, 2)
    heads = jnp.pad(jnp.stack([dt_bias, decay_rate, skip_gain]), ((0, 5), (0, LANES - hd)))
    group1 = group.astype(jnp.int32).reshape(1)
    state = ssm_state.reshape(n, chunks, rq, hp, width_n)
    scale_by = 1.0 / (HEADS // G * width_p)

    pieces = 4
    w = None
    piece_rows = rc // STREAMS
    heads_of = [tokens[i * piece_rows : (i + 1) * piece_rows] for i in range(STREAMS)]
    blocks = list(heads_of)
    first = n // 2
    split = first * STREAMS
    for s in range(n - 1):
        heads_of = [onward(a) for a in heads_of]
        lead = heads_of[0]
        if s < pieces:
            w = relayout(s, pieces, w_zx, w)
            lead, w = lax.optimization_barrier((lead, w))
        elif s == max(pieces, first):
            theirs_1, ext_1 = project(seq, 1 - inc1, blocks[:split], w, w_ext, BF, [F32])
            lead, theirs_1, ext_1 = lax.optimization_barrier((lead, theirs_1, ext_1))
        elif s == max(pieces, first) + 1:
            (mine_1,) = project(seq, inc1, blocks[:split], w, w_ext, F32, [])
            lead, mine_1 = lax.optimization_barrier((lead, mine_1))
        heads_of[0] = lead
        blocks += heads_of

    prepared = [meta, x_state, own_state, heads, w_ext]
    blocks[-1], prepared = lax.optimization_barrier((blocks[-1], prepared))
    meta, x_state, own_state, heads, w_ext = prepared

    ext = extra(seq, blocks[split:], w_ext, ext_1)
    ext_other = other(ext)
    (theirs,) = project(seq, 1 - inc1, blocks[split:], w, w_ext, BF, [], (theirs_1,))
    theirs, ext, ext_other = lax.optimization_barrier((theirs, ext, ext_other))
    ext = (ext + ext_other).astype(BF)
    bc_own = ext[:, :cw]
    dt = columns(ext[:, cw : cw + 2 * hd], inc * hd, hd)
    dt = jnp.pad(dt, ((0, 0), (0, LANES - hd)))
    got = []
    for k in range(member):
        pairs = []
        for g in range(G):
            width = member // 2
            sources = [g * width + i for i in range(width)] + [n // 2 + g * width + i for i in range(width)]
            for i in range(member):
                pairs.append((sources[(i + k) % member], g * member + i))
        got.append(lax.ppermute(bc_own, "outc", pairs))
    picked = []
    for i in range(member):
        piece = got[0]
        for k in range(1, member):
            piece = jnp.where((i - seat) % member == k, got[k], piece)
        picked.append(piece)
    b_raw = jnp.concatenate(picked[: member // 2], axis=1)
    c_raw = jnp.concatenate(picked[member // 2 :], axis=1)
    theirs = other(theirs)
    late, bc_own, dt = lax.optimization_barrier((blocks[-1], bc_own, dt))
    blocks[-1] = late
    (mine,) = project(seq, inc1, blocks[split:], w, w_ext, F32, [], (mine_1,))
    gated, ssq, xw, bconv, sw, xraw = ssm(
        group1, rb, meta, theirs, mine, dt, b_raw, c_raw, x_state, bc_state, conv_x, conv_bc, heads, norm_gain, state
    )

    def tails(a):
        return a.reshape(req, DRAFT, a.shape[-1])[:, : KW - 1]

    gated_theirs = other(gated)
    ssq = ssq + other(ssq)
    bc_own, gated, ssq = lax.optimization_barrier((bc_own, gated, ssq))
    d = 1
    while d < member:
        ssq = ssq + lax.ppermute(ssq, "outc", [(i, i ^ d) for i in range(n)])
        d *= 2
    history_bc = new_history(rb, meta, bc_own, own_state)
    history_bc = history_bc.reshape(req, DRAFT, cw)[:, : KW - 1].reshape(req * (KW - 1), cw)
    half_rows = req * (KW - 1) // 2
    history_bc = lax.dynamic_slice_in_dim(history_bc, inc * half_rows, half_rows, 0)
    widths = [n >> (i + 1) for i in range(n.bit_length() - 1)]

    def double(a, i):
        got = lax.ppermute(a, "outc", [(k, k ^ widths[i]) for k in range(n)])
        return jnp.where((me & widths[i]) != 0, jnp.stack([got, a], i), jnp.stack([a, got], i))

    history_bc = double(history_bc, 0)
    gated_theirs, ssq, history_bc = lax.optimization_barrier((gated_theirs, ssq, history_bc))
    history_bc = double(history_bc, 1)

    sums, partials = [], []

    def part(i, s):
        return lax.dynamic_slice_in_dim(partials[i], owner((s + 1) % n) * rc, rc, 0)

    for i in range(STREAMS):
        partials.append(out_project(inc1, gated, gated_theirs, w_out, ssq, scale_by, i, STREAMS))
        if i == 0:
            partials[0], history_bc = lax.optimization_barrier((partials[0], history_bc))
            for k in range(2, len(widths)):
                history_bc = double(history_bc, k)
        sums.append(part(i, 0))
    tails_x = []
    after = None
    for s in range(n - 1):
        if s in (0, 2):
            xw, sums[0] = lax.optimization_barrier((xw, sums[0]))
            piece = len(tails_x)
            after, tail = new_state(piece, 2, rb, meta, xw, bconv, sw, xraw, x_state, state, after)
            tails_x.append(tail)
            after, sums[0] = lax.optimization_barrier((after, sums[0]))
        if s == 3:
            history_bc, sums[0] = lax.optimization_barrier((history_bc, sums[0]))
            history_bc = history_bc.reshape(n, half_rows, cw)
            history_other = other(history_bc)
        if s == 4:
            history_other, sums[0] = lax.optimization_barrier((history_other, sums[0]))
            history_bc = jnp.where(
                inc != 0,
                jnp.concatenate([history_other, history_bc], axis=1),
                jnp.concatenate([history_bc, history_other], axis=1),
            )
        if s == 5:
            history_bc, tails_x, sums[1] = lax.optimization_barrier((history_bc, tails_x, sums[1]))
        for i in range(STREAMS):
            sums[i] = (onward(sums[i]).astype(F32) + part(i, s + 1).astype(F32)).astype(BF)
    new_bc = jnp.swapaxes(history_bc, 0, 1).reshape(req, KW - 1, n * cw)
    new_x = tails(jnp.concatenate(tails_x, axis=0)).reshape(req, KW - 1, hd, width_p)
    return jnp.concatenate(sums, axis=1), after.reshape(ssm_state.shape), new_x, new_bc


def solution(mesh):
    n = mesh.shape["outc"]
    placed = (
        P(("groups", "outc"), "inc"),
        P("inc", "outc", None),
        P("inc", "outc"),
        P("inc", "outc"),
        P(None, ("outc", "inc"), None),
        P(),
        P(("outc", "inc")),
        P(("outc", "inc")),
        P(("outc", "inc")),
        P(("outc", "inc"), None),
        P("outc", "inc"),
        P("groups", None, ("outc", "inc"), None),
        P("groups", None, None),
        P("groups", ("outc", "inc"), None, None),
        P("groups"),
        P("groups"),
    )
    return jax.shard_map(
        functools.partial(shards, n, 1),
        mesh=mesh,
        in_specs=placed,
        out_specs=(
            P(("groups", "outc"), "inc"),
            P("groups", ("outc", "inc"), None, None),
            P("groups", None, ("outc", "inc"), None),
            P("groups", None, None),
        ),
        check_vma=False,
    )
```

```python
import functools

import jax
import jax.numpy as jnp
from jax import lax
from jax.experimental import pallas as pl
from jax.experimental.pallas import tpu as pltpu
from jax.sharding import PartitionSpec as P

HEADS = 128
G = 4
KW = 4
DRAFT = 8
LANES = 128
STREAMS = 2
BF = jnp.bfloat16
F32 = jnp.float32
HIGH = lax.Precision.HIGHEST
NT = (((1,), (1,)), ((), ()))
TN = (((0,), (0,)), ((), ()))
MIB = 1 << 20


def params(mib):
    return pltpu.CompilerParams(vmem_limit_bytes=mib * MIB)


def cost(flops, nbytes):
    return pl.CostEstimate(flops=int(flops), bytes_accessed=int(nbytes), transcendentals=0)


def whole_block(shape):
    return pl.BlockSpec(shape, lambda *_: (0,) * len(shape))


def relayout_kernel(heads, w_ref, o_ref, perm):
    kb = 256 // heads

    @pl.when(pl.program_id(0) == 0)
    def _():
        r = lax.broadcasted_iota(jnp.int32, (256, 256), 0)
        c = lax.broadcasted_iota(jnp.int32, (256, 256), 1)
        hit = (r // kb == lax.rem(c, heads)) & (lax.rem(r, kb) == c // heads)
        perm[...] = jnp.where(hit, 1.0, 0.0).astype(BF)

    bk = w_ref.shape[0]
    half = heads // 2
    for i in range(0, bk // kb, 2):
        first = w_ref[i * kb : (i + 1) * kb].reshape(256, LANES)
        second = w_ref[(i + 1) * kb : (i + 2) * kb].reshape(256, LANES)
        both = jnp.concatenate([first, second], axis=1)
        out = jnp.dot(perm[...], both, preferred_element_type=F32).astype(BF)
        for u in range(2):
            for h in range(heads):
                at = (h % half) * LANES
                o_ref[h // half, (i + u) * kb : (i + u + 1) * kb, at : at + LANES] = out[
                    h * kb : (h + 1) * kb, u * LANES : (u + 1) * LANES
                ]


def relayout(piece, pieces, w_zx, into, bk=512):
    k, heads, width = w_zx.shape
    cols = heads // 2 * width
    bk = min(bk, k // pieces)
    steps = k // bk // pieces
    kernel = functools.partial(relayout_kernel, heads)
    specs = [pl.BlockSpec((bk, heads, width), lambda i: (piece * steps + i, 0, 0))]
    args, aliases = [w_zx], {}
    if into is not None:
        args.append(into)
        specs.append(pl.BlockSpec(memory_space=pl.ANY))
        aliases = {1: 0}

        def kernel(w_ref, _, o_ref, perm):
            relayout_kernel(heads, w_ref, o_ref, perm)

    return pl.pallas_call(
        kernel,
        grid=(steps,),
        in_specs=specs,
        out_specs=pl.BlockSpec((2, bk, cols), lambda i: (0, piece * steps + i, 0)),
        out_shape=jax.ShapeDtypeStruct((2, k, cols), BF),
        scratch_shapes=[pltpu.VMEM((256, 256), BF)],
        input_output_aliases=aliases,
        compiler_params=params(52),
        cost_estimate=cost(2 * k * heads * width * 256 // pieces, 4 * k * heads * width // pieces),
        name="relayout",
    )(*args)


def project_kernel(parts, old, seq_ref, which_ref, *refs):
    ins, w_ref, ext_ref = refs[:parts], refs[parts], refs[parts + 1]
    rest = refs[parts + 2 :]
    olds, rest = rest[:old], rest[old:]
    o_ref, exts, rows = rest[0], rest[1:-1], rest[-1]
    piece = ins[0].shape[0]
    blocks = parts // STREAMS
    rc = piece * STREAMS

    def put(out, new, before):
        if not old:
            out[...] = new.astype(out.dtype)
            return
        for i in range(blocks):
            at = pl.ds(pl.multiple_of(seq_ref[i] * rc, 16), rc)
            out[at, :] = before[i * rc : (i + 1) * rc, :].astype(out.dtype)
            at = pl.ds(pl.multiple_of(seq_ref[blocks + i] * rc, 16), rc)
            out[at, :] = new[i * rc : (i + 1) * rc].astype(out.dtype)

    @pl.when(pl.program_id(0) == 0)
    def _():
        for i in range(parts):
            rows[i * piece : (i + 1) * piece, :] = ins[i][...]
        if exts:
            total = jnp.dot(rows[...], ext_ref[...], preferred_element_type=F32)
            for e in exts:
                put(e, total, olds[1] if old else None)

    total = jnp.dot(rows[...], w_ref[0], preferred_element_type=F32)
    put(o_ref, total, olds[0] if old else None)


def project(seq, which, ins, w, w_ext, dtype, ext_dtypes, olds=(), bn=512, shape=pltpu.HBM):
    parts = len(ins)
    rc, k = ins[0].shape
    m = rc * parts
    out_m = 2 * m if olds else m
    cols, ext_cols = w.shape[2], w_ext.shape[1]
    bn = min(bn, cols)
    in_specs = [whole_block((rc, k)) for _ in ins] + [
        pl.BlockSpec((1, k, bn), lambda j, seq, which: (which[0], 0, j)),
        whole_block((k, ext_cols)) if ext_dtypes else pl.BlockSpec(memory_space=pl.ANY),
    ]
    if olds:
        in_specs.append(pl.BlockSpec((m, bn), lambda j, seq, which: (0, j)))
        if ext_dtypes:
            in_specs.append(whole_block((m, ext_cols)))
    return pl.pallas_call(
        functools.partial(project_kernel, parts, len(olds)),
        grid_spec=pltpu.PrefetchScalarGridSpec(
            num_scalar_prefetch=2,
            grid=(cols // bn,),
            in_specs=in_specs,
            out_specs=[pl.BlockSpec((out_m, bn), lambda j, seq, which: (0, j))]
            + [whole_block((out_m, ext_cols)) for _ in ext_dtypes],
            scratch_shapes=[pltpu.VMEM((m, k), BF)],
        ),
        out_shape=[shape((out_m, cols), dtype)]
        + [shape((out_m, ext_cols), d) for d in ext_dtypes],
        compiler_params=params(46),
        cost_estimate=cost(2 * m * k * (cols + ext_cols), 2 * k * cols + 2 * m * k),
        name="project",
    )(seq, which, *ins, w, w_ext, *olds)


def extra_kernel(parts, seq_ref, *refs):
    ins, ext_ref, old_ref, o_ref, rows = refs[:parts], *refs[parts:]
    piece = ins[0].shape[0]
    blocks = parts // STREAMS
    rc = piece * STREAMS
    for i in range(parts):
        rows[i * piece : (i + 1) * piece, :] = ins[i][...]
    total = jnp.dot(rows[...], ext_ref[...], preferred_element_type=F32)
    for i in range(blocks):
        at = pl.ds(pl.multiple_of(seq_ref[i] * rc, 16), rc)
        o_ref[at, :] = old_ref[i * rc : (i + 1) * rc, :]
        at = pl.ds(pl.multiple_of(seq_ref[blocks + i] * rc, 16), rc)
        o_ref[at, :] = total[i * rc : (i + 1) * rc]


def extra(seq, ins, w_ext, old):
    parts = len(ins)
    piece, k = ins[0].shape
    m, cols = old.shape
    args = [*ins, w_ext, old]
    return pl.pallas_call(
        functools.partial(extra_kernel, parts),
        grid_spec=pltpu.PrefetchScalarGridSpec(
            num_scalar_prefetch=1,
            grid=(1,),
            in_specs=[whole_block(a.shape) for a in args],
            out_specs=whole_block((2 * m, cols)),
            scratch_shapes=[pltpu.VMEM((m, k), BF)],
        ),
        out_shape=jax.ShapeDtypeStruct((2 * m, cols), F32),
        compiler_params=params(46),
        cost_estimate=cost(2 * m * k * cols, 2 * m * k + 2 * k * cols),
        name="extra",
    )(seq, *args)


def silu(v):
    return v / (1.0 + jnp.exp(-v))


def history_rows(state):
    state = state.astype(F32)
    empty = jnp.zeros((state.shape[1], DRAFT - KW + 1, state.shape[2]), F32)
    return jnp.concatenate([empty, *[state[j][:, None, :] for j in range(KW - 1)]], axis=1)


def ssm_kernel(
    group_ref, meta_ref, recv_ref, mine_ref, dt_ref, braw_ref, craw_ref, prevx_ref, prevb_ref, prevc_ref,
    tapx_ref, tapb_ref, tapc_ref, heads_ref, gain_ref, state_ref,
    gated_ref, ssq_ref, xw_ref, bconv_ref, sw_ref, xraw_ref,
):
    rb = recv_ref.shape[0]
    hp = gated_ref.shape[1]
    pairs = hp // LANES
    ss = meta_ref[..., 0:1].reshape(rb, 1)
    acc = meta_ref[..., 1:2].reshape(rb, 1)
    t = lax.broadcasted_iota(jnp.int32, (rb, 1), 0) & (DRAFT - 1)
    low = lax.broadcasted_iota(jnp.int32, (rb, LANES), 1) < LANES // 2
    seen = [
        jnp.where((t < ss) | (t - d >= ss), 1.0, 0.0).reshape(rb // DRAFT, DRAFT, 1) for d in range(KW)
    ]
    t3 = t.reshape(rb // DRAFT, DRAFT, 1)

    def pair(v, j):
        return jnp.concatenate([v[2 * j : 2 * j + 1, :], v[2 * j + 1 : 2 * j + 2, :]], axis=1)

    def conv(x, p3, taps):
        width = x.shape[1]
        x3 = x.reshape(rb // DRAFT, DRAFT, width)
        total = x3 * taps[KW - 1 : KW, :].reshape(1, 1, width)
        for d in range(1, KW):
            source = jnp.where(t3 >= d, pltpu.roll(x3, d, 1), pltpu.roll(p3, d, 1))
            total = total + (source * seen[d]) * taps[KW - 1 - d : KW - d, :].reshape(1, 1, width)
        return silu(total).reshape(rb, width)

    zx = (mine_ref[...].astype(F32) + recv_ref[...].astype(F32)).astype(BF).astype(F32)
    gates, xs = [], []
    for j in range(pairs):
        a = zx[:, 2 * j * LANES : (2 * j + 1) * LANES]
        b = zx[:, (2 * j + 1) * LANES : (2 * j + 2) * LANES]
        gates.append(jnp.where(low, a, pltpu.roll(b, LANES // 2, 1)))
        xs.append(jnp.where(low, pltpu.roll(a, LANES // 2, 1), b))
    prev_x = history_rows(prevx_ref[...])
    convs = []
    for j in range(pairs):
        cut = slice(j * LANES, (j + 1) * LANES)
        xraw_ref[:, cut] = xs[j].astype(BF)
        taps = jnp.concatenate([pair(tapx_ref[k], j) for k in range(KW)], axis=0)
        convs.append(conv(xs[j], prev_x[:, :, cut], taps))
    b_conv = conv(braw_ref[...].astype(F32), history_rows(prevb_ref[...]), tapb_ref[...])
    c_conv = conv(craw_ref[...].astype(F32), history_rows(prevc_ref[...]), tapc_ref[...])
    bconv_ref[...] = b_conv.astype(BF)

    raw = dt_ref[...].astype(F32) + heads_ref[0:1, :]
    step = jnp.maximum(raw, 0.0) + jnp.log1p(jnp.exp(-jnp.abs(raw)))
    log_a = -step * heads_ref[1:2, :]
    ri = lax.broadcasted_iota(jnp.int32, (rb, rb), 0)
    ci = lax.broadcasted_iota(jnp.int32, (rb, rb), 1)
    same = (ri // DRAFT) == (ci // DRAFT)
    tt, tq = ri & (DRAFT - 1), ci & (DRAFT - 1)
    lower = same & (tq <= tt)
    linked = lower & jnp.logical_not((tq < ss) & (ss <= tt))
    cum = jnp.dot(jnp.where(lower, 1.0, 0.0), log_a, precision=HIGH, preferred_element_type=F32)
    cum_acc = jnp.dot(
        jnp.where(same & (tq < acc), 1.0, 0.0), log_a, precision=HIGH, preferred_element_type=F32
    )
    cum_t = cum.T
    step_t = step.T
    scores = lax.dot_general(c_conv, b_conv, NT, precision=HIGH, preferred_element_type=F32)

    def spread(v, j):
        return jnp.where(low[: v.shape[0]], v[:, 2 * j : 2 * j + 1], v[:, 2 * j + 1 : 2 * j + 2])

    odd = (lax.broadcasted_iota(jnp.int32, (rb, 1), 0) & DRAFT) != 0
    c_pair = jnp.concatenate(
        [jnp.where(odd, 0.0, c_conv).astype(BF), jnp.where(odd, c_conv, 0.0).astype(BF)], axis=1
    )
    state = state_ref[...].reshape(rb // DRAFT, hp, LANES)
    carried = []
    for i in range(rb // (2 * DRAFT)):
        both = jnp.concatenate([state[2 * i], state[2 * i + 1]], axis=1)
        carried.append(
            lax.dot_general(
                c_pair[2 * DRAFT * i : 2 * DRAFT * (i + 1)], both, NT, preferred_element_type=F32
            )
        )
    carried = jnp.concatenate(carried, axis=0)

    kept = jnp.where(t < ss, jnp.exp(cum), 0.0)
    counted = (t < acc) & jnp.logical_not((t < ss) & (ss < acc))
    weight = jnp.where(counted, jnp.exp(jnp.where(counted, cum_acc - cum, 0.0)), 0.0) * step
    sw_ref[...] = jnp.where(ss < acc, 0.0, jnp.exp(cum_acc))
    skip = heads_ref[2:3, :]
    squares = jnp.zeros((rb, LANES), F32)
    for j in range(pairs):
        cut = slice(j * LANES, (j + 1) * LANES)
        mixes = []
        for h in (2 * j, 2 * j + 1):
            gap = cum[:, h : h + 1] - cum_t[h : h + 1, :]
            mixes.append((jnp.exp(jnp.where(linked, gap, -1e30)) * (scores * step_t[h : h + 1, :])).astype(BF))
        x_conv = convs[j]
        x_pair = jnp.concatenate(
            [jnp.where(low, x_conv, 0.0).astype(BF), jnp.where(low, 0.0, x_conv).astype(BF)], axis=0
        )
        intra = jnp.dot(jnp.concatenate(mixes, axis=1), x_pair, preferred_element_type=F32)
        mixed = spread(kept, j) * carried[:, cut] + intra + spread(skip, j) * x_conv
        gated = mixed * silu(gates[j])
        squares = squares + gated * gated
        gated_ref[:, cut] = (gated * pair(gain_ref, j)).astype(BF)
        xw_ref[:, cut] = (spread(weight, j) * x_conv).astype(BF)
    row_sum = jnp.broadcast_to(jnp.sum(squares, axis=1, keepdims=True), (rb, LANES))
    ssq_ref[...] = row_sum.T[:8]


def pick_tail(ss, acc, raw, prev):
    rb = raw.shape[0]
    ri = lax.broadcasted_iota(jnp.int32, (rb, rb), 0)
    ci = lax.broadcasted_iota(jnp.int32, (rb, rb), 1)
    same = (ri // DRAFT) == (ci // DRAFT)
    j, q = ri & (DRAFT - 1), ci & (DRAFT - 1)
    source = acc + j - (KW - 1)
    live = same & (j < KW - 1) & jnp.logical_not((source < ss) & (ss < acc))
    new = jnp.where(live & (q == source), 1.0, 0.0).astype(BF)
    old = jnp.where(live & (q == source + DRAFT), 1.0, 0.0).astype(BF)
    return jnp.dot(new, raw.astype(BF), preferred_element_type=F32) + jnp.dot(
        old, prev.astype(BF), preferred_element_type=F32
    )


def ssm(group, rb, meta, recv, mine, dt, b_raw, c_raw, x_state, bc_state, conv_x, conv_bc, heads, gain, state):
    rows = recv.shape[0]
    _, _, rq, hp, width_n = state.shape
    ob = rb // (rq * DRAFT)
    reqs = rb // DRAFT

    def flat(w):
        return pl.BlockSpec((rb, w), lambda i, group: (i, 0))

    def columns(shape, which):
        lead = (0,) * (len(shape) - 1)
        if len(shape) == 3:
            return pl.BlockSpec(shape, lambda i, group: (0, i, which * G + group[0]))
        return pl.BlockSpec(shape, lambda i, group: (*lead, which * G + group[0]))

    return pl.pallas_call(
        ssm_kernel,
        grid_spec=pltpu.PrefetchScalarGridSpec(
            num_scalar_prefetch=1,
            grid=(rows // rb,),
            in_specs=[
                flat(2),
                flat(recv.shape[1]),
                flat(mine.shape[1]),
                flat(LANES),
                flat(LANES),
                flat(LANES),
                pl.BlockSpec((KW - 1, reqs, hp), lambda i, group: (0, i, 0)),
                columns((KW - 1, reqs, LANES), 0),
                columns((KW - 1, reqs, LANES), 1),
                whole_block(conv_x.shape),
                columns((KW, LANES), 0),
                columns((KW, LANES), 1),
                whole_block(heads.shape),
                whole_block(gain.shape),
                pl.BlockSpec((ob, 1, rq, hp, width_n), lambda i, group: (i, 0, 0, 0, 0)),
            ],
            out_specs=[
                flat(hp),
                pl.BlockSpec((8, rb), lambda i, group: (0, i)),
                flat(hp),
                flat(LANES),
                flat(LANES),
                flat(hp),
            ],
        ),
        out_shape=[
            jax.ShapeDtypeStruct((rows, hp), BF),
            jax.ShapeDtypeStruct((8, rows), F32),
            pltpu.HBM((rows, hp), BF),
            pltpu.HBM((rows, LANES), BF),
            pltpu.HBM((rows, LANES), F32),
            pltpu.HBM((rows, hp), BF),
        ],
        compiler_params=params(46),
        cost_estimate=cost(2 * rows * hp * 4096, 6 * rows * hp * 16),
        name="ssm",
    )(group, meta, recv, mine, dt, b_raw, c_raw, x_state, bc_state, bc_state, conv_x, conv_bc, conv_bc, heads, gain, state)


def state_kernel(meta_ref, xw_ref, bconv_ref, sw_ref, xraw_ref, prevx_ref, state_ref, o_ref, tail_ref):
    rb, hp = xw_ref.shape
    width_p = LANES // 2
    ss = meta_ref[..., 0:1].reshape(rb, 1)
    acc = meta_ref[..., 1:2].reshape(rb, 1)
    tail_ref[...] = pick_tail(ss, acc, xraw_ref[...], history_rows(prevx_ref[...]).reshape(rb, hp)).astype(BF)
    request = lax.broadcasted_iota(jnp.int32, (rb, 1), 0) // DRAFT
    b_conv = bconv_ref[...].astype(F32)
    xw_t = xw_ref[...].astype(F32).T.astype(BF)
    rq = state_ref.shape[2]
    sw = sw_ref[...]
    for i in range(0, rb // DRAFT, 2):
        both = jnp.concatenate(
            [jnp.where(request == i + u, b_conv, 0.0).astype(BF) for u in range(2)], axis=1
        )
        added = jnp.dot(xw_t, both, preferred_element_type=F32)
        for u in range(2):
            r = i + u
            for h in range(hp // width_p):
                cut = slice(h * width_p, (h + 1) * width_p)
                old = state_ref[r // rq, 0, r % rq, cut, :].astype(F32)
                new = sw[r * DRAFT : r * DRAFT + 1, h : h + 1] * old + added[cut, u * LANES : (u + 1) * LANES]
                o_ref[r // rq, 0, r % rq, cut, :] = new.astype(BF)


def tail_kernel(meta_ref, raw_ref, prev_ref, o_ref):
    rb = raw_ref.shape[0]
    ss = meta_ref[..., 0:1].reshape(rb, 1)
    acc = meta_ref[..., 1:2].reshape(rb, 1)
    o_ref[...] = pick_tail(ss, acc, raw_ref[...], history_rows(prev_ref[...]).reshape(raw_ref.shape)).astype(BF)


def new_history(rb, meta, raw, prev):
    rows, cols = raw.shape

    def flat(w):
        return pl.BlockSpec((rb, w), lambda i: (i, 0))

    return pl.pallas_call(
        tail_kernel,
        grid=(rows // rb,),
        in_specs=[flat(2), flat(cols), pl.BlockSpec((KW - 1, rb // DRAFT, cols), lambda i: (0, i, 0))],
        out_specs=flat(cols),
        out_shape=jax.ShapeDtypeStruct((rows, cols), BF),
        compiler_params=params(24),
        cost_estimate=cost(4 * rows * rb * cols, 6 * rows * cols),
        name="new_history",
    )(meta, raw, prev)


def new_state(piece, pieces, rb, meta, xw, bconv, sw, xraw, prev_x, state, into):
    rows, hp = xw.shape
    n, _, rq, _, width_n = state.shape
    ob = rb // (rq * DRAFT)
    steps = rows // rb // pieces
    first = piece * steps

    def flat(w):
        return pl.BlockSpec((rb, w), lambda i: (first + i, 0))

    states = pl.BlockSpec((ob, 1, rq, hp, width_n), lambda i: (first + i, 0, 0, 0, 0))
    args = [meta, xw, bconv, sw, xraw, prev_x, state]
    specs = [
        flat(2),
        flat(hp),
        flat(LANES),
        flat(LANES),
        flat(hp),
        pl.BlockSpec((KW - 1, rb // DRAFT, hp), lambda i: (0, first + i, 0)),
        states,
    ]
    kernel, aliases = state_kernel, {}
    if into is not None:
        args.append(into)
        specs.append(pl.BlockSpec(memory_space=pl.ANY))
        aliases = {7: 0}

        def kernel(*refs):
            return state_kernel(*refs[:7], *refs[8:])

    return pl.pallas_call(
        kernel,
        grid=(steps,),
        in_specs=specs,
        out_specs=[states, pl.BlockSpec((rb, hp), lambda i: (i, 0))],
        out_shape=[jax.ShapeDtypeStruct(state.shape, BF), jax.ShapeDtypeStruct((rows // pieces, hp), BF)],
        input_output_aliases=aliases,
        compiler_params=params(40),
        cost_estimate=cost(2 * rows * hp * 4096 // pieces, 8 * rows * hp * 16 // pieces),
        name="new_state",
    )(*args)


def out_kernel(scale_by, inc_ref, mine_ref, theirs_ref, w_mine_ref, w_theirs_ref, ssq_ref, o_ref):
    product = jnp.dot(mine_ref[...], w_mine_ref[...], preferred_element_type=F32) + jnp.dot(
        theirs_ref[...], w_theirs_ref[...], preferred_element_type=F32
    )
    scale = lax.rsqrt(ssq_ref[...] * scale_by + 1e-05)
    rows = scale.shape[1]
    column = jnp.broadcast_to(scale[0:1], (LANES, rows)).T[:, 0:1]
    o_ref[...] = (product * column).astype(o_ref.dtype)


def out_project(inc, mine, theirs, w_out, ssq, scale_by, part, parts, bn=512):
    rows, hp = mine.shape
    cols = w_out.shape[1] // parts
    first = part * (cols // bn)
    return pl.pallas_call(
        functools.partial(out_kernel, scale_by),
        grid_spec=pltpu.PrefetchScalarGridSpec(
            num_scalar_prefetch=1,
            grid=(cols // bn,),
            in_specs=[
                pl.BlockSpec((rows, hp), lambda j, inc: (0, 0)),
                pl.BlockSpec((rows, hp), lambda j, inc: (0, 0)),
                pl.BlockSpec((hp, bn), lambda j, inc: (inc[0], first + j)),
                pl.BlockSpec((hp, bn), lambda j, inc: (1 - inc[0], first + j)),
                pl.BlockSpec((8, rows), lambda j, inc: (0, 0)),
            ],
            out_specs=pl.BlockSpec((rows, bn), lambda j, inc: (0, j)),
        ),
        out_shape=jax.ShapeDtypeStruct((rows, cols), BF),
        compiler_params=params(40),
        cost_estimate=cost(4 * rows * hp * cols, 4 * hp * cols + 4 * rows * cols),
        name="out_project",
    )(inc, mine, theirs, w_out, w_out, ssq)


def shards(n, chunks, tokens, w_zx, w_dt, w_bc, conv_x, conv_bc, dt_bias, decay_rate, skip_gain, norm_gain,
           w_out, conv_x_state, conv_bc_state, ssm_state, span_start, accepted):
    req, hd, width_p, width_n = ssm_state.shape
    hp = hd * width_p
    block_rows, half_d = tokens.shape
    cw = w_bc.shape[1]
    rc = block_rows // chunks
    rq = rc // DRAFT
    rows = n * rc
    rb = min(128, rows)
    order = list(range(0, n, 2)) + list(range(n - 1, 0, -2))
    ring = [(2 * order[i], 2 * order[(i + 1) % n]) for i in range(n)]
    ring += [(2 * order[(i + 1) % n] + 1, 2 * order[i] + 1) for i in range(n)]
    swap = [(0, 1), (1, 0)]
    me = lax.axis_index("outc")
    inc = lax.axis_index("inc")
    pos = jnp.where(me % 2 == 0, me // 2, n - 1 - me // 2)

    def owner(step):
        i = (pos + (2 * inc - 1) * step + n) % n
        return jnp.where(i < n // 2, 2 * i, 2 * n - 1 - 2 * i)

    seq = owner(jnp.arange(n, dtype=jnp.int32))
    inc1 = inc.astype(jnp.int32).reshape(1)

    def onward(a):
        return lax.ppermute(a, ("outc", "inc"), ring)

    def other(a):
        return lax.ppermute(a, "inc", swap)

    member = n // G
    group = me // member
    seat = me % member
    w_ext = jnp.concatenate([w_bc, w_dt, jnp.zeros((half_d, LANES - w_dt.shape[1]), BF)], axis=1)
    if w_ext.shape[1] % LANES:
        w_ext = jnp.pad(w_ext, ((0, 0), (0, LANES - w_ext.shape[1] % LANES)))

    def columns(a, start, size):
        return lax.dynamic_slice_in_dim(a, start, size, a.ndim - 1)

    x_state = jnp.swapaxes(conv_x_state.reshape(req, KW - 1, hp), 0, 1)
    bc_state = jnp.swapaxes(conv_bc_state, 0, 1)
    own_state = columns(bc_state, me * cw, cw)
    meta = jnp.stack([span_start, accepted], axis=-1).astype(jnp.int32)
    meta = jnp.broadcast_to(meta[:, None, :], (req, DRAFT, 2)).reshape(rows, 2)
    heads = jnp.pad(jnp.stack([dt_bias, decay_rate, skip_gain]), ((0, 5), (0, LANES - hd)))
    group1 = group.astype(jnp.int32).reshape(1)
    state = ssm_state.reshape(n, chunks, rq, hp, width_n)
    scale_by = 1.0 / (HEADS // G * width_p)

    pieces = 4
    w = None
    piece_rows = rc // STREAMS
    heads_of = [tokens[i * piece_rows : (i + 1) * piece_rows] for i in range(STREAMS)]
    blocks = list(heads_of)
    first = n // 2
    split = first * STREAMS
    for s in range(n - 1):
        heads_of = [onward(a) for a in heads_of]
        lead = heads_of[0]
        if s < pieces:
            w = relayout(s, pieces, w_zx, w)
            lead, w = lax.optimization_barrier((lead, w))
        elif s == max(pieces, first):
            theirs_1, ext_1 = project(seq, 1 - inc1, blocks[:split], w, w_ext, BF, [F32])
            lead, theirs_1, ext_1 = lax.optimization_barrier((lead, theirs_1, ext_1))
        elif s == max(pieces, first) + 1:
            (mine_1,) = project(seq, inc1, blocks[:split], w, w_ext, F32, [])
            lead, mine_1 = lax.optimization_barrier((lead, mine_1))
        heads_of[0] = lead
        blocks += heads_of

    prepared = [meta, x_state, own_state, heads, w_ext]
    blocks[-1], prepared = lax.optimization_barrier((blocks[-1], prepared))
    meta, x_state, own_state, heads, w_ext = prepared

    ext = extra(seq, blocks[split:], w_ext, ext_1)
    ext_other = other(ext)
    (theirs,) = project(seq, 1 - inc1, blocks[split:], w, w_ext, BF, [], (theirs_1,))
    theirs, ext, ext_other = lax.optimization_barrier((theirs, ext, ext_other))
    ext = (ext + ext_other).astype(BF)
    bc_own = ext[:, :cw]
    dt = columns(ext[:, cw : cw + 2 * hd], inc * hd, hd)
    dt = jnp.pad(dt, ((0, 0), (0, LANES - hd)))
    got = []
    for k in range(member):
        pairs = []
        for g in range(G):
            width = member // 2
            sources = [g * width + i for i in range(width)] + [n // 2 + g * width + i for i in range(width)]
            for i in range(member):
                pairs.append((sources[(i + k) % member], g * member + i))
        got.append(lax.ppermute(bc_own, "outc", pairs))
    picked = []
    for i in range(member):
        piece = got[0]
        for k in range(1, member):
            piece = jnp.where((i - seat) % member == k, got[k], piece)
        picked.append(piece)
    b_raw = jnp.concatenate(picked[: member // 2], axis=1)
    c_raw = jnp.concatenate(picked[member // 2 :], axis=1)
    theirs = other(theirs)
    late, bc_own, dt = lax.optimization_barrier((blocks[-1], bc_own, dt))
    blocks[-1] = late
    (mine,) = project(seq, inc1, blocks[split:], w, w_ext, F32, [], (mine_1,), shape=jax.ShapeDtypeStruct)
    gated, ssq, xw, bconv, sw, xraw = ssm(
        group1, rb, meta, theirs, mine, dt, b_raw, c_raw, x_state, bc_state, conv_x, conv_bc, heads, norm_gain, state
    )

    def tails(a):
        return a.reshape(req, DRAFT, a.shape[-1])[:, : KW - 1]

    gated_theirs = other(gated)
    ssq = ssq + other(ssq)
    bc_own, gated, ssq = lax.optimization_barrier((bc_own, gated, ssq))
    d = 1
    while d < member:
        ssq = ssq + lax.ppermute(ssq, "outc", [(i, i ^ d) for i in range(n)])
        d *= 2
    history_bc = new_history(rb, meta, bc_own, own_state)
    history_bc = history_bc.reshape(req, DRAFT, cw)[:, : KW - 1].reshape(req * (KW - 1), cw)
    half_rows = req * (KW - 1) // 2
    history_bc = lax.dynamic_slice_in_dim(history_bc, inc * half_rows, half_rows, 0)
    widths = [n >> (i + 1) for i in range(n.bit_length() - 1)]

    def double(a, i):
        got = lax.ppermute(a, "outc", [(k, k ^ widths[i]) for k in range(n)])
        return jnp.where((me & widths[i]) != 0, jnp.stack([got, a], i), jnp.stack([a, got], i))

    history_bc = double(history_bc, 0)
    gated_theirs, ssq, history_bc = lax.optimization_barrier((gated_theirs, ssq, history_bc))
    history_bc = double(history_bc, 1)

    sums, partials = [], []

    def part(i, s):
        return lax.dynamic_slice_in_dim(partials[i], owner((s + 1) % n) * rc, rc, 0)

    for i in range(STREAMS):
        partials.append(out_project(inc1, gated, gated_theirs, w_out, ssq, scale_by, i, STREAMS))
        if i == 0:
            partials[0], history_bc = lax.optimization_barrier((partials[0], history_bc))
            for k in range(2, len(widths)):
                history_bc = double(history_bc, k)
        sums.append(part(i, 0))
    tails_x = []
    after = None
    for s in range(n - 1):
        if s in (0, 2):
            xw, sums[0] = lax.optimization_barrier((xw, sums[0]))
            piece = len(tails_x)
            after, tail = new_state(piece, 2, rb, meta, xw, bconv, sw, xraw, x_state, state, after)
            tails_x.append(tail)
            after, sums[0] = lax.optimization_barrier((after, sums[0]))
        if s == 3:
            history_bc, sums[0] = lax.optimization_barrier((history_bc, sums[0]))
            history_bc = history_bc.reshape(n, half_rows, cw)
            history_other = other(history_bc)
        if s == 4:
            history_other, sums[0] = lax.optimization_barrier((history_other, sums[0]))
            history_bc = jnp.where(
                inc != 0,
                jnp.concatenate([history_other, history_bc], axis=1),
                jnp.concatenate([history_bc, history_other], axis=1),
            )
        if s == 5:
            history_bc, tails_x, sums[1] = lax.optimization_barrier((history_bc, tails_x, sums[1]))
        for i in range(STREAMS):
            sums[i] = (onward(sums[i]).astype(F32) + part(i, s + 1).astype(F32)).astype(BF)
    new_bc = jnp.swapaxes(history_bc, 0, 1).reshape(req, KW - 1, n * cw)
    new_x = tails(jnp.concatenate(tails_x, axis=0)).reshape(req, KW - 1, hd, width_p)
    return jnp.concatenate(sums, axis=1), after.reshape(ssm_state.shape), new_x, new_bc


def solution(mesh):
    n = mesh.shape["outc"]
    placed = (
        P(("groups", "outc"), "inc"),
        P("inc", "outc", None),
        P("inc", "outc"),
        P("inc", "outc"),
        P(None, ("outc", "inc"), None),
        P(),
        P(("outc", "inc")),
        P(("outc", "inc")),
        P(("outc", "inc")),
        P(("outc", "inc"), None),
        P("outc", "inc"),
        P("groups", None, ("outc", "inc"), None),
        P("groups", None, None),
        P("groups", ("outc", "inc"), None, None),
        P("groups"),
        P("groups"),
    )
    return jax.shard_map(
        functools.partial(shards, n, 1),
        mesh=mesh,
        in_specs=placed,
        out_specs=(
            P(("groups", "outc"), "inc"),
            P("groups", ("outc", "inc"), None, None),
            P("groups", None, ("outc", "inc"), None),
            P("groups", None, None),
        ),
        check_vma=False,
    )
```

```python
import functools

import jax
import jax.numpy as jnp
from jax import lax
from jax.experimental import pallas as pl
from jax.experimental.pallas import tpu as pltpu
from jax.sharding import PartitionSpec as P

HEADS = 128
G = 4
KW = 4
DRAFT = 8
LANES = 128
STREAMS = 2
BF = jnp.bfloat16
F32 = jnp.float32
HIGH = lax.Precision.HIGHEST
NT = (((1,), (1,)), ((), ()))
TN = (((0,), (0,)), ((), ()))
MIB = 1 << 20


def params(mib):
    return pltpu.CompilerParams(vmem_limit_bytes=mib * MIB)


def cost(flops, nbytes):
    return pl.CostEstimate(flops=int(flops), bytes_accessed=int(nbytes), transcendentals=0)


def whole_block(shape):
    return pl.BlockSpec(shape, lambda *_: (0,) * len(shape))


def relayout_kernel(heads, w_ref, o_ref, perm):
    kb = 256 // heads

    @pl.when(pl.program_id(0) == 0)
    def _():
        r = lax.broadcasted_iota(jnp.int32, (256, 256), 0)
        c = lax.broadcasted_iota(jnp.int32, (256, 256), 1)
        hit = (r // kb == lax.rem(c, heads)) & (lax.rem(r, kb) == c // heads)
        perm[...] = jnp.where(hit, 1.0, 0.0).astype(BF)

    bk = w_ref.shape[0]
    half = heads // 2
    for i in range(0, bk // kb, 2):
        first = w_ref[i * kb : (i + 1) * kb].reshape(256, LANES)
        second = w_ref[(i + 1) * kb : (i + 2) * kb].reshape(256, LANES)
        both = jnp.concatenate([first, second], axis=1)
        out = jnp.dot(perm[...], both, preferred_element_type=F32).astype(BF)
        for u in range(2):
            for h in range(heads):
                at = (h % half) * LANES
                o_ref[h // half, (i + u) * kb : (i + u + 1) * kb, at : at + LANES] = out[
                    h * kb : (h + 1) * kb, u * LANES : (u + 1) * LANES
                ]


def relayout(piece, pieces, w_zx, into, bk=512):
    k, heads, width = w_zx.shape
    cols = heads // 2 * width
    bk = min(bk, k // pieces)
    steps = k // bk // pieces
    kernel = functools.partial(relayout_kernel, heads)
    specs = [pl.BlockSpec((bk, heads, width), lambda i: (piece * steps + i, 0, 0))]
    args, aliases = [w_zx], {}
    if into is not None:
        args.append(into)
        specs.append(pl.BlockSpec(memory_space=pl.ANY))
        aliases = {1: 0}

        def kernel(w_ref, _, o_ref, perm):
            relayout_kernel(heads, w_ref, o_ref, perm)

    return pl.pallas_call(
        kernel,
        grid=(steps,),
        in_specs=specs,
        out_specs=pl.BlockSpec((2, bk, cols), lambda i: (0, piece * steps + i, 0)),
        out_shape=jax.ShapeDtypeStruct((2, k, cols), BF),
        scratch_shapes=[pltpu.VMEM((256, 256), BF)],
        input_output_aliases=aliases,
        compiler_params=params(52),
        cost_estimate=cost(2 * k * heads * width * 256 // pieces, 4 * k * heads * width // pieces),
        name="relayout",
    )(*args)


def project_kernel(parts, old, seq_ref, which_ref, *refs):
    ins, w_ref, ext_ref = refs[:parts], refs[parts], refs[parts + 1]
    rest = refs[parts + 2 :]
    olds, rest = rest[:old], rest[old:]
    o_ref, exts, rows = rest[0], rest[1:-1], rest[-1]
    piece = ins[0].shape[0]
    blocks = parts // STREAMS
    rc = piece * STREAMS

    def put(out, new, before):
        if not old:
            out[...] = new.astype(out.dtype)
            return
        for i in range(blocks):
            at = pl.ds(pl.multiple_of(seq_ref[i] * rc, 16), rc)
            out[at, :] = before[i * rc : (i + 1) * rc, :].astype(out.dtype)
            at = pl.ds(pl.multiple_of(seq_ref[blocks + i] * rc, 16), rc)
            out[at, :] = new[i * rc : (i + 1) * rc].astype(out.dtype)

    @pl.when(pl.program_id(0) == 0)
    def _():
        for i in range(parts):
            rows[i * piece : (i + 1) * piece, :] = ins[i][...]
        if exts:
            total = jnp.dot(rows[...], ext_ref[...], preferred_element_type=F32)
            for e in exts:
                put(e, total, olds[1] if old else None)

    total = jnp.dot(rows[...], w_ref[0], preferred_element_type=F32)
    put(o_ref, total, olds[0] if old else None)


def project(seq, which, ins, w, w_ext, dtype, ext_dtypes, olds=(), bn=512, shape=pltpu.HBM):
    parts = len(ins)
    rc, k = ins[0].shape
    m = rc * parts
    out_m = 2 * m if olds else m
    cols, ext_cols = w.shape[2], w_ext.shape[1]
    bn = min(bn, cols)
    in_specs = [whole_block((rc, k)) for _ in ins] + [
        pl.BlockSpec((1, k, bn), lambda j, seq, which: (which[0], 0, j)),
        whole_block((k, ext_cols)) if ext_dtypes else pl.BlockSpec(memory_space=pl.ANY),
    ]
    if olds:
        in_specs.append(pl.BlockSpec((m, bn), lambda j, seq, which: (0, j)))
        if ext_dtypes:
            in_specs.append(whole_block((m, ext_cols)))
    return pl.pallas_call(
        functools.partial(project_kernel, parts, len(olds)),
        grid_spec=pltpu.PrefetchScalarGridSpec(
            num_scalar_prefetch=2,
            grid=(cols // bn,),
            in_specs=in_specs,
            out_specs=[pl.BlockSpec((out_m, bn), lambda j, seq, which: (0, j))]
            + [whole_block((out_m, ext_cols)) for _ in ext_dtypes],
            scratch_shapes=[pltpu.VMEM((m, k), BF)],
        ),
        out_shape=[shape((out_m, cols), dtype)]
        + [shape((out_m, ext_cols), d) for d in ext_dtypes],
        compiler_params=params(46),
        cost_estimate=cost(2 * m * k * (cols + ext_cols), 2 * k * cols + 2 * m * k),
        name="project",
    )(seq, which, *ins, w, w_ext, *olds)


def extra_kernel(parts, seq_ref, *refs):
    ins, ext_ref, old_ref, o_ref, rows = refs[:parts], *refs[parts:]
    piece = ins[0].shape[0]
    blocks = parts // STREAMS
    rc = piece * STREAMS
    for i in range(parts):
        rows[i * piece : (i + 1) * piece, :] = ins[i][...]
    total = jnp.dot(rows[...], ext_ref[...], preferred_element_type=F32)
    for i in range(blocks):
        at = pl.ds(pl.multiple_of(seq_ref[i] * rc, 16), rc)
        o_ref[at, :] = old_ref[i * rc : (i + 1) * rc, :]
        at = pl.ds(pl.multiple_of(seq_ref[blocks + i] * rc, 16), rc)
        o_ref[at, :] = total[i * rc : (i + 1) * rc]


def extra(seq, ins, w_ext, old):
    parts = len(ins)
    piece, k = ins[0].shape
    m, cols = old.shape
    args = [*ins, w_ext, old]
    return pl.pallas_call(
        functools.partial(extra_kernel, parts),
        grid_spec=pltpu.PrefetchScalarGridSpec(
            num_scalar_prefetch=1,
            grid=(1,),
            in_specs=[whole_block(a.shape) for a in args],
            out_specs=whole_block((2 * m, cols)),
            scratch_shapes=[pltpu.VMEM((m, k), BF)],
        ),
        out_shape=jax.ShapeDtypeStruct((2 * m, cols), F32),
        compiler_params=params(46),
        cost_estimate=cost(2 * m * k * cols, 2 * m * k + 2 * k * cols),
        name="extra",
    )(seq, *args)


def silu(v):
    return v / (1.0 + jnp.exp(-v))


def history_rows(state):
    state = state.astype(F32)
    empty = jnp.zeros((state.shape[1], DRAFT - KW + 1, state.shape[2]), F32)
    return jnp.concatenate([empty, *[state[j][:, None, :] for j in range(KW - 1)]], axis=1)


def ssm_kernel(
    group_ref, meta_ref, recv_ref, mine_ref, dt_ref, braw_ref, craw_ref, prevx_ref, prevb_ref, prevc_ref,
    tapx_ref, tapb_ref, tapc_ref, heads_ref, gain_ref, state_ref,
    gated_ref, ssq_ref, xw_ref, bconv_ref, sw_ref, xraw_ref,
):
    rb = recv_ref.shape[0]
    hp = gated_ref.shape[1]
    pairs = hp // LANES
    ss = meta_ref[..., 0:1].reshape(rb, 1)
    acc = meta_ref[..., 1:2].reshape(rb, 1)
    t = lax.broadcasted_iota(jnp.int32, (rb, 1), 0) & (DRAFT - 1)
    low = lax.broadcasted_iota(jnp.int32, (rb, LANES), 1) < LANES // 2
    seen = [
        jnp.where((t < ss) | (t - d >= ss), 1.0, 0.0).reshape(rb // DRAFT, DRAFT, 1) for d in range(KW)
    ]
    t3 = t.reshape(rb // DRAFT, DRAFT, 1)

    def pair(v, j):
        return jnp.concatenate([v[2 * j : 2 * j + 1, :], v[2 * j + 1 : 2 * j + 2, :]], axis=1)

    def conv(x, p3, taps):
        width = x.shape[1]
        x3 = x.reshape(rb // DRAFT, DRAFT, width)
        total = x3 * taps[KW - 1 : KW, :].reshape(1, 1, width)
        for d in range(1, KW):
            source = jnp.where(t3 >= d, pltpu.roll(x3, d, 1), pltpu.roll(p3, d, 1))
            total = total + (source * seen[d]) * taps[KW - 1 - d : KW - d, :].reshape(1, 1, width)
        return silu(total).reshape(rb, width)

    zx = (mine_ref[...].astype(F32) + recv_ref[...].astype(F32)).astype(BF).astype(F32)
    gates, xs = [], []
    for j in range(pairs):
        a = zx[:, 2 * j * LANES : (2 * j + 1) * LANES]
        b = zx[:, (2 * j + 1) * LANES : (2 * j + 2) * LANES]
        gates.append(jnp.where(low, a, pltpu.roll(b, LANES // 2, 1)))
        xs.append(jnp.where(low, pltpu.roll(a, LANES // 2, 1), b))
    prev_x = history_rows(prevx_ref[...])
    convs = []
    for j in range(pairs):
        cut = slice(j * LANES, (j + 1) * LANES)
        xraw_ref[:, cut] = xs[j].astype(BF)
        taps = jnp.concatenate([pair(tapx_ref[k], j) for k in range(KW)], axis=0)
        convs.append(conv(xs[j], prev_x[:, :, cut], taps))
    b_conv = conv(braw_ref[...].astype(F32), history_rows(prevb_ref[...]), tapb_ref[...])
    c_conv = conv(craw_ref[...].astype(F32), history_rows(prevc_ref[...]), tapc_ref[...])
    bconv_ref[...] = b_conv.astype(BF)

    raw = dt_ref[...].astype(F32) + heads_ref[0:1, :]
    step = jnp.maximum(raw, 0.0) + jnp.log1p(jnp.exp(-jnp.abs(raw)))
    log_a = -step * heads_ref[1:2, :]
    ri = lax.broadcasted_iota(jnp.int32, (rb, rb), 0)
    ci = lax.broadcasted_iota(jnp.int32, (rb, rb), 1)
    same = (ri // DRAFT) == (ci // DRAFT)
    tt, tq = ri & (DRAFT - 1), ci & (DRAFT - 1)
    lower = same & (tq <= tt)
    linked = lower & jnp.logical_not((tq < ss) & (ss <= tt))
    cum = jnp.dot(jnp.where(lower, 1.0, 0.0), log_a, precision=HIGH, preferred_element_type=F32)
    cum_acc = jnp.dot(
        jnp.where(same & (tq < acc), 1.0, 0.0), log_a, precision=HIGH, preferred_element_type=F32
    )
    cum_t = cum.T
    step_t = step.T
    scores = lax.dot_general(c_conv, b_conv, NT, precision=HIGH, preferred_element_type=F32)

    def spread(v, j):
        return jnp.where(low[: v.shape[0]], v[:, 2 * j : 2 * j + 1], v[:, 2 * j + 1 : 2 * j + 2])

    odd = (lax.broadcasted_iota(jnp.int32, (rb, 1), 0) & DRAFT) != 0
    c_pair = jnp.concatenate(
        [jnp.where(odd, 0.0, c_conv).astype(BF), jnp.where(odd, c_conv, 0.0).astype(BF)], axis=1
    )
    state = state_ref[...].reshape(rb // DRAFT, hp, LANES)
    carried = []
    for i in range(rb // (2 * DRAFT)):
        both = jnp.concatenate([state[2 * i], state[2 * i + 1]], axis=1)
        carried.append(
            lax.dot_general(
                c_pair[2 * DRAFT * i : 2 * DRAFT * (i + 1)], both, NT, preferred_element_type=F32
            )
        )
    carried = jnp.concatenate(carried, axis=0)

    kept = jnp.where(t < ss, jnp.exp(cum), 0.0)
    counted = (t < acc) & jnp.logical_not((t < ss) & (ss < acc))
    weight = jnp.where(counted, jnp.exp(jnp.where(counted, cum_acc - cum, 0.0)), 0.0) * step
    sw_ref[...] = jnp.where(ss < acc, 0.0, jnp.exp(cum_acc))
    skip = heads_ref[2:3, :]
    squares = jnp.zeros((rb, LANES), F32)
    for j in range(pairs):
        cut = slice(j * LANES, (j + 1) * LANES)
        mixes = []
        for h in (2 * j, 2 * j + 1):
            gap = cum[:, h : h + 1] - cum_t[h : h + 1, :]
            mixes.append((jnp.exp(jnp.where(linked, gap, -1e30)) * (scores * step_t[h : h + 1, :])).astype(BF))
        x_conv = convs[j]
        x_pair = jnp.concatenate(
            [jnp.where(low, x_conv, 0.0).astype(BF), jnp.where(low, 0.0, x_conv).astype(BF)], axis=0
        )
        intra = jnp.dot(jnp.concatenate(mixes, axis=1), x_pair, preferred_element_type=F32)
        mixed = spread(kept, j) * carried[:, cut] + intra + spread(skip, j) * x_conv
        gated = mixed * silu(gates[j])
        squares = squares + gated * gated
        gated_ref[:, cut] = (gated * pair(gain_ref, j)).astype(BF)
        xw_ref[:, cut] = (spread(weight, j) * x_conv).astype(BF)
    row_sum = jnp.broadcast_to(jnp.sum(squares, axis=1, keepdims=True), (rb, LANES))
    ssq_ref[...] = row_sum.T[:8]


def pick_tail(ss, acc, raw, prev):
    rb = raw.shape[0]
    ri = lax.broadcasted_iota(jnp.int32, (rb, rb), 0)
    ci = lax.broadcasted_iota(jnp.int32, (rb, rb), 1)
    same = (ri // DRAFT) == (ci // DRAFT)
    j, q = ri & (DRAFT - 1), ci & (DRAFT - 1)
    source = acc + j - (KW - 1)
    live = same & (j < KW - 1) & jnp.logical_not((source < ss) & (ss < acc))
    new = jnp.where(live & (q == source), 1.0, 0.0).astype(BF)
    old = jnp.where(live & (q == source + DRAFT), 1.0, 0.0).astype(BF)
    return jnp.dot(new, raw.astype(BF), preferred_element_type=F32) + jnp.dot(
        old, prev.astype(BF), preferred_element_type=F32
    )


def ssm(group, rb, meta, recv, mine, dt, b_raw, c_raw, x_state, bc_state, conv_x, conv_bc, heads, gain, state):
    rows = recv.shape[0]
    _, _, rq, hp, width_n = state.shape
    ob = rb // (rq * DRAFT)
    reqs = rb // DRAFT

    def flat(w):
        return pl.BlockSpec((rb, w), lambda i, group: (i, 0))

    def columns(shape, which):
        lead = (0,) * (len(shape) - 1)
        if len(shape) == 3:
            return pl.BlockSpec(shape, lambda i, group: (0, i, which * G + group[0]))
        return pl.BlockSpec(shape, lambda i, group: (*lead, which * G + group[0]))

    return pl.pallas_call(
        ssm_kernel,
        grid_spec=pltpu.PrefetchScalarGridSpec(
            num_scalar_prefetch=1,
            grid=(rows // rb,),
            in_specs=[
                flat(2),
                flat(recv.shape[1]),
                flat(mine.shape[1]),
                flat(LANES),
                flat(LANES),
                flat(LANES),
                pl.BlockSpec((KW - 1, reqs, hp), lambda i, group: (0, i, 0)),
                columns((KW - 1, reqs, LANES), 0),
                columns((KW - 1, reqs, LANES), 1),
                whole_block(conv_x.shape),
                columns((KW, LANES), 0),
                columns((KW, LANES), 1),
                whole_block(heads.shape),
                whole_block(gain.shape),
                pl.BlockSpec((ob, 1, rq, hp, width_n), lambda i, group: (i, 0, 0, 0, 0)),
            ],
            out_specs=[
                flat(hp),
                pl.BlockSpec((8, rb), lambda i, group: (0, i)),
                flat(hp),
                flat(LANES),
                flat(LANES),
                flat(hp),
            ],
        ),
        out_shape=[
            jax.ShapeDtypeStruct((rows, hp), BF),
            jax.ShapeDtypeStruct((8, rows), F32),
            pltpu.HBM((rows, hp), BF),
            pltpu.HBM((rows, LANES), BF),
            pltpu.HBM((rows, LANES), F32),
            pltpu.HBM((rows, hp), BF),
        ],
        compiler_params=params(46),
        cost_estimate=cost(2 * rows * hp * 4096, 6 * rows * hp * 16),
        name="ssm",
    )(group, meta, recv, mine, dt, b_raw, c_raw, x_state, bc_state, bc_state, conv_x, conv_bc, conv_bc, heads, gain, state)


def state_kernel(meta_ref, xw_ref, bconv_ref, sw_ref, xraw_ref, prevx_ref, state_ref, o_ref, tail_ref):
    rb, hp = xw_ref.shape
    width_p = LANES // 2
    ss = meta_ref[..., 0:1].reshape(rb, 1)
    acc = meta_ref[..., 1:2].reshape(rb, 1)
    tail_ref[...] = pick_tail(ss, acc, xraw_ref[...], history_rows(prevx_ref[...]).reshape(rb, hp)).astype(BF)
    request = lax.broadcasted_iota(jnp.int32, (rb, 1), 0) // DRAFT
    b_conv = bconv_ref[...].astype(F32)
    xw_t = xw_ref[...].astype(F32).T.astype(BF)
    rq = state_ref.shape[2]
    sw = sw_ref[...]
    for i in range(0, rb // DRAFT, 2):
        both = jnp.concatenate(
            [jnp.where(request == i + u, b_conv, 0.0).astype(BF) for u in range(2)], axis=1
        )
        added = jnp.dot(xw_t, both, preferred_element_type=F32)
        for u in range(2):
            r = i + u
            for h in range(hp // width_p):
                cut = slice(h * width_p, (h + 1) * width_p)
                old = state_ref[r // rq, 0, r % rq, cut, :].astype(F32)
                new = sw[r * DRAFT : r * DRAFT + 1, h : h + 1] * old + added[cut, u * LANES : (u + 1) * LANES]
                o_ref[r // rq, 0, r % rq, cut, :] = new.astype(BF)


def tail_kernel(meta_ref, raw_ref, prev_ref, o_ref):
    rb = raw_ref.shape[0]
    ss = meta_ref[..., 0:1].reshape(rb, 1)
    acc = meta_ref[..., 1:2].reshape(rb, 1)
    o_ref[...] = pick_tail(ss, acc, raw_ref[...], history_rows(prev_ref[...]).reshape(raw_ref.shape)).astype(BF)


def new_history(rb, meta, raw, prev):
    rows, cols = raw.shape

    def flat(w):
        return pl.BlockSpec((rb, w), lambda i: (i, 0))

    return pl.pallas_call(
        tail_kernel,
        grid=(rows // rb,),
        in_specs=[flat(2), flat(cols), pl.BlockSpec((KW - 1, rb // DRAFT, cols), lambda i: (0, i, 0))],
        out_specs=flat(cols),
        out_shape=jax.ShapeDtypeStruct((rows, cols), BF),
        compiler_params=params(24),
        cost_estimate=cost(4 * rows * rb * cols, 6 * rows * cols),
        name="new_history",
    )(meta, raw, prev)


def new_state(piece, pieces, rb, meta, xw, bconv, sw, xraw, prev_x, state, into):
    rows, hp = xw.shape
    n, _, rq, _, width_n = state.shape
    ob = rb // (rq * DRAFT)
    steps = rows // rb // pieces
    first = piece * steps

    def flat(w):
        return pl.BlockSpec((rb, w), lambda i: (first + i, 0))

    states = pl.BlockSpec((ob, 1, rq, hp, width_n), lambda i: (first + i, 0, 0, 0, 0))
    args = [meta, xw, bconv, sw, xraw, prev_x, state]
    specs = [
        flat(2),
        flat(hp),
        flat(LANES),
        flat(LANES),
        flat(hp),
        pl.BlockSpec((KW - 1, rb // DRAFT, hp), lambda i: (0, first + i, 0)),
        states,
    ]
    kernel, aliases = state_kernel, {}
    if into is not None:
        args.append(into)
        specs.append(pl.BlockSpec(memory_space=pl.ANY))
        aliases = {7: 0}

        def kernel(*refs):
            return state_kernel(*refs[:7], *refs[8:])

    return pl.pallas_call(
        kernel,
        grid=(steps,),
        in_specs=specs,
        out_specs=[states, pl.BlockSpec((rb, hp), lambda i: (i, 0))],
        out_shape=[jax.ShapeDtypeStruct(state.shape, BF), jax.ShapeDtypeStruct((rows // pieces, hp), BF)],
        input_output_aliases=aliases,
        compiler_params=params(40),
        cost_estimate=cost(2 * rows * hp * 4096 // pieces, 8 * rows * hp * 16 // pieces),
        name="new_state",
    )(*args)


def out_kernel(scale_by, inc_ref, mine_ref, theirs_ref, w_mine_ref, w_theirs_ref, ssq_ref, o_ref):
    product = jnp.dot(mine_ref[...], w_mine_ref[...], preferred_element_type=F32) + jnp.dot(
        theirs_ref[...], w_theirs_ref[...], preferred_element_type=F32
    )
    scale = lax.rsqrt(ssq_ref[...] * scale_by + 1e-05)
    rows = scale.shape[1]
    column = jnp.broadcast_to(scale[0:1], (LANES, rows)).T[:, 0:1]
    o_ref[...] = (product * column).astype(o_ref.dtype)


def out_project(inc, mine, theirs, w_out, ssq, scale_by, part, parts, bn=1024):
    rows, hp = mine.shape
    cols = w_out.shape[1] // parts
    first = part * (cols // bn)
    return pl.pallas_call(
        functools.partial(out_kernel, scale_by),
        grid_spec=pltpu.PrefetchScalarGridSpec(
            num_scalar_prefetch=1,
            grid=(cols // bn,),
            in_specs=[
                pl.BlockSpec((rows, hp), lambda j, inc: (0, 0)),
                pl.BlockSpec((rows, hp), lambda j, inc: (0, 0)),
                pl.BlockSpec((hp, bn), lambda j, inc: (inc[0], first + j)),
                pl.BlockSpec((hp, bn), lambda j, inc: (1 - inc[0], first + j)),
                pl.BlockSpec((8, rows), lambda j, inc: (0, 0)),
            ],
            out_specs=pl.BlockSpec((rows, bn), lambda j, inc: (0, j)),
        ),
        out_shape=jax.ShapeDtypeStruct((rows, cols), BF),
        compiler_params=params(40),
        cost_estimate=cost(4 * rows * hp * cols, 4 * hp * cols + 4 * rows * cols),
        name="out_project",
    )(inc, mine, theirs, w_out, w_out, ssq)


def shards(n, chunks, tokens, w_zx, w_dt, w_bc, conv_x, conv_bc, dt_bias, decay_rate, skip_gain, norm_gain,
           w_out, conv_x_state, conv_bc_state, ssm_state, span_start, accepted):
    req, hd, width_p, width_n = ssm_state.shape
    hp = hd * width_p
    block_rows, half_d = tokens.shape
    cw = w_bc.shape[1]
    rc = block_rows // chunks
    rq = rc // DRAFT
    rows = n * rc
    rb = min(128, rows)
    order = list(range(0, n, 2)) + list(range(n - 1, 0, -2))
    ring = [(2 * order[i], 2 * order[(i + 1) % n]) for i in range(n)]
    ring += [(2 * order[(i + 1) % n] + 1, 2 * order[i] + 1) for i in range(n)]
    swap = [(0, 1), (1, 0)]
    me = lax.axis_index("outc")
    inc = lax.axis_index("inc")
    pos = jnp.where(me % 2 == 0, me // 2, n - 1 - me // 2)

    def owner(step):
        i = (pos + (2 * inc - 1) * step + n) % n
        return jnp.where(i < n // 2, 2 * i, 2 * n - 1 - 2 * i)

    seq = owner(jnp.arange(n, dtype=jnp.int32))
    inc1 = inc.astype(jnp.int32).reshape(1)

    def onward(a):
        return lax.ppermute(a, ("outc", "inc"), ring)

    def other(a):
        return lax.ppermute(a, "inc", swap)

    member = n // G
    group = me // member
    seat = me % member
    w_ext = jnp.concatenate([w_bc, w_dt, jnp.zeros((half_d, LANES - w_dt.shape[1]), BF)], axis=1)
    if w_ext.shape[1] % LANES:
        w_ext = jnp.pad(w_ext, ((0, 0), (0, LANES - w_ext.shape[1] % LANES)))

    def columns(a, start, size):
        return lax.dynamic_slice_in_dim(a, start, size, a.ndim - 1)

    x_state = jnp.swapaxes(conv_x_state.reshape(req, KW - 1, hp), 0, 1)
    bc_state = jnp.swapaxes(conv_bc_state, 0, 1)
    own_state = columns(bc_state, me * cw, cw)
    meta = jnp.stack([span_start, accepted], axis=-1).astype(jnp.int32)
    meta = jnp.broadcast_to(meta[:, None, :], (req, DRAFT, 2)).reshape(rows, 2)
    heads = jnp.pad(jnp.stack([dt_bias, decay_rate, skip_gain]), ((0, 5), (0, LANES - hd)))
    group1 = group.astype(jnp.int32).reshape(1)
    state = ssm_state.reshape(n, chunks, rq, hp, width_n)
    scale_by = 1.0 / (HEADS // G * width_p)

    pieces = 4
    w = None
    piece_rows = rc // STREAMS
    heads_of = [tokens[i * piece_rows : (i + 1) * piece_rows] for i in range(STREAMS)]
    blocks = list(heads_of)
    first = n // 2
    split = first * STREAMS
    for s in range(n - 1):
        heads_of = [onward(a) for a in heads_of]
        lead = heads_of[0]
        if s < pieces:
            w = relayout(s, pieces, w_zx, w)
            lead, w = lax.optimization_barrier((lead, w))
        elif s == max(pieces, first):
            theirs_1, ext_1 = project(seq, 1 - inc1, blocks[:split], w, w_ext, BF, [F32])
            lead, theirs_1, ext_1 = lax.optimization_barrier((lead, theirs_1, ext_1))
        elif s == max(pieces, first) + 1:
            (mine_1,) = project(seq, inc1, blocks[:split], w, w_ext, F32, [])
            lead, mine_1 = lax.optimization_barrier((lead, mine_1))
        heads_of[0] = lead
        blocks += heads_of

    prepared = [meta, x_state, own_state, heads, w_ext]
    blocks[-1], prepared = lax.optimization_barrier((blocks[-1], prepared))
    meta, x_state, own_state, heads, w_ext = prepared

    ext = extra(seq, blocks[split:], w_ext, ext_1)
    ext_other = other(ext)
    (theirs,) = project(seq, 1 - inc1, blocks[split:], w, w_ext, BF, [], (theirs_1,))
    theirs, ext, ext_other = lax.optimization_barrier((theirs, ext, ext_other))
    ext = (ext + ext_other).astype(BF)
    bc_own = ext[:, :cw]
    dt = columns(ext[:, cw : cw + 2 * hd], inc * hd, hd)
    dt = jnp.pad(dt, ((0, 0), (0, LANES - hd)))
    got = []
    for k in range(member):
        pairs = []
        for g in range(G):
            width = member // 2
            sources = [g * width + i for i in range(width)] + [n // 2 + g * width + i for i in range(width)]
            for i in range(member):
                pairs.append((sources[(i + k) % member], g * member + i))
        got.append(lax.ppermute(bc_own, "outc", pairs))
    picked = []
    for i in range(member):
        piece = got[0]
        for k in range(1, member):
            piece = jnp.where((i - seat) % member == k, got[k], piece)
        picked.append(piece)
    b_raw = jnp.concatenate(picked[: member // 2], axis=1)
    c_raw = jnp.concatenate(picked[member // 2 :], axis=1)
    theirs = other(theirs)
    late, bc_own, dt = lax.optimization_barrier((blocks[-1], bc_own, dt))
    blocks[-1] = late
    (mine,) = project(seq, inc1, blocks[split:], w, w_ext, F32, [], (mine_1,), shape=jax.ShapeDtypeStruct)
    gated, ssq, xw, bconv, sw, xraw = ssm(
        group1, rb, meta, theirs, mine, dt, b_raw, c_raw, x_state, bc_state, conv_x, conv_bc, heads, norm_gain, state
    )

    def tails(a):
        return a.reshape(req, DRAFT, a.shape[-1])[:, : KW - 1]

    gated_theirs = other(gated)
    ssq = ssq + other(ssq)
    bc_own, gated, ssq = lax.optimization_barrier((bc_own, gated, ssq))
    d = 1
    while d < member:
        ssq = ssq + lax.ppermute(ssq, "outc", [(i, i ^ d) for i in range(n)])
        d *= 2
    history_bc = new_history(rb, meta, bc_own, own_state)
    history_bc = history_bc.reshape(req, DRAFT, cw)[:, : KW - 1].reshape(req * (KW - 1), cw)
    half_rows = req * (KW - 1) // 2
    history_bc = lax.dynamic_slice_in_dim(history_bc, inc * half_rows, half_rows, 0)
    widths = [n >> (i + 1) for i in range(n.bit_length() - 1)]

    def double(a, i):
        got = lax.ppermute(a, "outc", [(k, k ^ widths[i]) for k in range(n)])
        return jnp.where((me & widths[i]) != 0, jnp.stack([got, a], i), jnp.stack([a, got], i))

    history_bc = double(history_bc, 0)
    gated_theirs, ssq, history_bc = lax.optimization_barrier((gated_theirs, ssq, history_bc))
    history_bc = double(history_bc, 1)

    sums, partials = [], []

    def part(i, s):
        return lax.dynamic_slice_in_dim(partials[i], owner((s + 1) % n) * rc, rc, 0)

    for i in range(STREAMS):
        partials.append(out_project(inc1, gated, gated_theirs, w_out, ssq, scale_by, i, STREAMS))
        if i == 0:
            partials[0], history_bc = lax.optimization_barrier((partials[0], history_bc))
            for k in range(2, len(widths)):
                history_bc = double(history_bc, k)
        sums.append(part(i, 0))
    tails_x = []
    after = None
    for s in range(n - 1):
        if s in (0, 2):
            xw, sums[0] = lax.optimization_barrier((xw, sums[0]))
            piece = len(tails_x)
            after, tail = new_state(piece, 2, rb, meta, xw, bconv, sw, xraw, x_state, state, after)
            tails_x.append(tail)
            after, sums[0] = lax.optimization_barrier((after, sums[0]))
        if s == 3:
            history_bc, sums[0] = lax.optimization_barrier((history_bc, sums[0]))
            history_bc = history_bc.reshape(n, half_rows, cw)
            history_other = other(history_bc)
        if s == 4:
            history_other, sums[0] = lax.optimization_barrier((history_other, sums[0]))
            history_bc = jnp.where(
                inc != 0,
                jnp.concatenate([history_other, history_bc], axis=1),
                jnp.concatenate([history_bc, history_other], axis=1),
            )
        if s == 5:
            history_bc, tails_x, sums[1] = lax.optimization_barrier((history_bc, tails_x, sums[1]))
        for i in range(STREAMS):
            sums[i] = (onward(sums[i]).astype(F32) + part(i, s + 1).astype(F32)).astype(BF)
    new_bc = jnp.swapaxes(history_bc, 0, 1).reshape(req, KW - 1, n * cw)
    new_x = tails(jnp.concatenate(tails_x, axis=0)).reshape(req, KW - 1, hd, width_p)
    return jnp.concatenate(sums, axis=1), after.reshape(ssm_state.shape), new_x, new_bc


def solution(mesh):
    n = mesh.shape["outc"]
    placed = (
        P(("groups", "outc"), "inc"),
        P("inc", "outc", None),
        P("inc", "outc"),
        P("inc", "outc"),
        P(None, ("outc", "inc"), None),
        P(),
        P(("outc", "inc")),
        P(("outc", "inc")),
        P(("outc", "inc")),
        P(("outc", "inc"), None),
        P("outc", "inc"),
        P("groups", None, ("outc", "inc"), None),
        P("groups", None, None),
        P("groups", ("outc", "inc"), None, None),
        P("groups"),
        P("groups"),
    )
    return jax.shard_map(
        functools.partial(shards, n, 1),
        mesh=mesh,
        in_specs=placed,
        out_specs=(
            P(("groups", "outc"), "inc"),
            P("groups", ("outc", "inc"), None, None),
            P("groups", None, ("outc", "inc"), None),
            P("groups", None, None),
        ),
        check_vma=False,
    )
```
